128 devices in a mesh: replica: 16 (over y_lo, x, core), fsdp: 8 (over y_hi, z).
Axes of the slice: x: 4, y: 4 (y_hi: 2, y_lo: 2; y = y_hi * 2 + y_lo), z: 4, core: 2. Of those that a mesh axis runs over, the one named last changes fastest.
Arguments:
- tokens: bfloat16 [16384, 1024], P(('replica', 'fsdp')), may hold values from -6 to 6
- counts: int32 [16, 8], P('replica'), may hold values from 64 to 128, as said below
- w_qkv: bfloat16 [1024, 3072], P('fsdp'), may hold values from -0.1875 to 0.1875
- bias_qv: bfloat16 [2048], P('fsdp'), may hold values from -3 to 3
- w_out: bfloat16 [1024, 1024], P('fsdp'), may hold values from -4 to 4
- bias_out: bfloat16 [1024], P('fsdp'), may hold values from -3 to 3
- gain_attn: bfloat16 [1024], P('fsdp'), may hold values from 0.099609375 to 1.8984375
- shift_attn: bfloat16 [1024], P('fsdp'), may hold values from -3 to 3
- w_up: bfloat16 [1024, 4096], P('fsdp'), may hold values from -0.1875 to 0.1875
- bias_up: bfloat16 [4096], P('fsdp'), may hold values from -3 to 3
- w_down: bfloat16 [4096, 1024], P('fsdp'), may hold values from -0.09375 to 0.09375
- bias_down: bfloat16 [1024], P('fsdp'), may hold values from -3 to 3
- gain_ffn: bfloat16 [1024], P('fsdp'), may hold values from 0.099609375 to 1.8984375
- shift_ffn: bfloat16 [1024], P('fsdp'), may hold values from -3 to 3
- cotangent: bfloat16 [16384, 1024], P(('replica', 'fsdp')), may hold values from -6 to 6
Outputs:
- layer_out: bfloat16 [16384, 1024], P(('replica', 'fsdp'))
- input_grad: float32 [16384, 1024], P(('replica', 'fsdp'))
- grad_w_qkv: float32 [1024, 3072], P('fsdp')
- grad_bias_qv: float32 [2048], P('fsdp')
- grad_w_out: float32 [1024, 1024], P('fsdp')
- grad_bias_out: float32 [1024], P('fsdp')
- grad_gain_attn: float32 [1024], P('fsdp')
- grad_shift_attn: float32 [1024], P('fsdp')
- grad_w_up: float32 [1024, 4096], P('fsdp')
- grad_bias_up: float32 [4096], P('fsdp')
- grad_w_down: float32 [4096, 1024], P('fsdp')
- grad_bias_down: float32 [1024], P('fsdp')
- grad_gain_ffn: float32 [1024], P('fsdp')
- grad_shift_ffn: float32 [1024], P('fsdp')
The draws below stay inside these ranges and needn't reach their ends.
Inputs may be any that keep to these rules, and one draw needn't show every extreme that they name: `counts`: one device of every sequence uses all its 128 slots.
All inputs are finite; a program needn't handle non-finite values.
Results may differ from the reference program's by a relative error of at most 0.025.
Values may be sent and summed in bfloat16 or wider, within the bound.
No kernel may reach another device: no remote copies, remote signals or barrier semaphores. Data moves between devices by JAX's collectives and lax.ppermute only.
A program may use at most 128 MiB of HBM per device.

```python
import jax
import jax.numpy as jnp
from jax import lax

D = 1024
FF = 4096
HEADS = 16
HEAD_DIM = 64
TOK_DEV = 128
TOKENS = 16384
N_REPLICA = 16
N_FSDP = 8


def draw_counts(key, part):
    key = jax.random.fold_in(key, 11)
    first, second = jax.random.split(key)
    drawn = jax.random.randint(first, (N_REPLICA, N_FSDP), TOK_DEV // 2, TOK_DEV + 1, dtype=jnp.int32)
    full_at = jax.random.randint(second, (N_REPLICA, 1), 0, N_FSDP, dtype=jnp.int32)
    spots = jnp.arange(N_FSDP, dtype=jnp.int32)[None, :]
    return jnp.where(spots == full_at, TOK_DEV, drawn).astype(jnp.int32)


def block_levels(key, dims, pieces, low, top_value):
    factor_of, own = 1.0, jax.random.fold_in(key, 6)
    for position, shards_of in pieces:
        steps = jnp.exp(jax.random.uniform(jax.random.fold_in(own, position), (shards_of,), jnp.float32, low / len(pieces), top_value / len(pieces)))
        factor_of = factor_of * jnp.repeat(steps, dims[position] // shards_of).reshape([-1 if axis == position else 1 for axis in range(len(dims))])
    return factor_of


def gaussian(own_key, extent, spread, reach, shards=(), kind=jnp.bfloat16):
    factor_of = block_levels(own_key, extent, shards, -0.22, 0.18) if shards else 1.0
    values = jax.random.normal(own_key, extent, jnp.float32) * spread * factor_of
    return jnp.minimum(jnp.maximum(values, -reach), reach).astype(kind)


def setup_inputs(seed: int = 0) -> dict:
    streams_of = jax.random.split(jax.random.key(seed), 16)
    tokens = gaussian(streams_of[0], (TOKENS, D), 1.0, 6.0, ((0, 128),))
    counts = draw_counts(jax.random.fold_in(streams_of[15], 71), 0)
    w_qkv = gaussian(streams_of[2], (D, 3 * D), D ** -0.5, 0.1875, ((0, 8),))
    bias_qv = gaussian(streams_of[3], (2 * D,), 0.5, 3.0, ((0, 8),))
    w_out = gaussian(streams_of[4], (D, D), 2 ** -0.5, 4.0, ((0, 8),))
    bias_out = gaussian(streams_of[5], (D,), 0.5, 3.0, ((0, 8),))
    gain_attn = jnp.clip(1.0 + 0.18 * jax.random.normal(streams_of[6], (D,), jnp.float32), 0.099609375, 1.8984375).astype(jnp.bfloat16)
    shift_attn = gaussian(streams_of[7], (D,), 0.5, 3.0, ((0, 8),))
    w_up = gaussian(streams_of[8], (D, FF), D ** -0.5, 0.1875, ((0, 8),))
    bias_up = gaussian(streams_of[9], (FF,), 0.5, 3.0, ((0, 8),))
    w_down = gaussian(streams_of[10], (FF, D), FF ** -0.5, 0.09375, ((0, 8),))
    bias_down = gaussian(streams_of[11], (D,), 0.5, 3.0, ((0, 8),))
    gain_ffn = jnp.clip(1.0 + 0.18 * jax.random.normal(streams_of[12], (D,), jnp.float32), 0.099609375, 1.8984375).astype(jnp.bfloat16)
    shift_ffn = gaussian(streams_of[13], (D,), 0.5, 3.0, ((0, 8),))
    cotangent = gaussian(streams_of[14], (TOKENS, D), 1.0, 6.0, ((0, 128),))
    return {"tokens": tokens, "counts": counts, "w_qkv": w_qkv, "bias_qv": bias_qv, "w_out": w_out, "bias_out": bias_out, "gain_attn": gain_attn, "shift_attn": shift_attn, "w_up": w_up, "bias_up": bias_up, "w_down": w_down, "bias_down": bias_down, "gain_ffn": gain_ffn, "shift_ffn": shift_ffn, "cotangent": cotangent}


@jax.custom_vjp
def low(v):
    return lax.optimization_barrier(v.astype(jnp.bfloat16)).astype(jnp.float32)

@jax.custom_vjp
def low_back(v):
    return v

def low_keep(v):
    return (low(v), None)

def low_pass(kept, grad):
    return (grad,)

def back_keep(v):
    return (v, None)

def back_low(kept, grad):
    return (low(grad),)
low.defvjp(low_keep, low_pass)
low_back.defvjp(back_keep, back_low)
highest = lax.Precision.HIGHEST
epsilon = 1e-05

def matmul(left, right):
    return jnp.dot(left, right, precision=highest)

def layer_norm(hidden, gain, shift):
    mean_row = lax.optimization_barrier(jnp.mean(hidden, axis=-1, keepdims=True))
    centered = hidden - mean_row
    variance = lax.optimization_barrier(jnp.mean(centered * centered, axis=-1, keepdims=True))
    return centered * lax.rsqrt(variance + epsilon) * gain + shift

def attend_head(inputs, key_ok):
    queries, keys_head, values_head = inputs
    scores = low_back(matmul(queries, keys_head.T) * HEAD_DIM ** (-0.5))
    scores = jnp.where(key_ok[None, :], scores, -1e+30)
    row_max = lax.optimization_barrier(jnp.max(scores, axis=-1, keepdims=True))
    expo = jnp.exp(scores - row_max)
    attn_probs = expo / lax.optimization_barrier(jnp.sum(expo, axis=-1, keepdims=True))
    return matmul(low(attn_probs), values_head)

def split_heads(matrix):
    return matrix.reshape(matrix.shape[0], HEADS, HEAD_DIM).transpose(1, 0, 2)

def forward(tokens_f, key_ok, row_ok, w_qkv, bias_qv, w_out, bias_out, gain_attn, shift_attn, w_up, bias_up, w_down, bias_down, gain_ffn, shift_ffn):
    span_rows = tokens_f.shape[0]
    projected = matmul(tokens_f, w_qkv)
    queries = low_back(low(projected[:, :D] + bias_qv[:D]))
    keys_all = low_back(low(projected[:, D:2 * D]))
    values_all = low_back(low(projected[:, 2 * D:] + bias_qv[D:]))

    def head_step(inputs):
        return attend_head(inputs, key_ok)
    context = lax.map(jax.checkpoint(head_step), (split_heads(queries), split_heads(keys_all), split_heads(values_all)))
    context = context.transpose(1, 0, 2).reshape(span_rows, D) * row_ok[:, None]
    context = low_back(low(context))
    attn_out = low_back(matmul(context, w_out) + bias_out)
    normed = layer_norm(tokens_f + attn_out, gain_attn, shift_attn)
    hidden = low_back(matmul(low(normed), w_up) + bias_up)
    active = low(jax.nn.gelu(hidden, approximate=False))
    ffn_out = low_back(matmul(active, w_down) + bias_down)
    return layer_norm(normed + ffn_out, gain_ffn, shift_ffn)

def reference(tokens, counts, w_qkv, bias_qv, w_out, bias_out, gain_attn, shift_attn, w_up, bias_up, w_down, bias_down, gain_ffn, shift_ffn, cotangent):
    group_rows = N_FSDP * TOK_DEV
    slots = jnp.arange(group_rows, dtype=jnp.int32)
    params = tuple((item.astype(jnp.float32) for item in (w_qkv, bias_qv, w_out, bias_out, gain_attn, shift_attn, w_up, bias_up, w_down, bias_down, gain_ffn, shift_ffn)))

    def one_group(totals, inputs):
        row_block, counts_row, grad_out = inputs
        limit_row = counts_row[slots // TOK_DEV]
        valid_row = slots % TOK_DEV < limit_row
        row_ok = valid_row.astype(jnp.float32)

        def run_layer(tokens_f, *weights):
            return forward(tokens_f, valid_row, row_ok, *weights)
        layer_val, pullback = jax.vjp(run_layer, row_block.astype(jnp.float32), *params)
        grad_all = pullback(grad_out.astype(jnp.float32))
        totals = tuple((total + grad_term for total, grad_term in zip(totals, grad_all[1:])))
        return (totals, (layer_val.astype(jnp.bfloat16), grad_all[0]))
    start = tuple((jnp.zeros(item.shape, jnp.float32) for item in params))
    totals, results = lax.scan(one_group, start, (tokens.reshape(N_REPLICA, group_rows, D), counts, cotangent.reshape(N_REPLICA, group_rows, D)))
    layer_out = results[0].reshape(N_REPLICA * group_rows, D)
    input_grad = results[1].reshape(N_REPLICA * group_rows, D)
    return (layer_out, input_grad, totals[0], totals[1], totals[2], totals[3], totals[4], totals[5], totals[6], totals[7], totals[8], totals[9], totals[10], totals[11])
```

```python
import jax
import jax.numpy as jnp
from jax import lax
from jax.experimental import pallas as pl
from jax.experimental.pallas import tpu as pltpu
from jax.sharding import PartitionSpec as P

HEAD_DIM = 64
EPSILON = 1e-05
BF = jnp.bfloat16
F32 = jnp.float32
BOTH = ("replica", "fsdp")


def all_pairs(move):
    pairs = []
    for yl in range(2):
        for x in range(4):
            for core in range(2):
                for yh in range(2):
                    for z in range(4):
                        a, b, c, d, e = move(yl, x, core, yh, z)
                        pairs.append(
                            (
                                ((yl * 4 + x) * 2 + core) * 8 + yh * 4 + z,
                                ((a * 4 + b) * 2 + c) * 8 + d * 4 + e,
                            )
                        )
    return pairs


def z_shift(value, k):
    return lax.ppermute(
        value, BOTH, all_pairs(lambda yl, x, c, yh, z: (yl, x, c, yh, (z + k) % 4))
    )


def x_shift(value, k):
    return lax.ppermute(
        value, BOTH, all_pairs(lambda yl, x, c, yh, z: (yl, (x + k) % 4, c, yh, z))
    )


def core_flip(value):
    return lax.ppermute(value, BOTH, all_pairs(lambda yl, x, c, yh, z: (yl, x, 1 - c, yh, z)))


def y_flip(value, lo, hi):
    return lax.ppermute(
        value, BOTH, all_pairs(lambda yl, x, c, yh, z: (yl ^ lo, x, c, yh ^ hi, z))
    )


def z_gather(value):
    return [value] + [z_shift(value, -k) for k in (1, 2, 3)]


def z_scatter(partial):
    rows = partial.shape[0] // 4
    terms = [partial[:rows]]
    for k in (1, 2, 3):
        terms.append(z_shift(partial[k * rows : (k + 1) * rows], k))
    return terms


def add_terms(terms):
    total = terms[0].astype(F32)
    for term in terms[1:]:
        total = total + term.astype(F32)
    return total


def dot(left, right):
    return jnp.dot(left, right, preferred_element_type=F32)


def dot_t(left, right):
    return lax.dot_general(left, right, (((1,), (1,)), ((), ())), preferred_element_type=F32)


def t_dot(left, right):
    return lax.dot_general(left, right, (((0,), (0,)), ((), ())), preferred_element_type=F32)


def pick(stacked, index, axis=0):
    return lax.dynamic_index_in_dim(stacked, index, axis, keepdims=False)


def attend_kernel(q_ref, own_ref, far_ref, mask_ref, ok_ref, ctx_ref, p_ref):
    queries = q_ref[...]
    width = queries.shape[1]
    half = own_ref.shape[0]
    head_of = lax.broadcasted_iota(jnp.int32, (1, width), 1) // HEAD_DIM
    context = jnp.zeros(queries.shape, F32)
    for h in range(width // HEAD_DIM):
        q_h = jnp.where(head_of == h, queries, jnp.zeros_like(queries))
        s_own = dot_t(q_h, own_ref[:, :width]) + mask_ref[:, :half]
        s_far = dot_t(q_h, far_ref[:, :width]) + mask_ref[:, half:]
        top = jnp.maximum(
            jnp.max(s_own, axis=1, keepdims=True), jnp.max(s_far, axis=1, keepdims=True)
        )
        e_own = jnp.exp(s_own - top)
        e_far = jnp.exp(s_far - top)
        scale = 1.0 / (
            jnp.sum(e_own, axis=1, keepdims=True) + jnp.sum(e_far, axis=1, keepdims=True)
        )
        p_own = (e_own * scale).astype(BF)
        p_far = (e_far * scale).astype(BF)
        p_ref[h, :, :half] = p_own
        p_ref[h, :, half:] = p_far
        out = dot(p_own, own_ref[:, width:]) + dot(p_far, far_ref[:, width:])
        context = jnp.where(head_of == h, out, context)
    ctx_ref[...] = (context * ok_ref[...]).astype(BF)


def attend(queries, kv_own, kv_far, key_mask, row_ok):
    rows, width = queries.shape
    heads = width // HEAD_DIM
    keys = 2 * kv_own.shape[0]
    step = 256
    return pl.pallas_call(
        attend_kernel,
        grid=(rows // step,),
        in_specs=[
            pl.BlockSpec((step, width), lambda i: (i, 0)),
            pl.BlockSpec(kv_own.shape, lambda i: (0, 0)),
            pl.BlockSpec(kv_far.shape, lambda i: (0, 0)),
            pl.BlockSpec((1, keys), lambda i: (0, 0)),
            pl.BlockSpec((step, 1), lambda i: (i, 0)),
        ],
        out_specs=[
            pl.BlockSpec((step, width), lambda i: (i, 0)),
            pl.BlockSpec((heads, step, keys), lambda i: (0, i, 0)),
        ],
        out_shape=[
            jax.ShapeDtypeStruct((rows, width), BF),
            jax.ShapeDtypeStruct((heads, rows, keys), BF),
        ],
        compiler_params=pltpu.CompilerParams(vmem_limit_bytes=48 * 1024 * 1024),
        cost_estimate=pl.CostEstimate(
            flops=16 * rows * keys * width, bytes_accessed=6 * 1024 * 1024, transcendentals=0
        ),
        name="attend",
    )(queries, kv_own, kv_far, key_mask, row_ok)


def attend_back_kernel(
    q_ref, own_ref, far_ref, grad_ref, p_ref, dq_ref, down_ref, dfar_ref, acc_own, acc_far
):
    at = pl.program_id(0)
    queries = q_ref[...]
    grads = grad_ref[...]
    width = queries.shape[1]
    half = own_ref.shape[0]
    head_of = lax.broadcasted_iota(jnp.int32, (1, width), 1) // HEAD_DIM
    zero = jnp.zeros_like(queries)

    @pl.when(at == 0)
    def _():
        acc_own[...] = jnp.zeros_like(acc_own)
        acc_far[...] = jnp.zeros_like(acc_far)

    d_queries = jnp.zeros(queries.shape, F32)
    for h in range(width // HEAD_DIM):
        q_h = jnp.where(head_of == h, queries, zero)
        g_h = jnp.where(head_of == h, grads, zero)
        p_own_low = p_ref[h, :, :half]
        p_far_low = p_ref[h, :, half:]
        p_own = p_own_low.astype(F32)
        p_far = p_far_low.astype(F32)
        t_own = p_own * dot_t(g_h, own_ref[:, width:])
        t_far = p_far * dot_t(g_h, far_ref[:, width:])
        inner = jnp.sum(t_own, axis=1, keepdims=True) + jnp.sum(t_far, axis=1, keepdims=True)
        ds_own = (t_own - p_own * inner).astype(BF)
        ds_far = (t_far - p_far * inner).astype(BF)
        out = dot(ds_own, own_ref[:, :width]) + dot(ds_far, far_ref[:, :width])
        d_queries = jnp.where(head_of == h, out, d_queries)
        acc_own[:, :width] += t_dot(ds_own, q_h)
        acc_far[:, :width] += t_dot(ds_far, q_h)
        acc_own[:, width:] += t_dot(p_own_low, g_h)
        acc_far[:, width:] += t_dot(p_far_low, g_h)
    dq_ref[...] = (d_queries * HEAD_DIM**-0.5).astype(BF)

    @pl.when(at == pl.num_programs(0) - 1)
    def _():
        down_ref[...] = acc_own[...]
        dfar_ref[...] = acc_far[...].astype(BF)


def attend_back(queries, kv_own, kv_far, d_context, probs):
    rows, width = queries.shape
    heads, _, keys = probs.shape
    step = 256
    return pl.pallas_call(
        attend_back_kernel,
        grid=(rows // step,),
        in_specs=[
            pl.BlockSpec((step, width), lambda i: (i, 0)),
            pl.BlockSpec(kv_own.shape, lambda i: (0, 0)),
            pl.BlockSpec(kv_far.shape, lambda i: (0, 0)),
            pl.BlockSpec((step, width), lambda i: (i, 0)),
            pl.BlockSpec((heads, step, keys), lambda i: (0, i, 0)),
        ],
        out_specs=[
            pl.BlockSpec((step, width), lambda i: (i, 0)),
            pl.BlockSpec(kv_own.shape, lambda i: (0, 0)),
            pl.BlockSpec(kv_own.shape, lambda i: (0, 0)),
        ],
        out_shape=[
            jax.ShapeDtypeStruct((rows, width), BF),
            jax.ShapeDtypeStruct(kv_own.shape, F32),
            jax.ShapeDtypeStruct(kv_own.shape, BF),
        ],
        scratch_shapes=[pltpu.VMEM(kv_own.shape, F32), pltpu.VMEM(kv_own.shape, F32)],
        compiler_params=pltpu.CompilerParams(vmem_limit_bytes=48 * 1024 * 1024),
        cost_estimate=pl.CostEstimate(
            flops=40 * rows * keys * width, bytes_accessed=8 * 1024 * 1024, transcendentals=0
        ),
        name="attend_back",
    )(queries, kv_own, kv_far, d_context, probs)


def norm_stats(values):
    mean = jnp.mean(values, axis=-1, keepdims=True)
    centered = values - mean
    rstd = lax.rsqrt(jnp.mean(centered * centered, axis=-1, keepdims=True) + EPSILON)
    return centered * rstd, rstd


def norm_back(grad_out, gain, xhat, rstd):
    g = grad_out * gain
    return rstd * (
        g
        - jnp.mean(g, axis=-1, keepdims=True)
        - xhat * jnp.mean(g * xhat, axis=-1, keepdims=True)
    )


def unroll_ring(blocks, index):
    stacked = jnp.concatenate([b[None] for b in blocks + blocks], axis=0)
    return lax.dynamic_slice_in_dim(stacked, (4 - index) % 4, 4, axis=0)


def reduce_pieces(pieces, vectors, place):
    yl, x, core, yh, z = place
    keep_vec = vectors is not None
    extra = 0 if vectors is None else vectors.shape[0]
    cols = pieces.shape[-1]

    def attach(block, vec):
        flat = block.reshape(-1, cols)
        return jnp.concatenate([flat, vec], axis=0) if keep_vec else flat

    def detach(flat, shape):
        if not keep_vec:
            return flat.reshape(shape), None
        return flat[:-extra].reshape(shape), flat[-extra:]

    rows = pieces.shape[3]
    mine = pick(pieces, core, 1)
    got, got_vec = detach(core_flip(attach(pick(pieces, 1 - core, 1), vectors)), mine.shape)
    mine = add_terms([mine, got]).astype(BF)
    if keep_vec:
        vectors = add_terms([vectors, got_vec]).astype(BF)
    terms = [pick(mine, x, 1)]
    vec_terms = [vectors]
    for k in (1, 2, 3):
        sent = attach(pick(mine, (x + k) % 4, 1), vectors)
        got, got_vec = detach(x_shift(sent, k), terms[0].shape)
        terms.append(got)
        vec_terms.append(got_vec)
    mine = add_terms(terms).astype(BF)
    if keep_vec:
        vectors = add_terms(vec_terms).astype(BF)
    own = pick(mine, yh, 0)
    other = pick(mine, 1 - yh, 0)
    terms = [own]
    vec_terms = [vectors]
    for block, lo, hi in ((own, 1, 0), (other, 0, 1), (other, 1, 1)):
        got, got_vec = detach(y_flip(attach(block, vectors), lo, hi), own.shape)
        terms.append(got)
        vec_terms.append(got_vec)
    total = add_terms(terms).astype(BF)
    if keep_vec:
        vectors = add_terms(vec_terms)
    return total, vectors


def spread_pieces(piece, place):
    yl, x, core, yh, z = place
    ring = unroll_ring([piece] + [x_shift(piece, -k) for k in (1, 2, 3)], x)
    far = core_flip(ring)
    return jnp.where(
        core == 0, jnp.stack([ring, far], axis=0), jnp.stack([far, ring], axis=0)
    )


def on_device(
    tokens,
    counts,
    w_qkv,
    bias_qv,
    w_out,
    bias_out,
    gain_attn,
    shift_attn,
    w_up,
    bias_up,
    w_down,
    bias_down,
    gain_ffn,
    shift_ffn,
    cotangent,
):
    row_count, model_width = tokens.shape
    replica = lax.axis_index("replica")
    group = lax.axis_index("fsdp")
    yl, x, core = replica // 8, (replica // 2) % 4, replica % 2
    yh, z = group // 4, group % 4
    place = (yl, x, core, yh, z)
    lanes = 128
    counts_row = counts[0]

    ring = (z + jnp.arange(4, dtype=jnp.int32)) % 4
    own_counts = jnp.take(counts_row, yh * 4 + ring)
    far_counts = jnp.take(counts_row, (1 - yh) * 4 + ring)
    slot = jnp.arange(row_count, dtype=jnp.int32)
    own_ok = (slot[None, :] < own_counts[:, None]).reshape(-1)
    far_ok = (slot[None, :] < far_counts[:, None]).reshape(-1)
    key_mask = jnp.where(jnp.concatenate([own_ok, far_ok]), 0.0, -1e30).astype(F32)[None, :]
    row_ok = own_ok.astype(F32)[:, None]

    vec_in = jnp.concatenate(
        [bias_qv, bias_out, gain_attn, shift_attn, bias_up, bias_down, gain_ffn, shift_ffn]
    ).reshape(2, 768)
    vec_in = jnp.pad(vec_in, ((0, 14), (0, 0)))
    qkv_blocks = w_qkv.reshape(row_count, 3, 2, 4, lanes).transpose(3, 0, 1, 2, 4)
    qkv_blocks = qkv_blocks.reshape(4, row_count, 6 * lanes)
    sent = jnp.concatenate(
        [qkv_blocks, jnp.broadcast_to(vec_in[None], (4, 16, 6 * lanes))], axis=1
    )
    sent = jnp.concatenate([sent, sent], axis=0)
    token_blocks = z_gather(tokens)
    got = lax.all_to_all(sent, "fsdp", 0, 0, tiled=True)
    qkv_w = got[:, :row_count].reshape(8 * row_count, 6 * lanes)
    vec_all = got[:, row_count : row_count + 2].reshape(8, 1536).astype(F32)
    bias_qv_all = vec_all[:, :256].reshape(2, 2, 4, lanes)
    bias_own = pick(bias_qv_all, z, 2).reshape(2, 2 * lanes)
    bout_all = vec_all[:, 256:384].reshape(1, -1)
    ga_all = vec_all[:, 384:512].reshape(1, -1)
    sa_all = vec_all[:, 512:640].reshape(1, -1)
    bup_own = pick(vec_all[:, 640:1152].reshape(2, 4, 512), z, 1).reshape(1, -1)
    bdown_all = vec_all[:, 1152:1280].reshape(1, -1)
    gf_all = vec_all[:, 1280:1408].reshape(1, -1)
    sf_all = vec_all[:, 1408:1536].reshape(1, -1)

    tokens_all = jnp.concatenate(token_blocks, axis=0)
    projected = dot(tokens_all, qkv_w)
    queries = ((projected[:, :256] + bias_own[0:1]).astype(BF) * HEAD_DIM**-0.5).astype(BF)
    kv_own = jnp.concatenate(
        [projected[:, 256:512], projected[:, 512:] + bias_own[1:2]], axis=1
    ).astype(BF)
    kv_far = y_flip(kv_own, 0, 1)

    out_far = y_flip(w_out, 0, 1)
    up_blocks = w_up.reshape(row_count, 2, 4, 512)
    up_pieces = [
        pick(up_blocks, (z + k) % 4, 2).reshape(row_count, 1024) for k in range(4)
    ]
    up_ring = [up_pieces[0]] + [z_shift(up_pieces[k], k) for k in (1, 2, 3)]
    up_ring = unroll_ring([up_ring[0], up_ring[3], up_ring[2], up_ring[1]], z)
    up_half = up_ring.reshape(4 * row_count, 1024)
    up_far = y_flip(up_half, 0, 1)
    down_far = y_flip(w_down, 0, 1)

    def order(own, far):
        return jnp.where(
            yh == 0, jnp.concatenate([own, far], axis=0), jnp.concatenate([far, own], axis=0)
        )

    out_w = order(w_out, out_far)
    up_w = order(up_half, up_far)
    down_w = order(w_down, down_far)

    context, probs = attend(queries, kv_own, kv_far, key_mask, row_ok)
    attn_part = dot(context, out_w).astype(BF)
    resid1 = add_terms([tokens] + z_scatter(attn_part)) + bout_all
    xhat1, rstd1 = norm_stats(resid1)
    normed = xhat1 * ga_all + sa_all
    normed_all = jnp.concatenate(z_gather(normed.astype(BF)), axis=0)
    hidden = dot(normed_all, up_w) + bup_own
    cdf = 0.5 * (1.0 + lax.erf(hidden * 0.7071067811865476))
    active = (hidden * cdf).astype(BF)
    slope = cdf + hidden * (0.3989422804014327 * jnp.exp(-0.5 * hidden * hidden))
    ffn_part = dot(active, down_w).astype(BF)
    resid2 = add_terms([normed] + z_scatter(ffn_part)) + bdown_all
    xhat2, rstd2 = norm_stats(resid2)
    layer_out = (xhat2 * gf_all + sf_all).astype(BF)

    cot = cotangent.astype(F32)
    d_resid2 = norm_back(cot, gf_all, xhat2, rstd2)

    def with_sums(block, sums):
        rows = jnp.stack(sums, axis=0).astype(BF)
        rows = jnp.pad(rows, ((0, 16 - rows.shape[0]), (0, 0)))
        return jnp.concatenate([block.astype(BF), rows], axis=0)

    def split_sums(blocks, number):
        whole = jnp.concatenate([b[:row_count] for b in blocks], axis=0)
        sums = add_terms([b[row_count : row_count + number] for b in blocks])
        return whole, sums

    gathered = z_gather(
        with_sums(d_resid2, [jnp.sum(cot * xhat2, axis=0), jnp.sum(cot, axis=0)])
    )
    dffn_all, ffn_sums = split_sums(gathered, 2)
    d_hidden = (slope * dot_t(dffn_all, down_w)).astype(BF)
    dn_part = dot_t(d_hidden, up_w).astype(BF)
    d_normed = add_terms([d_resid2] + z_scatter(dn_part))
    d_resid1 = norm_back(d_normed, ga_all, xhat1, rstd1)
    gathered = z_gather(
        with_sums(d_resid1, [jnp.sum(d_normed * xhat1, axis=0), jnp.sum(d_normed, axis=0)])
    )
    dattn_all, attn_sums = split_sums(gathered, 2)
    d_context = (dot_t(dattn_all, out_w) * row_ok).astype(BF)

    grad_down = t_dot(active, dffn_all).astype(BF)
    grad_up = t_dot(normed_all, d_hidden).astype(BF)
    grad_out = t_dot(context, dattn_all).astype(BF)
    first = jnp.concatenate(
        [
            grad_down.reshape(2, 8, 64, 1024),
            grad_up.reshape(2, 4, 8, 16, 1024).transpose(0, 2, 1, 3, 4).reshape(2, 8, 64, 1024),
            grad_out.reshape(2, 8, 16, 1024),
        ],
        axis=2,
    ).reshape(2, 2, 4, 144, 1024)
    first_sum, _ = reduce_pieces(first, None, place)

    def z_swap(block):
        blocks = [pick(block, z)] + [z_shift(pick(block, (z + k) % 4), k) for k in (1, 2, 3)]
        return unroll_ring([blocks[0], blocks[3], blocks[2], blocks[1]], z)

    up_sum = z_swap(first_sum[64:128].reshape(4, 16, 1024)).reshape(64, 1024)
    first_all = spread_pieces(
        jnp.concatenate([first_sum[:64], up_sum, first_sum[128:]], axis=0), place
    ).reshape(8, 144, 1024)
    grad_w_down = first_all[:, :64].reshape(512, 1024).astype(F32)
    grad_w_out = first_all[:, 128:].reshape(128, 1024).astype(F32)
    grad_w_up = (
        first_all[:, 64:128]
        .reshape(8, 4, 16, 2, 512)
        .transpose(0, 2, 3, 1, 4)
        .reshape(128, 4096)
        .astype(F32)
    )

    d_queries, dkv_own, dkv_far = attend_back(queries, kv_own, kv_far, d_context, probs)
    dkv = (dkv_own + y_flip(dkv_far, 0, 1).astype(F32)).astype(BF)
    d_projected = jnp.concatenate([d_queries, dkv], axis=1)
    grad_qkv = t_dot(tokens_all, d_projected).astype(BF)
    vectors = jnp.concatenate(
        [
            jnp.sum(d_queries.astype(F32), axis=0),
            jnp.sum(dkv[:, 256:].astype(F32), axis=0),
            jnp.sum(d_hidden.astype(F32), axis=0),
            jnp.sum(dattn_all.astype(F32), axis=0),
            attn_sums[0],
            attn_sums[1],
            jnp.sum(dffn_all.astype(F32), axis=0),
            ffn_sums[0],
            ffn_sums[1],
        ]
    ).astype(BF)
    vectors = jnp.pad(vectors.reshape(10, 768), ((0, 6), (0, 0)))
    second = grad_qkv.reshape(2, 4, 8, 16, 768).transpose(0, 2, 1, 3, 4)
    second_sum, vec_sum = reduce_pieces(second.reshape(2, 2, 4, 64, 768), vectors, place)
    bqv_row = jnp.pad(vec_sum[0:1].astype(BF), ((0, 15), (0, 0)))
    swapped = z_swap(
        jnp.concatenate(
            [second_sum.reshape(4, 16, 768), jnp.broadcast_to(bqv_row[None], (4, 16, 768))], axis=1
        )
    )
    second_all = spread_pieces(swapped[:, :16].reshape(64, 768), place)
    grad_w_qkv = (
        second_all.reshape(8, 4, 16, 3, 2, lanes)
        .transpose(0, 2, 3, 4, 1, 5)
        .reshape(128, 3072)
        .astype(F32)
    )
    bqv_all = swapped[:, 16, :512].astype(F32).reshape(4, 2, 2, lanes).transpose(1, 2, 0, 3)
    grad_bqv = pick(bqv_all.reshape(8, 256), group)
    flat = vec_sum[:10].reshape(-1)
    grad_bup = pick(flat[512:1536].reshape(2, 512), yh)
    rest = flat[1536:].reshape(6, 8, 128)
    rest = pick(rest, group, 1)

    input_part = dot_t(d_projected, qkv_w).astype(BF)
    input_grad = add_terms([d_resid1] + z_scatter(input_part))

    return (
        layer_out,
        input_grad,
        grad_w_qkv,
        grad_bqv,
        grad_w_out,
        rest[0],
        rest[1],
        rest[2],
        grad_w_up,
        grad_bup,
        grad_w_down,
        rest[3],
        rest[4],
        rest[5],
    )


def solution(mesh):
    in_specs = (
        P(("replica", "fsdp"), None),
        P("replica", None),
        P("fsdp", None),
        P("fsdp"),
        P("fsdp", None),
        P("fsdp"),
        P("fsdp"),
        P("fsdp"),
        P("fsdp", None),
        P("fsdp"),
        P("fsdp", None),
        P("fsdp"),
        P("fsdp"),
        P("fsdp"),
        P(("replica", "fsdp"), None),
    )
    out_specs = (
        P(("replica", "fsdp"), None),
        P(("replica", "fsdp"), None),
        P("fsdp", None),
        P("fsdp"),
        P("fsdp", None),
        P("fsdp"),
        P("fsdp"),
        P("fsdp"),
        P("fsdp", None),
        P("fsdp"),
        P("fsdp", None),
        P("fsdp"),
        P("fsdp"),
        P("fsdp"),
    )
    return jax.shard_map(
        on_device, mesh=mesh, in_specs=in_specs, out_specs=out_specs, check_vma=False
    )
```

```python
import jax
import jax.numpy as jnp
from jax import lax
from jax.experimental import pallas as pl
from jax.experimental.pallas import tpu as pltpu
from jax.sharding import PartitionSpec as P

HEAD_DIM = 64
EPSILON = 1e-05
BF = jnp.bfloat16
F32 = jnp.float32
BOTH = ("replica", "fsdp")


def all_pairs(move):
    pairs = []
    for yl in range(2):
        for x in range(4):
            for core in range(2):
                for yh in range(2):
                    for z in range(4):
                        a, b, c, d, e = move(yl, x, core, yh, z)
                        pairs.append(
                            (
                                ((yl * 4 + x) * 2 + core) * 8 + yh * 4 + z,
                                ((a * 4 + b) * 2 + c) * 8 + d * 4 + e,
                            )
                        )
    return pairs


def z_shift(value, k):
    return lax.ppermute(
        value, BOTH, all_pairs(lambda yl, x, c, yh, z: (yl, x, c, yh, (z + k) % 4))
    )


def x_shift(value, k):
    return lax.ppermute(
        value, BOTH, all_pairs(lambda yl, x, c, yh, z: (yl, (x + k) % 4, c, yh, z))
    )


def core_flip(value):
    return lax.ppermute(value, BOTH, all_pairs(lambda yl, x, c, yh, z: (yl, x, 1 - c, yh, z)))


def y_flip(value, lo, hi):
    return lax.ppermute(
        value, BOTH, all_pairs(lambda yl, x, c, yh, z: (yl ^ lo, x, c, yh ^ hi, z))
    )


def z_gather(value):
    return [value] + [z_shift(value, -k) for k in (1, 2, 3)]


def z_scatter(partial):
    rows = partial.shape[0] // 4
    terms = [partial[:rows]]
    for k in (1, 2, 3):
        terms.append(z_shift(partial[k * rows : (k + 1) * rows], k))
    return terms


def add_terms(terms):
    total = terms[0].astype(F32)
    for term in terms[1:]:
        total = total + term.astype(F32)
    return total


def dot(left, right):
    return jnp.dot(left, right, preferred_element_type=F32)


def dot_t(left, right):
    return lax.dot_general(left, right, (((1,), (1,)), ((), ())), preferred_element_type=F32)


def t_dot(left, right):
    return lax.dot_general(left, right, (((0,), (0,)), ((), ())), preferred_element_type=F32)


def after(value, *others):
    return lax.optimization_barrier((value,) + others)[0]


def pick(stacked, index, axis=0):
    return lax.dynamic_index_in_dim(stacked, index, axis, keepdims=False)


def pack_rows(vectors, rows, cols):
    total = jnp.zeros((rows, cols), vectors[0].dtype)
    for i, vec in enumerate(vectors):
        total = total + jnp.pad(
            vec.reshape(1, -1), ((i, rows - 1 - i), (0, cols - vec.shape[0]))
        )
    return total


def pack_qkv_kernel(w_ref, *refs):
    out_ref = refs[-1]
    out_ref[:, 128:] = jnp.zeros((8, 16, 768), BF)
    for f in range(8):
        for part in range(6):
            at = 512 * part + 128 * (f % 4)
            out_ref[f, :128, 128 * part : 128 * (part + 1)] = w_ref[:, at : at + 128]
    row_of = lax.broadcasted_iota(jnp.int32, (16, 1), 0)
    total = jnp.zeros((16, 768), F32)
    for i, v_ref in enumerate(refs[:-1]):
        vec = v_ref[...].astype(F32)
        wide = vec
        if vec.shape[1] < 768:
            wide = jnp.concatenate([vec, jnp.zeros((1, 768 - vec.shape[1]), F32)], axis=1)
        total = jnp.where(row_of == i, wide, total)
    for f in range(8):
        out_ref[f, 128:] = total.astype(BF)


def pack_qkv(w_qkv, vectors):
    return pl.pallas_call(
        pack_qkv_kernel,
        out_shape=jax.ShapeDtypeStruct((8, 144, 768), BF),
        compiler_params=pltpu.CompilerParams(vmem_limit_bytes=8 * 1024 * 1024),
        name="pack_qkv",
    )(w_qkv, *[v.reshape(1, -1) for v in vectors])


def pack_up_kernel(w_ref, out_ref):
    for z in range(4):
        for part in range(2):
            at = 2048 * part + 512 * z
            out_ref[z, :, 512 * part : 512 * (part + 1)] = w_ref[:, at : at + 512]


def pack_up(w_up):
    return pl.pallas_call(
        pack_up_kernel,
        out_shape=jax.ShapeDtypeStruct((4, 128, 1024), BF),
        compiler_params=pltpu.CompilerParams(vmem_limit_bytes=8 * 1024 * 1024),
        name="pack_up",
    )(w_up)


def project_kernel(t0_ref, t1_ref, t2_ref, t3_ref, w_ref, bias_ref, q_ref, kv_ref):
    weights = jnp.concatenate([w_ref[f, :128] for f in range(8)], axis=0)
    width = q_ref.shape[1]
    for i, t_ref in enumerate((t0_ref, t1_ref, t2_ref, t3_ref)):
        rows = pl.ds(128 * i, 128)
        out = dot(t_ref[...], weights)
        queries = (out[:, :width] + bias_ref[0:1]).astype(BF).astype(F32)
        q_ref[rows] = (queries * HEAD_DIM**-0.5).astype(BF)
        kv_ref[rows, :width] = out[:, width : 2 * width].astype(BF)
        kv_ref[rows, width:] = (out[:, 2 * width :] + bias_ref[1:2]).astype(BF)


def project(token_blocks, weights, bias):
    rows = 4 * token_blocks[0].shape[0]
    width = bias.shape[1]
    return pl.pallas_call(
        project_kernel,
        out_shape=[
            jax.ShapeDtypeStruct((rows, width), BF),
            jax.ShapeDtypeStruct((rows, 2 * width), BF),
        ],
        compiler_params=pltpu.CompilerParams(vmem_limit_bytes=12 * 1024 * 1024),
        cost_estimate=pl.CostEstimate(
            flops=6 * rows * 1024 * width, bytes_accessed=4 * 1024 * 1024, transcendentals=0
        ),
        name="project",
    )(*token_blocks, weights, bias)


def attend_kernel(q_ref, own_ref, far_ref, mask_ref, ok_ref, w_ref, ctx_ref, p_ref, out_ref):
    queries = q_ref[...]
    width = queries.shape[1]
    half = own_ref.shape[0]
    head_of = lax.broadcasted_iota(jnp.int32, (1, width), 1) // HEAD_DIM
    context = jnp.zeros(queries.shape, F32)
    for h in range(width // HEAD_DIM):
        q_h = jnp.where(head_of == h, queries, jnp.zeros_like(queries))
        s_own = dot_t(q_h, own_ref[:, :width]) + mask_ref[:, :half]
        s_far = dot_t(q_h, far_ref[:, :width]) + mask_ref[:, half:]
        top = jnp.maximum(
            jnp.max(s_own, axis=1, keepdims=True), jnp.max(s_far, axis=1, keepdims=True)
        )
        e_own = jnp.exp(s_own - top)
        e_far = jnp.exp(s_far - top)
        scale = 1.0 / (
            jnp.sum(e_own, axis=1, keepdims=True) + jnp.sum(e_far, axis=1, keepdims=True)
        )
        p_own = (e_own * scale).astype(BF)
        p_far = (e_far * scale).astype(BF)
        p_ref[h, :, :half] = p_own
        p_ref[h, :, half:] = p_far
        out = dot(p_own, own_ref[:, width:]) + dot(p_far, far_ref[:, width:])
        context = jnp.where(head_of == h, out, context)
    low = (context * ok_ref[...]).astype(BF)
    ctx_ref[...] = low
    out_ref[...] = dot(low, w_ref[...]).astype(BF)


def attend(queries, kv_own, kv_far, key_mask, row_ok, out_w):
    rows, width = queries.shape
    heads = width // HEAD_DIM
    keys = 2 * kv_own.shape[0]
    step = 256
    return pl.pallas_call(
        attend_kernel,
        grid=(rows // step,),
        in_specs=[
            pl.BlockSpec((step, width), lambda i: (i, 0)),
            pl.BlockSpec(kv_own.shape, lambda i: (0, 0)),
            pl.BlockSpec(kv_far.shape, lambda i: (0, 0)),
            pl.BlockSpec((1, keys), lambda i: (0, 0)),
            pl.BlockSpec((step, 1), lambda i: (i, 0)),
            pl.BlockSpec(out_w.shape, lambda i: (0, 0)),
        ],
        out_specs=[
            pl.BlockSpec((step, width), lambda i: (i, 0)),
            pl.BlockSpec((heads, step, keys), lambda i: (0, i, 0)),
            pl.BlockSpec((step, out_w.shape[1]), lambda i: (i, 0)),
        ],
        out_shape=[
            jax.ShapeDtypeStruct((rows, width), BF),
            jax.ShapeDtypeStruct((heads, rows, keys), BF),
            jax.ShapeDtypeStruct((rows, out_w.shape[1]), BF),
        ],
        compiler_params=pltpu.CompilerParams(vmem_limit_bytes=20 * 1024 * 1024),
        cost_estimate=pl.CostEstimate(
            flops=16 * rows * keys * width, bytes_accessed=6 * 1024 * 1024, transcendentals=0
        ),
        name="attend",
    )(queries, kv_own, kv_far, key_mask, row_ok, out_w)


def attend_back_kernel(
    q_ref,
    own_ref,
    far_ref,
    grad_ref,
    ok_ref,
    w_ref,
    p_ref,
    here_ref,
    far_grad_ref,
    acc_own,
    acc_far,
):
    at = pl.program_id(0)
    queries = q_ref[...]
    grads = (dot_t(grad_ref[...], w_ref[...]) * ok_ref[...]).astype(BF)
    width = queries.shape[1]
    half = own_ref.shape[0]
    head_of = lax.broadcasted_iota(jnp.int32, (1, width), 1) // HEAD_DIM
    zero = jnp.zeros_like(queries)

    @pl.when(at == 0)
    def _():
        acc_own[...] = jnp.zeros_like(acc_own)
        acc_far[...] = jnp.zeros_like(acc_far)

    d_queries = jnp.zeros(queries.shape, F32)
    for h in range(width // HEAD_DIM):
        q_h = jnp.where(head_of == h, queries, zero)
        g_h = jnp.where(head_of == h, grads, zero)
        p_own_low = p_ref[h, :, :half]
        p_far_low = p_ref[h, :, half:]
        p_own = p_own_low.astype(F32)
        p_far = p_far_low.astype(F32)
        t_own = p_own * dot_t(g_h, own_ref[:, width:])
        t_far = p_far * dot_t(g_h, far_ref[:, width:])
        inner = jnp.sum(t_own, axis=1, keepdims=True) + jnp.sum(t_far, axis=1, keepdims=True)
        ds_own = (t_own - p_own * inner).astype(BF)
        ds_far = (t_far - p_far * inner).astype(BF)
        out = dot(ds_own, own_ref[:, :width]) + dot(ds_far, far_ref[:, :width])
        d_queries = jnp.where(head_of == h, out, d_queries)
        acc_own[:, :width] += t_dot(ds_own, q_h)
        acc_far[:, :width] += t_dot(ds_far, q_h)
        acc_own[:, width:] += t_dot(p_own_low, g_h)
        acc_far[:, width:] += t_dot(p_far_low, g_h)
    rows = pl.ds(pl.multiple_of(at * queries.shape[0], queries.shape[0]), queries.shape[0])
    here_ref[rows, :width] = (d_queries * HEAD_DIM**-0.5).astype(BF)

    @pl.when(at == pl.num_programs(0) - 1)
    def _():
        here_ref[:, width:] = acc_own[...].astype(BF)
        far_grad_ref[...] = acc_far[...].astype(BF)


def attend_back(queries, kv_own, kv_far, d_attn, row_ok, out_w, probs):
    rows, width = queries.shape
    heads, _, keys = probs.shape
    step = 256
    return pl.pallas_call(
        attend_back_kernel,
        grid=(rows // step,),
        in_specs=[
            pl.BlockSpec((step, width), lambda i: (i, 0)),
            pl.BlockSpec(kv_own.shape, lambda i: (0, 0)),
            pl.BlockSpec(kv_far.shape, lambda i: (0, 0)),
            pl.BlockSpec((step, d_attn.shape[1]), lambda i: (i, 0)),
            pl.BlockSpec((step, 1), lambda i: (i, 0)),
            pl.BlockSpec(out_w.shape, lambda i: (0, 0)),
            pl.BlockSpec((heads, step, keys), lambda i: (0, i, 0)),
        ],
        out_specs=[
            pl.BlockSpec((rows, 3 * width), lambda i: (0, 0)),
            pl.BlockSpec(kv_own.shape, lambda i: (0, 0)),
        ],
        out_shape=[
            jax.ShapeDtypeStruct((rows, 3 * width), BF),
            jax.ShapeDtypeStruct(kv_own.shape, BF),
        ],
        scratch_shapes=[pltpu.VMEM(kv_own.shape, F32), pltpu.VMEM(kv_own.shape, F32)],
        compiler_params=pltpu.CompilerParams(vmem_limit_bytes=24 * 1024 * 1024),
        cost_estimate=pl.CostEstimate(
            flops=40 * rows * keys * width, bytes_accessed=8 * 1024 * 1024, transcendentals=0
        ),
        name="attend_back",
    )(queries, kv_own, kv_far, d_attn, row_ok, out_w, probs)


def grad_second_kernel(
    tok_ref, tok_far_ref, here_ref, far_ref, ctx_ref, attn_ref, sums_ref, out_ref, vec_ref
):
    grads = t_dot(tok_ref[...], here_ref[...])
    grads_far = t_dot(tok_far_ref[...], far_ref[...])
    queries = grads[:, :256].astype(BF)
    others = (grads[:, 256:] + grads_far).astype(BF)
    attn = t_dot(ctx_ref[...], attn_ref[...]).astype(BF)
    for p in range(8):
        for z in range(4):
            rows = slice(128 * z + 16 * p, 128 * z + 16 * p + 16)
            to = slice(16 * z, 16 * z + 16)
            out_ref[p // 4, p % 4, 0, to, :256] = queries[rows]
            out_ref[p // 4, p % 4, 0, to, 256:768] = others[rows]
            out_ref[p // 4, p % 4, 0, to, 768:] = attn[
                16 * p : 16 * p + 16, 256 * z : 256 * z + 256
            ]

    @pl.when(pl.program_id(0) == 0)
    def _():
        here = jnp.sum(here_ref[...].astype(F32), axis=0, keepdims=True)
        far = jnp.sum(far_ref[...].astype(F32), axis=0, keepdims=True)
        bias = jnp.concatenate(
            [here[:, :256], here[:, 512:] + far[:, 256:], jnp.zeros((1, 512), F32)], axis=1
        )
        attn_sum = jnp.sum(attn_ref[...].astype(F32), axis=0, keepdims=True)
        row_of = lax.broadcasted_iota(jnp.int32, (16, 1), 0)
        total = jnp.where(row_of == 0, bias, sums_ref[...])
        vec_ref[...] = jnp.where(row_of == 2, attn_sum, total).astype(BF)


def grad_second(tokens_own, tokens_far, d_here, d_far, context, d_attn, sums):
    rows, cols = tokens_own.shape
    half = cols // 2
    return pl.pallas_call(
        grad_second_kernel,
        grid=(2,),
        in_specs=[
            pl.BlockSpec((rows, half), lambda i: (0, i)),
            pl.BlockSpec((rows, half), lambda i: (0, i)),
            pl.BlockSpec(d_here.shape, lambda i: (0, 0)),
            pl.BlockSpec(d_far.shape, lambda i: (0, 0)),
            pl.BlockSpec((rows, context.shape[1] // 2), lambda i: (0, i)),
            pl.BlockSpec(d_attn.shape, lambda i: (0, 0)),
            pl.BlockSpec(sums.shape, lambda i: (0, 0)),
        ],
        out_specs=[
            pl.BlockSpec((2, 4, 1, 64, 1024), lambda i: (0, 0, i, 0, 0)),
            pl.BlockSpec(sums.shape, lambda i: (0, 0)),
        ],
        out_shape=[
            jax.ShapeDtypeStruct((2, 4, 2, 64, 1024), BF),
            jax.ShapeDtypeStruct(sums.shape, BF),
        ],
        compiler_params=pltpu.CompilerParams(vmem_limit_bytes=20 * 1024 * 1024),
        cost_estimate=pl.CostEstimate(
            flops=3 * rows * cols * 1024, bytes_accessed=8 * 1024 * 1024, transcendentals=0
        ),
        name="grad_second",
    )(tokens_own, tokens_far, d_here, d_far, context, d_attn, sums)


def norm_stats(values):
    mean = jnp.mean(values, axis=-1, keepdims=True)
    centered = values - mean
    rstd = lax.rsqrt(jnp.mean(centered * centered, axis=-1, keepdims=True) + EPSILON)
    return centered * rstd, rstd


def norm_back(grad_out, gain, xhat, rstd):
    g = grad_out * gain
    return rstd * (
        g
        - jnp.mean(g, axis=-1, keepdims=True)
        - xhat * jnp.mean(g * xhat, axis=-1, keepdims=True)
    )


def unroll_ring(blocks, index):
    stacked = jnp.concatenate([b[None] for b in blocks + blocks], axis=0)
    return lax.dynamic_slice_in_dim(stacked, (4 - index) % 4, 4, axis=0)


def swap(value, axis, groups):
    return lax.all_to_all(value, axis, 0, 0, axis_index_groups=groups, tiled=True)


Z_RINGS = [[0, 1, 2, 3], [4, 5, 6, 7]]
X_RINGS = [[8 * yl + 2 * x + core for x in range(4)] for yl in range(2) for core in range(2)]


def with_rows(block, vectors):
    flat = block.reshape(-1, block.shape[-1])
    return flat if vectors is None else jnp.concatenate([flat, vectors], axis=0)


def core_send(pieces, vectors, core):
    return core_flip(with_rows(pick(pieces, 1 - core).reshape(8, -1, pieces.shape[-1]), vectors))


def core_sum(pieces, vectors, got, core):
    mine = pick(pieces, core)
    rows = mine.size // mine.shape[-1]
    total = (mine.astype(F32) + got[:rows].reshape(mine.shape).astype(F32)).astype(BF)
    if vectors is None:
        return total, None
    return total, (vectors.astype(F32) + got[rows:].astype(F32)).astype(BF)


def x_send(pieces, x):
    return [pick(pieces, x)] + [x_shift(pick(pieces, (x + k) % 4), k) for k in (1, 2, 3)]


def x_swap(pieces, vectors):
    flat = pieces.reshape(4, -1, pieces.shape[-1])
    if vectors is not None:
        flat = jnp.concatenate([flat, jnp.broadcast_to(vectors, (4,) + vectors.shape)], axis=1)
    return swap(flat, "replica", X_RINGS)


def x_sum(got, rows):
    total = jnp.sum(got.astype(F32), axis=0).astype(BF)
    return total[: 2 * rows].reshape(2, rows, -1), total[2 * rows :]


def y_send(pieces, vectors, yh):
    own, other = pick(pieces, yh), pick(pieces, 1 - yh)
    got = [
        y_flip(with_rows(block, vectors), lo, hi)
        for block, lo, hi in ((own, 1, 0), (other, 0, 1), (other, 1, 1))
    ]
    return [with_rows(own, vectors)] + got


def spread(piece):
    ring = jnp.stack([piece] + [x_shift(piece, -k) for k in (1, 2, 3)], axis=0)
    return ring, core_flip(ring)


def lay_first_kernel(where_ref, ring_ref, far_ref, down_ref, up_ref):
    def lay(src_ref):
        for k in range(4):
            x = (where_ref[2] + k) % 4
            down_ref[pl.ds(pl.multiple_of(64 * x, 64), 64)] = src_ref[k, :64].astype(F32)
            rows = pl.ds(pl.multiple_of(16 * x, 16), 16)
            for z in range(4):
                block = src_ref[k, 64 + 16 * z : 80 + 16 * z].astype(F32)
                up_ref[rows, 512 * z : 512 * (z + 1)] = block[:, :512]
                up_ref[rows, 2048 + 512 * z : 2048 + 512 * (z + 1)] = block[:, 512:]

    at = pl.program_id(0)
    pl.when(at == 0)(lambda: lay(ring_ref))
    pl.when(at == 1)(lambda: lay(far_ref))


def lay_second_kernel(where_ref, ring_ref, far_ref, qkv_ref, out_ref):
    def lay(src_ref):
        for k in range(4):
            rows = pl.ds(pl.multiple_of(16 * ((where_ref[2] + k) % 4), 16), 16)
            for z in range(4):
                block = src_ref[k, 16 * z : 16 * (z + 1)].astype(F32)
                for part in range(6):
                    at = 512 * part + 128 * z
                    qkv_ref[rows, at : at + 128] = block[:, 128 * part : 128 * (part + 1)]
                out_ref[rows, 256 * z : 256 * (z + 1)] = block[:, 768:]

    at = pl.program_id(0)
    pl.when(at == 0)(lambda: lay(ring_ref))
    pl.when(at == 1)(lambda: lay(far_ref))


def lay_pieces(kernel, ring, far, blocks, place, name):
    x, core = place[1], place[2]
    where = jnp.stack([core, 1 - core, x]).astype(jnp.int32)
    return pl.pallas_call(
        kernel,
        grid_spec=pltpu.PrefetchScalarGridSpec(
            num_scalar_prefetch=1,
            grid=(2,),
            in_specs=[
                pl.BlockSpec(ring.shape, lambda i, where: (0, 0, 0)),
                pl.BlockSpec(far.shape, lambda i, where: (0, 0, 0)),
            ],
            out_specs=[
                pl.BlockSpec((4 * rows, cols), lambda i, where: (where[i], 0))
                for rows, cols in blocks
            ],
        ),
        out_shape=[jax.ShapeDtypeStruct((8 * rows, cols), F32) for rows, cols in blocks],
        compiler_params=pltpu.CompilerParams(vmem_limit_bytes=16 * 1024 * 1024),
        name=name,
    )(where, ring, far)


def on_device(
    tokens,
    counts,
    w_qkv,
    bias_qv,
    w_out,
    bias_out,
    gain_attn,
    shift_attn,
    w_up,
    bias_up,
    w_down,
    bias_down,
    gain_ffn,
    shift_ffn,
    cotangent,
):
    row_count, model_width = tokens.shape
    replica = lax.axis_index("replica")
    group = lax.axis_index("fsdp")
    yl, x, core = replica // 8, (replica // 2) % 4, replica % 2
    yh, z = group // 4, group % 4
    place = (yl, x, core, yh, z)
    lanes = 128
    counts_row = counts[0]

    ring = (z + jnp.arange(4, dtype=jnp.int32)) % 4
    own_counts = jnp.take(counts_row, yh * 4 + ring)
    far_counts = jnp.take(counts_row, (1 - yh) * 4 + ring)
    slot = jnp.arange(row_count, dtype=jnp.int32)
    own_ok = (slot[None, :] < own_counts[:, None]).reshape(-1)
    far_ok = (slot[None, :] < far_counts[:, None]).reshape(-1)
    key_mask = jnp.where(jnp.concatenate([own_ok, far_ok]), 0.0, -1e30).astype(F32)[None, :]
    row_ok = own_ok.astype(F32)[:, None]

    small = (bias_qv, bias_out, gain_attn, shift_attn, bias_up, bias_down, gain_ffn, shift_ffn)
    sent = pack_qkv(w_qkv, small)
    up_sent = pack_up(w_up)
    token_blocks = z_gather(tokens)
    out_far = y_flip(w_out, 0, 1)
    got = lax.all_to_all(sent, "fsdp", 0, 0, tiled=True)
    vec_all = got[:, row_count : row_count + 8].astype(F32)
    bias_own = pick(vec_all[:, 0, :256].reshape(2, 2, 4, lanes), z, 2).reshape(2, 2 * lanes)
    bout_all = vec_all[:, 1, :lanes].reshape(1, -1)
    ga_all = vec_all[:, 2, :lanes].reshape(1, -1)
    sa_all = vec_all[:, 3, :lanes].reshape(1, -1)
    bup_own = pick(vec_all[:, 4, :512].reshape(2, 4, 512), z, 1).reshape(1, -1)
    bdown_all = vec_all[:, 5, :lanes].reshape(1, -1)
    gf_all = vec_all[:, 6, :lanes].reshape(1, -1)
    sf_all = vec_all[:, 7, :lanes].reshape(1, -1)

    tokens_all = jnp.concatenate(token_blocks, axis=0)
    queries, kv_own = project(token_blocks, got, bias_own)
    kv_far = y_flip(kv_own, 0, 1)

    up_half = swap(after(up_sent, kv_own), "fsdp", Z_RINGS).reshape(4 * row_count, 1024)

    up_mine = y_flip(pick(after(up_half, kv_far).reshape(2, 256, 1024), core), 0, 1)
    down_mine = y_flip(after(pick(w_down.reshape(2, 256, 1024), core), up_mine), 0, 1)
    far_mine = (up_mine, down_mine)
    far_other = (core_flip(up_mine), core_flip(down_mine))
    up_far = jnp.where(
        core == 0,
        jnp.concatenate([far_mine[0], far_other[0]], axis=0),
        jnp.concatenate([far_other[0], far_mine[0]], axis=0),
    )
    down_far = jnp.where(
        core == 0,
        jnp.concatenate([far_mine[1], far_other[1]], axis=0),
        jnp.concatenate([far_other[1], far_mine[1]], axis=0),
    )
    tokens_far = y_flip(after(tokens_all, down_far), 0, 1)
    qkv_w = got[:, :row_count].reshape(8 * row_count, 6 * lanes)

    def order(own, far):
        return jnp.where(
            yh == 0, jnp.concatenate([own, far], axis=0), jnp.concatenate([far, own], axis=0)
        )

    out_w = order(w_out, out_far)
    up_w = order(up_half, up_far)
    down_w = order(w_down, down_far)

    context, probs, attn_part = attend(queries, kv_own, kv_far, key_mask, row_ok, out_w)
    resid1 = add_terms([tokens] + z_scatter(attn_part)) + bout_all
    xhat1, rstd1 = norm_stats(resid1)
    normed = xhat1 * ga_all + sa_all
    normed_all = jnp.concatenate(z_gather(normed.astype(BF)), axis=0)
    hidden = dot(normed_all, up_w) + bup_own
    cdf = 0.5 * (1.0 + lax.erf(hidden * 0.7071067811865476))
    active = (hidden * cdf).astype(BF)
    slope = cdf + hidden * (0.3989422804014327 * jnp.exp(-0.5 * hidden * hidden))
    ffn_part = dot(active, down_w).astype(BF)
    resid2 = add_terms([normed] + z_scatter(ffn_part)) + bdown_all
    xhat2, rstd2 = norm_stats(resid2)
    layer_out = (xhat2 * gf_all + sf_all).astype(BF)

    cot = cotangent.astype(F32)
    d_resid2 = norm_back(cot, gf_all, xhat2, rstd2)

    dffn_all = jnp.concatenate(z_gather(d_resid2.astype(BF)), axis=0)
    d_hidden = (slope * dot_t(dffn_all, down_w)).astype(BF)
    dn_part = dot_t(d_hidden, up_w).astype(BF)
    dn_terms = z_scatter(dn_part)

    grad_down = t_dot(active, dffn_all).astype(BF)
    grad_up = t_dot(normed_all, d_hidden).astype(BF)
    first = jnp.concatenate(
        [
            grad_down.reshape(2, 8, 64, 1024),
            grad_up.reshape(2, 4, 8, 16, 1024).transpose(0, 2, 1, 3, 4).reshape(2, 8, 64, 1024),
        ],
        axis=2,
    )
    first = first.transpose(1, 0, 2, 3).reshape(2, 4, 2, 128, 1024)
    first_got = core_send(first, None, core)

    d_normed = add_terms([d_resid2] + dn_terms)
    d_resid1 = norm_back(d_normed, ga_all, xhat1, rstd1)
    dattn_blocks = z_gather(d_resid1.astype(BF))
    first_core, _ = core_sum(first, None, after(first_got, d_resid1), core)
    first_got = x_send(first_core, x)
    dattn_all = jnp.concatenate(dattn_blocks, axis=0)
    d_here, dkv_far = attend_back(
        queries, kv_own, kv_far, dattn_all, row_ok, out_w, probs
    )

    zero = jnp.zeros((1024,), F32)
    sums = pack_rows(
        [
            zero,
            jnp.sum(d_hidden.astype(F32), axis=0),
            zero,
            jnp.sum(dffn_all.astype(F32), axis=0),
            jnp.sum(d_normed * xhat1, axis=0),
            jnp.sum(d_normed, axis=0),
            jnp.sum(cot * xhat2, axis=0),
            jnp.sum(cot, axis=0),
        ],
        16,
        1024,
    )
    far_terms = y_flip(dkv_far, 0, 1)
    second, vectors = grad_second(
        tokens_all, tokens_far, after(d_here, *first_got), dkv_far, context, dattn_all, sums
    )

    second_got = core_send(second, vectors, core)
    first_x = add_terms(after(tuple(first_got), second)).astype(BF)
    first_terms = y_send(after(first_x, far_terms), None, yh)
    second_core, vec_core = core_sum(second, vectors, after(second_got, first_x), core)
    second_got = x_swap(second_core, vec_core)

    dkv = (d_here[:, 256:].astype(F32) + far_terms.astype(F32)).astype(BF)
    d_projected = jnp.concatenate([d_here[:, :256], dkv], axis=1)
    input_part = dot_t(after(d_projected, second_core), qkv_w).astype(BF)
    input_terms = z_scatter(input_part)

    first_terms = after(tuple(first_terms), second_core, input_part)
    first_sum = add_terms(first_terms).astype(BF)
    second_x, vec_x = x_sum(after(second_got, first_sum), 64)
    second_terms = y_send(second_x, vec_x, yh)
    input_terms = after(tuple(input_terms), second_x)
    input_grad = add_terms([d_resid1] + list(input_terms))

    up_sum = swap(after(first_sum, input_grad)[64:].reshape(4, 16, 1024), "fsdp", Z_RINGS)
    up_sum = up_sum.reshape(64, 1024)
    ring, far = spread(jnp.concatenate([first_sum[:64], up_sum], axis=0))
    grad_w_down, grad_w_up = lay_pieces(
        lay_first_kernel, ring, far, ((64, 1024), (16, 4096)), place, "lay_first"
    )

    second_all = add_terms(after(tuple(second_terms), up_sum)).astype(BF)
    second_sum, vec_sum = second_all[:64], second_all[64:]
    bias_row = jnp.broadcast_to(vec_sum[None, 0:1, :512], (4, 1, 512))
    norm_row = pick(vec_sum[4:8].reshape(4, 2, 4, lanes), yh, 1).transpose(1, 0, 2)
    side = jnp.pad(
        jnp.concatenate([bias_row, norm_row.reshape(4, 1, 512)], axis=1),
        ((0, 0), (0, 14), (0, 256)),
    )
    swapped = swap(
        jnp.concatenate([second_sum[:, :768].reshape(4, 16, 768), side], axis=1), "fsdp", Z_RINGS
    )
    swapped = after(swapped, ring)
    ring, far = spread(
        jnp.concatenate([swapped[:, :16].reshape(64, 768), second_sum[:, 768:]], axis=1)
    )
    grad_w_qkv, grad_w_out = lay_pieces(
        lay_second_kernel, ring, far, ((16, 3072), (16, 1024)), place, "lay_second"
    )
    bqv_all = swapped[:, 16, :512].astype(F32).reshape(4, 2, 2, lanes).transpose(1, 2, 0, 3)
    grad_bqv = pick(bqv_all.reshape(8, 256), group)
    norms = jnp.sum(swapped[:, 17, :512].astype(F32), axis=0).reshape(4, lanes)
    grad_bup = pick(vec_sum[1].reshape(2, 512), yh).astype(F32)
    rest = pick(vec_sum[2:4].reshape(2, 8, lanes), group, 1).astype(F32)

    return (
        layer_out,
        input_grad,
        grad_w_qkv,
        grad_bqv,
        grad_w_out,
        rest[0],
        norms[0],
        norms[1],
        grad_w_up,
        grad_bup,
        grad_w_down,
        rest[1],
        norms[2],
        norms[3],
    )


def solution(mesh):
    in_specs = (
        P(("replica", "fsdp"), None),
        P("replica", None),
        P("fsdp", None),
        P("fsdp"),
        P("fsdp", None),
        P("fsdp"),
        P("fsdp"),
        P("fsdp"),
        P("fsdp", None),
        P("fsdp"),
        P("fsdp", None),
        P("fsdp"),
        P("fsdp"),
        P("fsdp"),
        P(("replica", "fsdp"), None),
    )
    out_specs = (
        P(("replica", "fsdp"), None),
        P(("replica", "fsdp"), None),
        P("fsdp", None),
        P("fsdp"),
        P("fsdp", None),
        P("fsdp"),
        P("fsdp"),
        P("fsdp"),
        P("fsdp", None),
        P("fsdp"),
        P("fsdp", None),
        P("fsdp"),
        P("fsdp"),
        P("fsdp"),
    )
    return jax.shard_map(
        on_device, mesh=mesh, in_specs=in_specs, out_specs=out_specs, check_vma=False
    )
```

```python
import functools

import jax
import jax.numpy as jnp
from jax import lax
from jax.experimental import pallas as pl
from jax.experimental.pallas import tpu as pltpu
from jax.sharding import PartitionSpec as P

HEAD_DIM = 64
EPSILON = 1e-05
BF = jnp.bfloat16
F32 = jnp.float32
BOTH = ("replica", "fsdp")


def all_pairs(move):
    pairs = []
    for yl in range(2):
        for x in range(4):
            for core in range(2):
                for yh in range(2):
                    for z in range(4):
                        a, b, c, d, e = move(yl, x, core, yh, z)
                        pairs.append(
                            (
                                ((yl * 4 + x) * 2 + core) * 8 + yh * 4 + z,
                                ((a * 4 + b) * 2 + c) * 8 + d * 4 + e,
                            )
                        )
    return pairs


def z_shift(value, k):
    return lax.ppermute(
        value, BOTH, all_pairs(lambda yl, x, c, yh, z: (yl, x, c, yh, (z + k) % 4))
    )


def x_shift(value, k):
    return lax.ppermute(
        value, BOTH, all_pairs(lambda yl, x, c, yh, z: (yl, (x + k) % 4, c, yh, z))
    )


def core_flip(value):
    return lax.ppermute(value, BOTH, all_pairs(lambda yl, x, c, yh, z: (yl, x, 1 - c, yh, z)))


def y_flip(value, lo, hi):
    return lax.ppermute(
        value, BOTH, all_pairs(lambda yl, x, c, yh, z: (yl ^ lo, x, c, yh ^ hi, z))
    )


def z_gather(value):
    return [value] + [z_shift(value, -k) for k in (1, 2, 3)]


def z_scatter(partial):
    rows = partial.shape[0] // 4
    terms = [partial[:rows]]
    for k in (1, 2, 3):
        terms.append(z_shift(partial[k * rows : (k + 1) * rows], k))
    return terms


def add_terms(terms):
    total = terms[0].astype(F32)
    for term in terms[1:]:
        total = total + term.astype(F32)
    return total


def dot(left, right):
    return jnp.dot(left, right, preferred_element_type=F32)


def dot_t(left, right):
    return lax.dot_general(left, right, (((1,), (1,)), ((), ())), preferred_element_type=F32)


def t_dot(left, right):
    return lax.dot_general(left, right, (((0,), (0,)), ((), ())), preferred_element_type=F32)


def after(value, *others):
    return lax.optimization_barrier((value,) + others)[0]


def pick(stacked, index, axis=0):
    return lax.dynamic_index_in_dim(stacked, index, axis, keepdims=False)


def pack_rows(vectors, rows, cols):
    total = jnp.zeros((rows, cols), vectors[0].dtype)
    for i, vec in enumerate(vectors):
        total = total + jnp.pad(
            vec.reshape(1, -1), ((i, rows - 1 - i), (0, cols - vec.shape[0]))
        )
    return total


def rows_of(v_refs, cols):
    row_of = lax.broadcasted_iota(jnp.int32, (16, 1), 0)
    total = jnp.zeros((16, cols), F32)
    for i, v_ref in enumerate(v_refs):
        vec = v_ref[...].astype(F32)
        wide = jnp.concatenate([vec, jnp.zeros((1, cols - vec.shape[1]), F32)], axis=1)
        total = jnp.where(row_of == i, wide, total)
    return total.astype(BF)


def pack_kernel(width, core_ref, w_ref, *refs):
    out_ref = refs[-1]
    parts = w_ref.shape[1] // (4 * width)
    rows = rows_of(refs[:-1], out_ref.shape[2])
    for f in range(8):
        for part in range(parts):
            at = width * (4 * part + f % 4)
            out_ref[f, :64, width * part : width * (part + 1)] = w_ref[:, at : at + width]
        out_ref[f, 64:] = rows


def pack(weight, vectors, core, width, name):
    cols = weight.shape[1]
    out = (8, 80, cols // 4)
    return pl.pallas_call(
        functools.partial(pack_kernel, width),
        grid_spec=pltpu.PrefetchScalarGridSpec(
            num_scalar_prefetch=1,
            grid=(1,),
            in_specs=[pl.BlockSpec((64, cols), lambda i, core: (core[0], 0))]
            + [pl.BlockSpec((1, v.shape[0]), lambda i, core: (0, 0)) for v in vectors],
            out_specs=pl.BlockSpec(out, lambda i, core: (0, 0, 0)),
        ),
        out_shape=jax.ShapeDtypeStruct(out, BF),
        compiler_params=pltpu.CompilerParams(vmem_limit_bytes=8 * 1024 * 1024),
        name=name,
    )(core.reshape(1), weight, *[v.reshape(1, -1) for v in vectors])


def project_kernel(
    core_ref, t0_ref, t1_ref, t2_ref, t3_ref, own_ref, far_ref, bias_ref, q_ref, kv_ref, w_ref
):
    lay_halves(core_ref[0], own_ref, far_ref, w_ref)
    weights = w_ref[...]
    width = q_ref.shape[1]
    for i, t_ref in enumerate((t0_ref, t1_ref, t2_ref, t3_ref)):
        rows = pl.ds(128 * i, 128)
        out = dot(t_ref[...], weights)
        queries = (out[:, :width] + bias_ref[0:1]).astype(BF).astype(F32)
        q_ref[rows] = (queries * HEAD_DIM**-0.5).astype(BF)
        kv_ref[rows, :width] = out[:, width : 2 * width].astype(BF)
        kv_ref[rows, width:] = (out[:, 2 * width :] + bias_ref[1:2]).astype(BF)


def project(token_blocks, own, far, bias, core):
    rows = 4 * token_blocks[0].shape[0]
    width = bias.shape[1]
    vmem = pl.BlockSpec(memory_space=pltpu.VMEM)
    return pl.pallas_call(
        project_kernel,
        in_specs=[pl.BlockSpec(memory_space=pltpu.SMEM)] + [vmem] * 7,
        out_specs=[vmem] * 3,
        out_shape=[
            jax.ShapeDtypeStruct((rows, width), BF),
            jax.ShapeDtypeStruct((rows, 2 * width), BF),
            jax.ShapeDtypeStruct((1024, 3 * width), BF),
        ],
        compiler_params=pltpu.CompilerParams(vmem_limit_bytes=12 * 1024 * 1024),
        cost_estimate=pl.CostEstimate(
            flops=6 * rows * 1024 * width, bytes_accessed=4 * 1024 * 1024, transcendentals=0
        ),
        name="project",
    )(core.reshape(1), *token_blocks, own, far, bias)


def attend_kernel(q_ref, own_ref, far_ref, mask_ref, ok_ref, w_ref, ctx_ref, p_ref, out_ref):
    queries = q_ref[...]
    width = queries.shape[1]
    half = own_ref.shape[0]
    head_of = lax.broadcasted_iota(jnp.int32, (1, width), 1) // HEAD_DIM
    context = jnp.zeros(queries.shape, F32)
    for h in range(width // HEAD_DIM):
        q_h = jnp.where(head_of == h, queries, jnp.zeros_like(queries))
        s_own = dot_t(q_h, own_ref[:, :width]) + mask_ref[:, :half]
        s_far = dot_t(q_h, far_ref[:, :width]) + mask_ref[:, half:]
        top = jnp.maximum(
            jnp.max(s_own, axis=1, keepdims=True), jnp.max(s_far, axis=1, keepdims=True)
        )
        e_own = jnp.exp(s_own - top)
        e_far = jnp.exp(s_far - top)
        scale = 1.0 / (
            jnp.sum(e_own, axis=1, keepdims=True) + jnp.sum(e_far, axis=1, keepdims=True)
        )
        p_own = (e_own * scale).astype(BF)
        p_far = (e_far * scale).astype(BF)
        p_ref[h, :, :half] = p_own
        p_ref[h, :, half:] = p_far
        out = dot(p_own, own_ref[:, width:]) + dot(p_far, far_ref[:, width:])
        context = jnp.where(head_of == h, out, context)
    low = (context * ok_ref[...]).astype(BF)
    ctx_ref[...] = low
    out_ref[...] = dot(low, w_ref[...]).astype(BF)


def attend(queries, kv_own, kv_far, key_mask, row_ok, out_w):
    rows, width = queries.shape
    heads = width // HEAD_DIM
    keys = 2 * kv_own.shape[0]
    step = 256
    return pl.pallas_call(
        attend_kernel,
        grid=(rows // step,),
        in_specs=[
            pl.BlockSpec((step, width), lambda i: (i, 0)),
            pl.BlockSpec(kv_own.shape, lambda i: (0, 0)),
            pl.BlockSpec(kv_far.shape, lambda i: (0, 0)),
            pl.BlockSpec((1, keys), lambda i: (0, 0)),
            pl.BlockSpec((step, 1), lambda i: (i, 0)),
            pl.BlockSpec(out_w.shape, lambda i: (0, 0)),
        ],
        out_specs=[
            pl.BlockSpec((step, width), lambda i: (i, 0)),
            pl.BlockSpec((heads, step, keys), lambda i: (0, i, 0)),
            pl.BlockSpec((step, out_w.shape[1]), lambda i: (i, 0)),
        ],
        out_shape=[
            jax.ShapeDtypeStruct((rows, width), BF),
            jax.ShapeDtypeStruct((heads, rows, keys), BF),
            jax.ShapeDtypeStruct((rows, out_w.shape[1]), BF),
        ],
        compiler_params=pltpu.CompilerParams(vmem_limit_bytes=16 * 1024 * 1024),
        cost_estimate=pl.CostEstimate(
            flops=16 * rows * keys * width, bytes_accessed=6 * 1024 * 1024, transcendentals=0
        ),
        name="attend",
    )(queries, kv_own, kv_far, key_mask, row_ok, out_w)


def attend_back_kernel(
    q_ref,
    own_ref,
    far_ref,
    grad_ref,
    ok_ref,
    w_ref,
    p_ref,
    here_ref,
    far_grad_ref,
    acc_own,
    acc_far,
):
    at = pl.program_id(0)
    queries = q_ref[...]
    grads = (dot_t(grad_ref[...], w_ref[...]) * ok_ref[...]).astype(BF)
    width = queries.shape[1]
    half = own_ref.shape[0]
    head_of = lax.broadcasted_iota(jnp.int32, (1, width), 1) // HEAD_DIM
    zero = jnp.zeros_like(queries)

    @pl.when(at == 0)
    def _():
        acc_own[...] = jnp.zeros_like(acc_own)
        acc_far[...] = jnp.zeros_like(acc_far)

    d_queries = jnp.zeros(queries.shape, F32)
    for h in range(width // HEAD_DIM):
        q_h = jnp.where(head_of == h, queries, zero)
        g_h = jnp.where(head_of == h, grads, zero)
        p_own_low = p_ref[h, :, :half]
        p_far_low = p_ref[h, :, half:]
        p_own = p_own_low.astype(F32)
        p_far = p_far_low.astype(F32)
        t_own = p_own * dot_t(g_h, own_ref[:, width:])
        t_far = p_far * dot_t(g_h, far_ref[:, width:])
        inner = jnp.sum(t_own, axis=1, keepdims=True) + jnp.sum(t_far, axis=1, keepdims=True)
        ds_own = (t_own - p_own * inner).astype(BF)
        ds_far = (t_far - p_far * inner).astype(BF)
        out = dot(ds_own, own_ref[:, :width]) + dot(ds_far, far_ref[:, :width])
        d_queries = jnp.where(head_of == h, out, d_queries)
        acc_own[:, :width] += t_dot(ds_own, q_h)
        acc_far[:, :width] += t_dot(ds_far, q_h)
        acc_own[:, width:] += t_dot(p_own_low, g_h)
        acc_far[:, width:] += t_dot(p_far_low, g_h)
    rows = pl.ds(pl.multiple_of(at * queries.shape[0], queries.shape[0]), queries.shape[0])
    here_ref[rows, :width] = (d_queries * HEAD_DIM**-0.5).astype(BF)

    @pl.when(at == pl.num_programs(0) - 1)
    def _():
        here_ref[:, width:] = acc_own[...].astype(BF)
        far_grad_ref[...] = acc_far[...].astype(BF)


def attend_back(queries, kv_own, kv_far, d_attn, row_ok, out_w, probs):
    rows, width = queries.shape
    heads, _, keys = probs.shape
    step = 256
    return pl.pallas_call(
        attend_back_kernel,
        grid=(rows // step,),
        in_specs=[
            pl.BlockSpec((step, width), lambda i: (i, 0)),
            pl.BlockSpec(kv_own.shape, lambda i: (0, 0)),
            pl.BlockSpec(kv_far.shape, lambda i: (0, 0)),
            pl.BlockSpec((step, d_attn.shape[1]), lambda i: (i, 0)),
            pl.BlockSpec((step, 1), lambda i: (i, 0)),
            pl.BlockSpec(out_w.shape, lambda i: (0, 0)),
            pl.BlockSpec((heads, step, keys), lambda i: (0, i, 0)),
        ],
        out_specs=[
            pl.BlockSpec((rows, 3 * width), lambda i: (0, 0)),
            pl.BlockSpec(kv_own.shape, lambda i: (0, 0)),
        ],
        out_shape=[
            jax.ShapeDtypeStruct((rows, 3 * width), BF),
            jax.ShapeDtypeStruct(kv_own.shape, BF),
        ],
        scratch_shapes=[pltpu.VMEM(kv_own.shape, F32), pltpu.VMEM(kv_own.shape, F32)],
        compiler_params=pltpu.CompilerParams(vmem_limit_bytes=20 * 1024 * 1024),
        cost_estimate=pl.CostEstimate(
            flops=40 * rows * keys * width, bytes_accessed=8 * 1024 * 1024, transcendentals=0
        ),
        name="attend_back",
    )(queries, kv_own, kv_far, d_attn, row_ok, out_w, probs)


def lay_halves(core, own_ref, far_ref, to_ref):
    def lay(low_ref, high_ref):
        for f in range(8):
            to_ref[128 * f : 128 * f + 64] = low_ref[f, :64]
            to_ref[128 * f + 64 : 128 * f + 128] = high_ref[f, :64]

    pl.when(core == 0)(lambda: lay(own_ref, far_ref))
    pl.when(core != 0)(lambda: lay(far_ref, own_ref))


def lay_down(where_ref, own_ref, mine_ref, other_ref, at, to_ref):
    def lay(from_ref):
        to_ref[...] = from_ref[...]

    own = where_ref[1] == at // 2
    mine = where_ref[0] == at % 2
    pl.when(own)(lambda: lay(own_ref))
    pl.when(jnp.logical_not(own) & mine)(lambda: lay(mine_ref))
    pl.when(jnp.logical_not(own) & jnp.logical_not(mine))(lambda: lay(other_ref))


def weight_specs(step, width):
    return [
        pl.BlockSpec((8, 64, step), lambda j, where: (0, 0, j)),
        pl.BlockSpec((8, 64, step), lambda j, where: (0, 0, j)),
        pl.BlockSpec((step, width), lambda j, where: (j % 2, 0)),
        pl.BlockSpec((step, width), lambda j, where: (0, 0)),
        pl.BlockSpec((step, width), lambda j, where: (0, 0)),
    ]


def ffn_kernel(
    where_ref, x0_ref, x1_ref, x2_ref, x3_ref, bias_ref, up_own_ref, up_far_ref, down_ref,
    down_mine_ref, down_other_ref, act_ref, slope_ref, part_ref, x_ref, acc_ref, up_ref, w_ref,
):
    at = pl.program_id(0)
    lay_halves(where_ref[0], up_own_ref, up_far_ref, up_ref)
    lay_down(where_ref, down_ref, down_mine_ref, down_other_ref, at, w_ref)

    @pl.when(at == 0)
    def _():
        for i, block_ref in enumerate((x0_ref, x1_ref, x2_ref, x3_ref)):
            x_ref[128 * i : 128 * (i + 1)] = block_ref[...]
        acc_ref[...] = jnp.zeros_like(acc_ref)

    hidden = dot(x_ref[...], up_ref[...]) + bias_ref[...]
    cdf = 0.5 * (1.0 + lax.erf(hidden * 0.7071067811865476))
    active = (hidden * cdf).astype(BF)
    act_ref[...] = active
    slope = cdf + hidden * (0.3989422804014327 * jnp.exp(-0.5 * hidden * hidden))
    slope_ref[...] = slope.astype(BF)
    acc_ref[...] += dot(active, w_ref[...])

    @pl.when(at == pl.num_programs(0) - 1)
    def _():
        part_ref[...] = acc_ref[...].astype(BF)


def ffn(blocks, bias, weights, where):
    rows, width = 4 * blocks[0].shape[0], 1024
    units, step = 1024, 256
    whole = pl.BlockSpec((rows, width), lambda j, where: (0, 0))
    part = pl.BlockSpec((rows, step), lambda j, where: (0, j))
    return pl.pallas_call(
        ffn_kernel,
        grid_spec=pltpu.PrefetchScalarGridSpec(
            num_scalar_prefetch=1,
            grid=(units // step,),
            in_specs=[pl.BlockSpec(blocks[0].shape, lambda j, where: (0, 0))] * 4
            + [pl.BlockSpec((1, step), lambda j, where: (0, j))]
            + weight_specs(step, width),
            out_specs=[part, part, whole, whole],
            scratch_shapes=[
                pltpu.VMEM((rows, width), F32),
                pltpu.VMEM((width, step), BF),
                pltpu.VMEM((step, width), BF),
            ],
        ),
        out_shape=[
            jax.ShapeDtypeStruct((rows, units), BF),
            jax.ShapeDtypeStruct((rows, units), BF),
            jax.ShapeDtypeStruct((rows, width), BF),
            jax.ShapeDtypeStruct((rows, width), BF),
        ],
        compiler_params=pltpu.CompilerParams(vmem_limit_bytes=18 * 1024 * 1024),
        cost_estimate=pl.CostEstimate(
            flops=4 * rows * width * units, bytes_accessed=8 * 1024 * 1024, transcendentals=0
        ),
        name="ffn",
    )(where, *blocks, bias, *weights)


def ffn_back_kernel(
    where_ref, d0_ref, d1_ref, d2_ref, d3_ref, act_ref, slope_ref, x_ref, up_own_ref, up_far_ref,
    down_ref, down_mine_ref, down_other_ref, part_ref, mine_ref, send_ref, hidden_sum_ref,
    out_sum_ref, d_ref, acc_ref, turned_ref, up_ref, w_ref,
):
    at = pl.program_id(0)
    lay_halves(where_ref[0], up_own_ref, up_far_ref, up_ref)
    lay_down(where_ref, down_ref, down_mine_ref, down_other_ref, at, w_ref)

    @pl.when(at == 0)
    def _():
        total = jnp.zeros(out_sum_ref.shape, F32)
        for i, block_ref in enumerate((d0_ref, d1_ref, d2_ref, d3_ref)):
            block = block_ref[...]
            d_ref[128 * i : 128 * (i + 1)] = block
            total += jnp.sum(block.astype(F32), axis=0, keepdims=True)
        out_sum_ref[...] = total
        turned_ref[...] = x_ref[...].T
        acc_ref[...] = jnp.zeros_like(acc_ref)

    d_out = d_ref[...]
    d_hidden = (slope_ref[...].astype(F32) * dot_t(d_out, w_ref[...])).astype(BF)
    hidden_sum_ref[...] = jnp.sum(d_hidden.astype(F32), axis=0, keepdims=True)
    acc_ref[...] += dot_t(d_hidden, up_ref[...])

    down = t_dot(act_ref[...], d_out).astype(BF)
    up = dot(turned_ref[...], d_hidden).astype(BF)
    cols = pl.ds(pl.multiple_of(at * 256, 256), 256)

    def store_down(to_ref):
        for x in range(4):
            to_ref[x, at // 2, :64] = down[64 * x : 64 * (x + 1)]

    def store_up(to_ref, core):
        for yh in range(2):
            for z in range(4):
                for x in range(4):
                    row = 512 * yh + 128 * z + 64 * core + 16 * x
                    to_ref[x, yh, 64 + 16 * z : 80 + 16 * z, cols] = up[row : row + 16]

    def store_all(core):
        store_up(mine_ref, core)
        store_up(send_ref, 1 - core)

    pl.when(at % 2 == where_ref[0])(lambda: store_down(mine_ref))
    pl.when(at % 2 != where_ref[0])(lambda: store_down(send_ref))
    pl.when(where_ref[0] == 0)(lambda: store_all(0))
    pl.when(where_ref[0] != 0)(lambda: store_all(1))

    @pl.when(at == pl.num_programs(0) - 1)
    def _():
        part_ref[...] = acc_ref[...].astype(BF)


def ffn_back(blocks, active, slope, normed, weights, where):
    rows, units = active.shape
    width = normed.shape[1]
    step = 256
    once = pl.Buffered(buffer_count=1)
    whole = pl.BlockSpec((rows, width), lambda j, where: (0, 0), pipeline_mode=once)
    part = pl.BlockSpec((rows, step), lambda j, where: (0, j))
    grads = (4, 2, 128, 1024)
    grad_spec = pl.BlockSpec(grads, lambda j, where: (0, 0, 0, 0), pipeline_mode=once)
    return pl.pallas_call(
        ffn_back_kernel,
        grid_spec=pltpu.PrefetchScalarGridSpec(
            num_scalar_prefetch=1,
            grid=(units // step,),
            in_specs=[
                pl.BlockSpec(blocks[0].shape, lambda j, where: (0, 0), pipeline_mode=once)
            ]
            * 4
            + [part, part, whole]
            + weight_specs(step, width),
            out_specs=[
                whole,
                grad_spec,
                grad_spec,
                pl.BlockSpec((1, step), lambda j, where: (0, j)),
                pl.BlockSpec((1, width), lambda j, where: (0, 0)),
            ],
            scratch_shapes=[
                pltpu.VMEM((rows, width), BF),
                pltpu.VMEM((rows, width), F32),
                pltpu.VMEM((width, rows), BF),
                pltpu.VMEM((width, step), BF),
                pltpu.VMEM((step, width), BF),
            ],
        ),
        out_shape=[
            jax.ShapeDtypeStruct((rows, width), BF),
            jax.ShapeDtypeStruct(grads, BF),
            jax.ShapeDtypeStruct(grads, BF),
            jax.ShapeDtypeStruct((1, units), F32),
            jax.ShapeDtypeStruct((1, width), F32),
        ],
        compiler_params=pltpu.CompilerParams(vmem_limit_bytes=20 * 1024 * 1024),
        cost_estimate=pl.CostEstimate(
            flops=8 * rows * width * units, bytes_accessed=12 * 1024 * 1024, transcendentals=0
        ),
        name="ffn_back",
    )(where, *blocks, active, slope, normed, *weights)


def grad_second_kernel(
    core_ref, tok_ref, tok_far_ref, here_ref, far_ref, ctx_ref, attn_ref, sums_ref, mine_ref,
    send_ref, vec_ref,
):
    at = pl.program_id(0)
    grads = t_dot(tok_ref[...], here_ref[...])
    grads_far = t_dot(tok_far_ref[...], far_ref[...])
    queries = grads[:, :256].astype(BF)
    others = (grads[:, 256:] + grads_far).astype(BF)
    attn = t_dot(ctx_ref[...], attn_ref[...]).astype(BF)

    def store(core, put):
        for x in range(4):
            for z in range(4):
                row = 64 * core + 16 * x
                rows = slice(128 * z + row, 128 * z + row + 16)
                put(x, z, slice(0, 256), queries[rows])
                put(x, z, slice(256, 768), others[rows])
                put(x, z, slice(768, 1024), attn[row : row + 16, 256 * z : 256 * z + 256])

    def put_mine(x, z, cols, value):
        mine_ref[x, 0, 16 * z : 16 * z + 16, cols] = value

    def put_send(x, z, cols, value):
        first = pl.multiple_of(128 * x + 64 * at + 16 * z, 16)
        send_ref[pl.ds(first, 16), cols] = value

    def store_all(core):
        store(core, put_mine)
        store(1 - core, put_send)

    pl.when(core_ref[0] == 0)(lambda: store_all(0))
    pl.when(core_ref[0] != 0)(lambda: store_all(1))

    @pl.when(pl.program_id(0) == 0)
    def _():
        here = jnp.sum(here_ref[...].astype(F32), axis=0, keepdims=True)
        far = jnp.sum(far_ref[...].astype(F32), axis=0, keepdims=True)
        bias = jnp.concatenate(
            [here[:, :256], here[:, 512:] + far[:, 256:], jnp.zeros((1, 512), F32)], axis=1
        )
        attn_sum = jnp.sum(attn_ref[...].astype(F32), axis=0, keepdims=True)
        row_of = lax.broadcasted_iota(jnp.int32, (16, 1), 0)
        total = jnp.where(row_of == 0, bias, sums_ref[...])
        low = jnp.where(row_of == 2, attn_sum, total).astype(BF)
        vec_ref[...] = low
        send_ref[512:] = low


def grad_second(tokens_own, tokens_far, d_here, d_far, context, d_attn, sums, core):
    rows, cols = tokens_own.shape
    half = cols // 2
    return pl.pallas_call(
        grad_second_kernel,
        grid_spec=pltpu.PrefetchScalarGridSpec(
            num_scalar_prefetch=1,
            grid=(2,),
            in_specs=[
                pl.BlockSpec((rows, half), lambda i, core: (0, i)),
                pl.BlockSpec((rows, half), lambda i, core: (0, i)),
                pl.BlockSpec(d_here.shape, lambda i, core: (0, 0)),
                pl.BlockSpec(d_far.shape, lambda i, core: (0, 0)),
                pl.BlockSpec((rows, context.shape[1] // 2), lambda i, core: (0, i)),
                pl.BlockSpec(d_attn.shape, lambda i, core: (0, 0)),
                pl.BlockSpec(sums.shape, lambda i, core: (0, 0)),
            ],
            out_specs=[
                pl.BlockSpec((4, 1, 64, 1024), lambda i, core: (0, i, 0, 0)),
                pl.BlockSpec((528, 1024), lambda i, core: (0, 0)),
                pl.BlockSpec(sums.shape, lambda i, core: (0, 0)),
            ],
        ),
        out_shape=[
            jax.ShapeDtypeStruct((4, 2, 64, 1024), BF),
            jax.ShapeDtypeStruct((528, 1024), BF),
            jax.ShapeDtypeStruct(sums.shape, BF),
        ],
        compiler_params=pltpu.CompilerParams(vmem_limit_bytes=16 * 1024 * 1024),
        cost_estimate=pl.CostEstimate(
            flops=3 * rows * cols * 1024, bytes_accessed=8 * 1024 * 1024, transcendentals=0
        ),
        name="grad_second",
    )(core.reshape(1), tokens_own, tokens_far, d_here, d_far, context, d_attn, sums)


def norm_stats(values):
    mean = jnp.mean(values, axis=-1, keepdims=True)
    centered = values - mean
    rstd = lax.rsqrt(jnp.mean(centered * centered, axis=-1, keepdims=True) + EPSILON)
    return centered * rstd, rstd


def norm_back(grad_out, gain, xhat, rstd):
    g = grad_out * gain
    return rstd * (
        g
        - jnp.mean(g, axis=-1, keepdims=True)
        - xhat * jnp.mean(g * xhat, axis=-1, keepdims=True)
    )


def unroll_ring(blocks, index):
    stacked = jnp.concatenate([b[None] for b in blocks + blocks], axis=0)
    return lax.dynamic_slice_in_dim(stacked, (4 - index) % 4, 4, axis=0)


def swap(value, axis, groups):
    return lax.all_to_all(value, axis, 0, 0, axis_index_groups=groups, tiled=True)


Z_RINGS = [[0, 1, 2, 3], [4, 5, 6, 7]]
X_RINGS = [[8 * yl + 2 * x + core for x in range(4)] for yl in range(2) for core in range(2)]


def with_rows(block, vectors):
    flat = block.reshape(-1, block.shape[-1])
    return flat if vectors is None else jnp.concatenate([flat, vectors], axis=0)


def core_sum(mine, vectors, got):
    rows = mine.size // mine.shape[-1]
    total = (mine.astype(F32) + got[:rows].reshape(mine.shape).astype(F32)).astype(BF)
    if vectors is None:
        return total, None
    return total, (vectors.astype(F32) + got[rows:].astype(F32)).astype(BF)


def x_send(pieces, x):
    return [pick(pieces, x)] + [x_shift(pick(pieces, (x + k) % 4), k) for k in (1, 2, 3)]


def x_flat(pieces, vectors):
    flat = pieces.reshape(4, -1, pieces.shape[-1])
    return jnp.concatenate([flat, jnp.broadcast_to(vectors, (4,) + vectors.shape)], axis=1)


def x_sum(got, rows):
    total = jnp.sum(got.astype(F32), axis=0).astype(BF)
    return total[: 2 * rows].reshape(2, rows, -1), total[2 * rows :]


def y_send(pieces, vectors, yh):
    own, other = pick(pieces, yh), pick(pieces, 1 - yh)
    got = [
        y_flip(with_rows(block, vectors), lo, hi)
        for block, lo, hi in ((own, 1, 0), (other, 0, 1), (other, 1, 1))
    ]
    return [with_rows(own, vectors)] + got


def ring_of(piece):
    return [piece] + [x_shift(piece, -k) for k in (1, 2, 3)]


def both_cores(blocks, *others):
    ring = jnp.stack(after(tuple(blocks), *others), axis=0)
    return ring, core_flip(ring)


def lay_first_kernel(where_ref, ring_ref, far_ref, down_ref, up_ref):
    def lay(src_ref):
        for k in range(4):
            x = (where_ref[2] + k) % 4
            down_ref[pl.ds(pl.multiple_of(64 * x, 64), 64)] = src_ref[k, :64].astype(F32)
            rows = pl.ds(pl.multiple_of(16 * x, 16), 16)
            for z in range(4):
                block = src_ref[k, 64 + 16 * z : 80 + 16 * z].astype(F32)
                up_ref[rows, 512 * z : 512 * (z + 1)] = block[:, :512]
                up_ref[rows, 2048 + 512 * z : 2048 + 512 * (z + 1)] = block[:, 512:]

    at = pl.program_id(0)
    pl.when(at == 0)(lambda: lay(ring_ref))
    pl.when(at == 1)(lambda: lay(far_ref))


def lay_second_kernel(where_ref, ring_ref, far_ref, qkv_ref, out_ref):
    def lay(src_ref):
        for k in range(4):
            rows = pl.ds(pl.multiple_of(16 * ((where_ref[2] + k) % 4), 16), 16)
            for z in range(4):
                block = src_ref[k, 16 * z : 16 * (z + 1)].astype(F32)
                for part in range(6):
                    at = 512 * part + 128 * z
                    qkv_ref[rows, at : at + 128] = block[:, 128 * part : 128 * (part + 1)]
                out_ref[rows, 256 * z : 256 * (z + 1)] = block[:, 768:]

    at = pl.program_id(0)
    pl.when(at == 0)(lambda: lay(ring_ref))
    pl.when(at == 1)(lambda: lay(far_ref))


def lay_pieces(kernel, ring, far, blocks, place, name):
    x, core = place[1], place[2]
    where = jnp.stack([core, 1 - core, x]).astype(jnp.int32)
    return pl.pallas_call(
        kernel,
        grid_spec=pltpu.PrefetchScalarGridSpec(
            num_scalar_prefetch=1,
            grid=(2,),
            in_specs=[
                pl.BlockSpec(ring.shape, lambda i, where: (0, 0, 0)),
                pl.BlockSpec(far.shape, lambda i, where: (0, 0, 0)),
            ],
            out_specs=[
                pl.BlockSpec((4 * rows, cols), lambda i, where: (where[i], 0))
                for rows, cols in blocks
            ],
        ),
        out_shape=[jax.ShapeDtypeStruct((8 * rows, cols), F32) for rows, cols in blocks],
        compiler_params=pltpu.CompilerParams(vmem_limit_bytes=16 * 1024 * 1024),
        name=name,
    )(where, ring, far)


def on_device(
    tokens,
    counts,
    w_qkv,
    bias_qv,
    w_out,
    bias_out,
    gain_attn,
    shift_attn,
    w_up,
    bias_up,
    w_down,
    bias_down,
    gain_ffn,
    shift_ffn,
    cotangent,
):
    row_count, model_width = tokens.shape
    replica = lax.axis_index("replica")
    group = lax.axis_index("fsdp")
    yl, x, core = replica // 8, (replica // 2) % 4, replica % 2
    yh, z = group // 4, group % 4
    place = (yl, x, core, yh, z)
    lanes = 128
    counts_row = counts[0]

    ring = (z + jnp.arange(4, dtype=jnp.int32)) % 4
    own_counts = jnp.take(counts_row, yh * 4 + ring)
    far_counts = jnp.take(counts_row, (1 - yh) * 4 + ring)
    slot = jnp.arange(row_count, dtype=jnp.int32)
    own_ok = (slot[None, :] < own_counts[:, None]).reshape(-1)
    far_ok = (slot[None, :] < far_counts[:, None]).reshape(-1)
    key_mask = jnp.where(jnp.concatenate([own_ok, far_ok]), 0.0, -1e30).astype(F32)[None, :]
    row_ok = own_ok.astype(F32)[:, None]

    sent = pack(w_qkv, (bias_qv,), core, lanes, "pack_qkv")
    small = (bias_out, gain_attn, shift_attn, bias_up, bias_down, gain_ffn, shift_ffn)
    up_sent = pack(w_up, small, core, 512, "pack_up")
    token_blocks = z_gather(tokens)
    out_far = y_flip(w_out, 0, 1)
    got = lax.all_to_all(sent, "fsdp", 0, 0, tiled=True)
    got_far = core_flip(got.reshape(640, 768)).reshape(8, 80, 768)
    bias_own = got[:, 64, :256].astype(F32).reshape(2, 2, 4, lanes)
    bias_own = pick(bias_own, z, 2).reshape(2, 2 * lanes)

    tokens_all = jnp.concatenate(token_blocks, axis=0)
    queries, kv_own, qkv_w = project(token_blocks, got, got_far, bias_own, core)
    kv_far = y_flip(kv_own, 0, 1)

    up_own = swap(after(up_sent, got), "fsdp", None)
    vec_all = up_own[:, 64:72].astype(F32)
    bout_all = vec_all[:, 0, :lanes].reshape(1, -1)
    ga_all = vec_all[:, 1, :lanes].reshape(1, -1)
    sa_all = vec_all[:, 2, :lanes].reshape(1, -1)
    bup_own = pick(vec_all[:, 3, :512].reshape(2, 4, 512), z, 1).reshape(1, -1)
    bdown_all = vec_all[:, 4, :lanes].reshape(1, -1)
    gf_all = vec_all[:, 5, :lanes].reshape(1, -1)
    sf_all = vec_all[:, 6, :lanes].reshape(1, -1)
    up_far = core_flip(after(up_own, kv_far).reshape(640, 1024)).reshape(8, 80, 1024)
    down_mine = y_flip(pick(after(w_down, kv_far).reshape(2, 256, 1024), core), 0, 1)
    where = jnp.stack([core, yh]).astype(jnp.int32)
    tokens_far = y_flip(after(tokens_all, down_mine), 0, 1)

    def order(own, far):
        return jnp.where(
            yh == 0, jnp.concatenate([own, far], axis=0), jnp.concatenate([far, own], axis=0)
        )

    out_w = order(w_out, out_far)
    context, probs, attn_part = attend(queries, kv_own, kv_far, key_mask, row_ok, out_w)
    resid1 = add_terms([tokens] + z_scatter(attn_part)) + bout_all
    xhat1, rstd1 = norm_stats(resid1)
    normed = xhat1 * ga_all + sa_all
    normed_blocks = z_gather(normed.astype(BF))
    down_other = core_flip(after(down_mine, normed_blocks[2]))
    weights = (up_own, up_far, w_down, down_mine, down_other)
    active, slope, ffn_part, normed_all = ffn(normed_blocks, bup_own, weights, where)
    resid2 = add_terms([normed] + z_scatter(ffn_part)) + bdown_all
    xhat2, rstd2 = norm_stats(resid2)
    layer_out = (xhat2 * gf_all + sf_all).astype(BF)

    cot = cotangent.astype(F32)
    d_resid2 = norm_back(cot, gf_all, xhat2, rstd2)

    dn_part, first, first_sent, hidden_sum, ffn_sum = ffn_back(
        z_gather(d_resid2.astype(BF)), active, slope, normed_all, weights, where
    )
    dn_terms = z_scatter(dn_part)
    first_got = core_flip(first_sent.reshape(1024, 1024))

    first_core, _ = core_sum(first, None, first_got)
    d_normed = after(add_terms([d_resid2] + dn_terms), first_core)
    d_resid1 = norm_back(d_normed, ga_all, xhat1, rstd1)
    dattn_blocks = z_gather(d_resid1.astype(BF))
    first_got = x_send(first_core, x)
    dattn_all = jnp.concatenate(dattn_blocks, axis=0)
    d_here, dkv_far = attend_back(
        queries, kv_own, kv_far, dattn_all, row_ok, out_w, probs
    )

    zero = jnp.zeros((1024,), F32)
    sums = pack_rows(
        [
            zero,
            hidden_sum[0],
            zero,
            ffn_sum[0],
            jnp.sum(d_normed * xhat1, axis=0),
            jnp.sum(d_normed, axis=0),
            jnp.sum(cot * xhat2, axis=0),
            jnp.sum(cot, axis=0),
        ],
        16,
        1024,
    )
    far_terms = y_flip(dkv_far, 0, 1)
    second, second_sent, vectors = grad_second(
        tokens_all, tokens_far, after(d_here, *first_got), dkv_far, context, dattn_all, sums, core
    )

    second_got = core_flip(second_sent)
    first_x = add_terms(after(tuple(first_got), second)).astype(BF)
    first_terms = y_send(first_x, None, yh)
    second_core, vec_core = core_sum(second, vectors, after(second_got, first_x))
    second_flat = x_flat(second_core, vec_core)
    second_got = swap(second_flat, "replica", X_RINGS)
    far_terms = after(far_terms, second_flat)

    dkv = (d_here[:, 256:].astype(F32) + far_terms.astype(F32)).astype(BF)
    d_projected = jnp.concatenate([d_here[:, :256], dkv], axis=1)

    first_terms = after(tuple(first_terms), second_flat)
    first_sum = add_terms(first_terms).astype(BF)
    second_x, vec_x = x_sum(after(second_got, first_sum), 64)
    second_terms = y_send(second_x, vec_x, yh)
    up_sum = swap(after(first_sum, second_x)[64:].reshape(4, 16, 1024), "fsdp", Z_RINGS)
    up_sum = up_sum.reshape(64, 1024)

    first_ring = ring_of(jnp.concatenate([first_sum[:64], up_sum], axis=0))
    second_all = add_terms(after(tuple(second_terms), up_sum)).astype(BF)
    second_sum, vec_sum = second_all[:64], second_all[64:]
    input_part = dot_t(after(d_projected, second_all), qkv_w).astype(BF)
    input_grad = add_terms([d_resid1] + z_scatter(input_part))
    bias_row = jnp.broadcast_to(vec_sum[None, 0:1, :512], (4, 1, 512))
    norm_row = pick(vec_sum[4:8].reshape(4, 2, 4, lanes), yh, 1).transpose(1, 0, 2)
    side = jnp.pad(
        jnp.concatenate([bias_row, norm_row.reshape(4, 1, 512)], axis=1),
        ((0, 0), (0, 14), (0, 256)),
    )
    swapped = swap(
        jnp.concatenate([second_sum[:, :768].reshape(4, 16, 768), side], axis=1), "fsdp", Z_RINGS
    )
    second_ring = ring_of(
        jnp.concatenate([swapped[:, :16].reshape(64, 768), second_sum[:, 768:]], axis=1)
    )
    ring, far = both_cores(first_ring, swapped)
    grad_w_down, grad_w_up = lay_pieces(
        lay_first_kernel, ring, far, ((64, 1024), (16, 4096)), place, "lay_first"
    )
    ring, far = both_cores(second_ring, grad_w_down)
    grad_w_qkv, grad_w_out = lay_pieces(
        lay_second_kernel, ring, far, ((16, 3072), (16, 1024)), place, "lay_second"
    )
    bqv_all = swapped[:, 16, :512].astype(F32).reshape(4, 2, 2, lanes).transpose(1, 2, 0, 3)
    grad_bqv = pick(bqv_all.reshape(8, 256), group)
    norms = jnp.sum(swapped[:, 17, :512].astype(F32), axis=0).reshape(4, lanes)
    grad_bup = pick(vec_sum[1].reshape(2, 512), yh).astype(F32)
    rest = pick(vec_sum[2:4].reshape(2, 8, lanes), group, 1).astype(F32)

    return (
        layer_out,
        input_grad,
        grad_w_qkv,
        grad_bqv,
        grad_w_out,
        rest[0],
        norms[0],
        norms[1],
        grad_w_up,
        grad_bup,
        grad_w_down,
        rest[1],
        norms[2],
        norms[3],
    )


def solution(mesh):
    in_specs = (
        P(("replica", "fsdp"), None),
        P("replica", None),
        P("fsdp", None),
        P("fsdp"),
        P("fsdp", None),
        P("fsdp"),
        P("fsdp"),
        P("fsdp"),
        P("fsdp", None),
        P("fsdp"),
        P("fsdp", None),
        P("fsdp"),
        P("fsdp"),
        P("fsdp"),
        P(("replica", "fsdp"), None),
    )
    out_specs = (
        P(("replica", "fsdp"), None),
        P(("replica", "fsdp"), None),
        P("fsdp", None),
        P("fsdp"),
        P("fsdp", None),
        P("fsdp"),
        P("fsdp"),
        P("fsdp"),
        P("fsdp", None),
        P("fsdp"),
        P("fsdp", None),
        P("fsdp"),
        P("fsdp"),
        P("fsdp"),
    )
    return jax.shard_map(
        on_device, mesh=mesh, in_specs=in_specs, out_specs=out_specs, check_vma=False
    )
```

```python
import functools

import jax
import jax.numpy as jnp
from jax import lax
from jax.experimental import pallas as pl
from jax.experimental.pallas import tpu as pltpu
from jax.sharding import PartitionSpec as P

HEAD_DIM = 64
EPSILON = 1e-05
BF = jnp.bfloat16
F32 = jnp.float32
BOTH = ("replica", "fsdp")


def all_pairs(move):
    pairs = []
    for yl in range(2):
        for x in range(4):
            for core in range(2):
                for yh in range(2):
                    for z in range(4):
                        a, b, c, d, e = move(yl, x, core, yh, z)
                        pairs.append(
                            (
                                ((yl * 4 + x) * 2 + core) * 8 + yh * 4 + z,
                                ((a * 4 + b) * 2 + c) * 8 + d * 4 + e,
                            )
                        )
    return pairs


def z_shift(value, k):
    return lax.ppermute(
        value, BOTH, all_pairs(lambda yl, x, c, yh, z: (yl, x, c, yh, (z + k) % 4))
    )


def x_shift(value, k):
    return lax.ppermute(
        value, BOTH, all_pairs(lambda yl, x, c, yh, z: (yl, (x + k) % 4, c, yh, z))
    )


def core_flip(value):
    return lax.ppermute(value, BOTH, all_pairs(lambda yl, x, c, yh, z: (yl, x, 1 - c, yh, z)))


def y_flip(value, lo, hi):
    return lax.ppermute(
        value, BOTH, all_pairs(lambda yl, x, c, yh, z: (yl ^ lo, x, c, yh ^ hi, z))
    )


def z_gather(value):
    return [value] + [z_shift(value, -k) for k in (1, 2, 3)]


def z_scatter(partial):
    rows = partial.shape[0] // 4
    terms = [partial[:rows]]
    for k in (1, 2, 3):
        terms.append(z_shift(partial[k * rows : (k + 1) * rows], k))
    return terms


def add_terms(terms):
    total = terms[0].astype(F32)
    for term in terms[1:]:
        total = total + term.astype(F32)
    return total


def dot(left, right):
    return jnp.dot(left, right, preferred_element_type=F32)


def dot_t(left, right):
    return lax.dot_general(left, right, (((1,), (1,)), ((), ())), preferred_element_type=F32)


def t_dot(left, right):
    return lax.dot_general(left, right, (((0,), (0,)), ((), ())), preferred_element_type=F32)


def after(value, *others):
    return lax.optimization_barrier((value,) + others)[0]


def pick(stacked, index, axis=0):
    return lax.dynamic_index_in_dim(stacked, index, axis, keepdims=False)


def pack_rows(vectors, rows, cols):
    total = jnp.zeros((rows, cols), vectors[0].dtype)
    for i, vec in enumerate(vectors):
        total = total + jnp.pad(
            vec.reshape(1, -1), ((i, rows - 1 - i), (0, cols - vec.shape[0]))
        )
    return total


def rows_of(v_refs, cols):
    row_of = lax.broadcasted_iota(jnp.int32, (16, 1), 0)
    total = jnp.zeros((16, cols), F32)
    for i, v_ref in enumerate(v_refs):
        vec = v_ref[...].astype(F32)
        wide = jnp.concatenate([vec, jnp.zeros((1, cols - vec.shape[1]), F32)], axis=1)
        total = jnp.where(row_of == i, wide, total)
    return total.astype(BF)


def pack_kernel(width, core_ref, w_ref, *refs):
    out_ref = refs[-1]
    parts = w_ref.shape[1] // (4 * width)
    rows = rows_of(refs[:-1], out_ref.shape[2])
    for f in range(8):
        for part in range(parts):
            at = width * (4 * part + f % 4)
            out_ref[f, :64, width * part : width * (part + 1)] = w_ref[:, at : at + width]
        out_ref[f, 64:] = rows


def pack(weight, vectors, core, width, name):
    cols = weight.shape[1]
    out = (8, 80, cols // 4)
    return pl.pallas_call(
        functools.partial(pack_kernel, width),
        grid_spec=pltpu.PrefetchScalarGridSpec(
            num_scalar_prefetch=1,
            grid=(1,),
            in_specs=[pl.BlockSpec((64, cols), lambda i, core: (core[0], 0))]
            + [pl.BlockSpec((1, v.shape[0]), lambda i, core: (0, 0)) for v in vectors],
            out_specs=pl.BlockSpec(out, lambda i, core: (0, 0, 0)),
        ),
        out_shape=jax.ShapeDtypeStruct(out, BF),
        compiler_params=pltpu.CompilerParams(vmem_limit_bytes=8 * 1024 * 1024),
        name=name,
    )(core.reshape(1), weight, *[v.reshape(1, -1) for v in vectors])


def project_kernel(
    core_ref, t0_ref, t1_ref, t2_ref, t3_ref, own_ref, far_ref, bias_ref, q_ref, kv_ref, w_ref
):
    lay_halves(core_ref[0], own_ref, far_ref, w_ref)
    weights = w_ref[...]
    width = q_ref.shape[1]
    for i, t_ref in enumerate((t0_ref, t1_ref, t2_ref, t3_ref)):
        rows = pl.ds(128 * i, 128)
        out = dot(t_ref[...], weights)
        queries = (out[:, :width] + bias_ref[0:1]).astype(BF).astype(F32)
        q_ref[rows] = (queries * HEAD_DIM**-0.5).astype(BF)
        kv_ref[rows, :width] = out[:, width : 2 * width].astype(BF)
        kv_ref[rows, width:] = (out[:, 2 * width :] + bias_ref[1:2]).astype(BF)


def project(token_blocks, own, far, bias, core):
    rows = 4 * token_blocks[0].shape[0]
    width = bias.shape[1]
    vmem = pl.BlockSpec(memory_space=pltpu.VMEM)
    return pl.pallas_call(
        project_kernel,
        in_specs=[pl.BlockSpec(memory_space=pltpu.SMEM)] + [vmem] * 7,
        out_specs=[vmem] * 3,
        out_shape=[
            jax.ShapeDtypeStruct((rows, width), BF),
            jax.ShapeDtypeStruct((rows, 2 * width), BF),
            jax.ShapeDtypeStruct((1024, 3 * width), BF),
        ],
        compiler_params=pltpu.CompilerParams(vmem_limit_bytes=12 * 1024 * 1024),
        cost_estimate=pl.CostEstimate(
            flops=6 * rows * 1024 * width, bytes_accessed=4 * 1024 * 1024, transcendentals=0
        ),
        name="project",
    )(core.reshape(1), *token_blocks, own, far, bias)


def attend_kernel(q_ref, own_ref, far_ref, mask_ref, ok_ref, w_ref, ctx_ref, p_ref, out_ref):
    queries = q_ref[...]
    width = queries.shape[1]
    half = own_ref.shape[0]
    head_of = lax.broadcasted_iota(jnp.int32, (1, width), 1) // HEAD_DIM
    context = jnp.zeros(queries.shape, F32)
    for h in range(width // HEAD_DIM):
        q_h = jnp.where(head_of == h, queries, jnp.zeros_like(queries))
        s_own = dot_t(q_h, own_ref[:, :width]) + mask_ref[:, :half]
        s_far = dot_t(q_h, far_ref[:, :width]) + mask_ref[:, half:]
        top = jnp.maximum(
            jnp.max(s_own, axis=1, keepdims=True), jnp.max(s_far, axis=1, keepdims=True)
        )
        e_own = jnp.exp(s_own - top)
        e_far = jnp.exp(s_far - top)
        scale = 1.0 / (
            jnp.sum(e_own, axis=1, keepdims=True) + jnp.sum(e_far, axis=1, keepdims=True)
        )
        p_own = (e_own * scale).astype(BF)
        p_far = (e_far * scale).astype(BF)
        p_ref[h, :, :half] = p_own
        p_ref[h, :, half:] = p_far
        out = dot(p_own, own_ref[:, width:]) + dot(p_far, far_ref[:, width:])
        context = jnp.where(head_of == h, out, context)
    low = (context * ok_ref[...]).astype(BF)
    ctx_ref[...] = low
    out_ref[...] = dot(low, w_ref[...]).astype(BF)


def attend(queries, kv_own, kv_far, key_mask, row_ok, out_w):
    rows, width = queries.shape
    heads = width // HEAD_DIM
    keys = 2 * kv_own.shape[0]
    step = 256
    return pl.pallas_call(
        attend_kernel,
        grid=(rows // step,),
        in_specs=[
            pl.BlockSpec((step, width), lambda i: (i, 0)),
            pl.BlockSpec(kv_own.shape, lambda i: (0, 0)),
            pl.BlockSpec(kv_far.shape, lambda i: (0, 0)),
            pl.BlockSpec((1, keys), lambda i: (0, 0)),
            pl.BlockSpec((step, 1), lambda i: (i, 0)),
            pl.BlockSpec(out_w.shape, lambda i: (0, 0)),
        ],
        out_specs=[
            pl.BlockSpec((step, width), lambda i: (i, 0)),
            pl.BlockSpec((heads, step, keys), lambda i: (0, i, 0)),
            pl.BlockSpec((step, out_w.shape[1]), lambda i: (i, 0)),
        ],
        out_shape=[
            jax.ShapeDtypeStruct((rows, width), BF),
            jax.ShapeDtypeStruct((heads, rows, keys), BF),
            jax.ShapeDtypeStruct((rows, out_w.shape[1]), BF),
        ],
        compiler_params=pltpu.CompilerParams(vmem_limit_bytes=16 * 1024 * 1024),
        cost_estimate=pl.CostEstimate(
            flops=16 * rows * keys * width, bytes_accessed=6 * 1024 * 1024, transcendentals=0
        ),
        name="attend",
    )(queries, kv_own, kv_far, key_mask, row_ok, out_w)


def attend_back_kernel(
    q_ref,
    own_ref,
    far_ref,
    grad_ref,
    ok_ref,
    w_ref,
    p_ref,
    here_ref,
    far_grad_ref,
    acc_own,
    acc_far,
):
    at = pl.program_id(0)
    queries = q_ref[...]
    grads = (dot_t(grad_ref[...], w_ref[...]) * ok_ref[...]).astype(BF)
    width = queries.shape[1]
    half = own_ref.shape[0]
    head_of = lax.broadcasted_iota(jnp.int32, (1, width), 1) // HEAD_DIM
    zero = jnp.zeros_like(queries)

    @pl.when(at == 0)
    def _():
        acc_own[...] = jnp.zeros_like(acc_own)
        acc_far[...] = jnp.zeros_like(acc_far)

    d_queries = jnp.zeros(queries.shape, F32)
    for h in range(width // HEAD_DIM):
        q_h = jnp.where(head_of == h, queries, zero)
        g_h = jnp.where(head_of == h, grads, zero)
        p_own_low = p_ref[h, :, :half]
        p_far_low = p_ref[h, :, half:]
        p_own = p_own_low.astype(F32)
        p_far = p_far_low.astype(F32)
        t_own = p_own * dot_t(g_h, own_ref[:, width:])
        t_far = p_far * dot_t(g_h, far_ref[:, width:])
        inner = jnp.sum(t_own, axis=1, keepdims=True) + jnp.sum(t_far, axis=1, keepdims=True)
        ds_own = (t_own - p_own * inner).astype(BF)
        ds_far = (t_far - p_far * inner).astype(BF)
        out = dot(ds_own, own_ref[:, :width]) + dot(ds_far, far_ref[:, :width])
        d_queries = jnp.where(head_of == h, out, d_queries)
        acc_own[:, :width] += t_dot(ds_own, q_h)
        acc_far[:, :width] += t_dot(ds_far, q_h)
        acc_own[:, width:] += t_dot(p_own_low, g_h)
        acc_far[:, width:] += t_dot(p_far_low, g_h)
    rows = pl.ds(pl.multiple_of(at * queries.shape[0], queries.shape[0]), queries.shape[0])
    here_ref[rows, :width] = (d_queries * HEAD_DIM**-0.5).astype(BF)

    @pl.when(at == pl.num_programs(0) - 1)
    def _():
        here_ref[:, width:] = acc_own[...].astype(BF)
        far_grad_ref[...] = acc_far[...].astype(BF)


def attend_back(queries, kv_own, kv_far, d_attn, row_ok, out_w, probs):
    rows, width = queries.shape
    heads, _, keys = probs.shape
    step = 256
    return pl.pallas_call(
        attend_back_kernel,
        grid=(rows // step,),
        in_specs=[
            pl.BlockSpec((step, width), lambda i: (i, 0)),
            pl.BlockSpec(kv_own.shape, lambda i: (0, 0)),
            pl.BlockSpec(kv_far.shape, lambda i: (0, 0)),
            pl.BlockSpec((step, d_attn.shape[1]), lambda i: (i, 0)),
            pl.BlockSpec((step, 1), lambda i: (i, 0)),
            pl.BlockSpec(out_w.shape, lambda i: (0, 0)),
            pl.BlockSpec((heads, step, keys), lambda i: (0, i, 0)),
        ],
        out_specs=[
            pl.BlockSpec((rows, 3 * width), lambda i: (0, 0)),
            pl.BlockSpec(kv_own.shape, lambda i: (0, 0)),
        ],
        out_shape=[
            jax.ShapeDtypeStruct((rows, 3 * width), BF),
            jax.ShapeDtypeStruct(kv_own.shape, BF),
        ],
        scratch_shapes=[pltpu.VMEM(kv_own.shape, F32), pltpu.VMEM(kv_own.shape, F32)],
        compiler_params=pltpu.CompilerParams(vmem_limit_bytes=20 * 1024 * 1024),
        cost_estimate=pl.CostEstimate(
            flops=40 * rows * keys * width, bytes_accessed=8 * 1024 * 1024, transcendentals=0
        ),
        name="attend_back",
    )(queries, kv_own, kv_far, d_attn, row_ok, out_w, probs)


def lay_halves(core, own_ref, far_ref, to_ref):
    def lay(low_ref, high_ref):
        for f in range(8):
            to_ref[128 * f : 128 * f + 64] = low_ref[f, :64]
            to_ref[128 * f + 64 : 128 * f + 128] = high_ref[f, :64]

    pl.when(core == 0)(lambda: lay(own_ref, far_ref))
    pl.when(core != 0)(lambda: lay(far_ref, own_ref))


def lay_down(where_ref, own_ref, mine_ref, other_ref, to_ref):
    def lay(y_hi, core):
        far = 512 * (1 - y_hi)
        to_ref[512 * y_hi : 512 * (y_hi + 1)] = own_ref[...]
        to_ref[far + 256 * core : far + 256 * (core + 1)] = mine_ref[...]
        to_ref[far + 256 * (1 - core) : far + 256 * (2 - core)] = other_ref[...]

    for y_hi in range(2):
        for core in range(2):
            here = (where_ref[0] == core) & (where_ref[1] == y_hi)
            pl.when(here)(functools.partial(lay, y_hi, core))


STEP = 256


def ffn_kernel(
    where_ref, x0_ref, x1_ref, x2_ref, x3_ref, bias_ref, up_own_ref, up_far_ref, down_ref,
    down_mine_ref, down_other_ref, act_ref, slope_ref, part_ref, x_ref, up_ref, w_ref,
):
    lay_halves(where_ref[0], up_own_ref, up_far_ref, up_ref)
    lay_down(where_ref, down_ref, down_mine_ref, down_other_ref, w_ref)
    for i, block_ref in enumerate((x0_ref, x1_ref, x2_ref, x3_ref)):
        rows = slice(128 * i, 128 * (i + 1))
        x_ref[rows] = block_ref[...]
    for i in range(2):
        rows = slice(256 * i, 256 * (i + 1))
        total = jnp.zeros((256, part_ref.shape[1]), F32)
        for at in range(0, act_ref.shape[1], STEP):
            cols = slice(at, at + STEP)
            hidden = dot(x_ref[rows], up_ref[:, cols]) + bias_ref[:, cols]
            cdf = 0.5 * (1.0 + lax.erf(hidden * 0.7071067811865476))
            active = (hidden * cdf).astype(BF)
            act_ref[rows, cols] = active
            slope = cdf + hidden * (0.3989422804014327 * jnp.exp(-0.5 * hidden * hidden))
            slope_ref[rows, cols] = slope.astype(BF)
            total += dot(active, w_ref[cols])
        part_ref[rows] = total.astype(BF)


def ffn(blocks, bias, weights, where):
    rows, width, units = 4 * blocks[0].shape[0], 1024, 1024
    vmem = pl.BlockSpec(memory_space=pltpu.VMEM)
    return pl.pallas_call(
        ffn_kernel,
        in_specs=[pl.BlockSpec(memory_space=pltpu.SMEM)] + [vmem] * 10,
        out_specs=[vmem] * 4,
        out_shape=[
            jax.ShapeDtypeStruct((rows, units), BF),
            jax.ShapeDtypeStruct((rows, units), BF),
            jax.ShapeDtypeStruct((rows, width), BF),
            jax.ShapeDtypeStruct((rows, width), BF),
        ],
        scratch_shapes=[pltpu.VMEM((width, units), BF), pltpu.VMEM((units, width), BF)],
        compiler_params=pltpu.CompilerParams(vmem_limit_bytes=24 * 1024 * 1024),
        cost_estimate=pl.CostEstimate(
            flops=4 * rows * width * units, bytes_accessed=8 * 1024 * 1024, transcendentals=0
        ),
        name="ffn",
    )(where, *blocks, bias, *weights)


def ffn_back_kernel(
    where_ref, d0_ref, d1_ref, d2_ref, d3_ref, act_ref, slope_ref, x_ref, up_own_ref, up_far_ref,
    down_ref, down_mine_ref, down_other_ref, part_ref, mine_ref, send_ref, hidden_sum_ref,
    out_sum_ref, d_ref, acc_ref, turned_ref, up_ref, w_ref,
):
    lay_halves(where_ref[0], up_own_ref, up_far_ref, up_ref)
    lay_down(where_ref, down_ref, down_mine_ref, down_other_ref, w_ref)
    total = jnp.zeros(out_sum_ref.shape, F32)
    for i, block_ref in enumerate((d0_ref, d1_ref, d2_ref, d3_ref)):
        block = block_ref[...]
        d_ref[128 * i : 128 * (i + 1)] = block
        total += jnp.sum(block.astype(F32), axis=0, keepdims=True)
    out_sum_ref[...] = total
    turned_ref[...] = x_ref[...].T
    own_core = where_ref[0]

    for at in range(4):
        cols = slice(STEP * at, STEP * (at + 1))
        d_hidden = slope_ref[:, cols].astype(F32) * dot_t(d_ref[...], w_ref[cols])
        d_hidden = d_hidden.astype(BF)
        hidden_sum_ref[:, cols] = jnp.sum(d_hidden.astype(F32), axis=0, keepdims=True)
        d_normed = dot_t(d_hidden, up_ref[:, cols])
        if at == 0:
            acc_ref[...] = d_normed
        elif at < 3:
            acc_ref[...] += d_normed
        else:
            part_ref[...] = (acc_ref[...] + d_normed).astype(BF)

        down = t_dot(act_ref[:, cols], d_ref[...]).astype(BF)
        up = dot(turned_ref[...], d_hidden).astype(BF)

        def store(to_ref, core, at=at, cols=cols, down=down, up=up):
            for x in range(4):
                if at % 2 == core:
                    to_ref[x, at // 2, :64] = down[64 * x : 64 * (x + 1)]
                for yh in range(2):
                    for z in range(4):
                        row = 512 * yh + 128 * z + 64 * core + 16 * x
                        to_ref[x, yh, 64 + 16 * z : 80 + 16 * z, cols] = up[row : row + 16]

        def store_all(core, store=store):
            store(mine_ref, core)
            store(send_ref, 1 - core)

        pl.when(own_core == 0)(functools.partial(store_all, 0))
        pl.when(own_core != 0)(functools.partial(store_all, 1))


def ffn_back(blocks, active, slope, normed, weights, where):
    rows, units = active.shape
    width = normed.shape[1]
    vmem = pl.BlockSpec(memory_space=pltpu.VMEM)
    grads = (4, 2, 128, 1024)
    return pl.pallas_call(
        ffn_back_kernel,
        in_specs=[pl.BlockSpec(memory_space=pltpu.SMEM)] + [vmem] * 12,
        out_specs=[vmem] * 5,
        out_shape=[
            jax.ShapeDtypeStruct((rows, width), BF),
            jax.ShapeDtypeStruct(grads, BF),
            jax.ShapeDtypeStruct(grads, BF),
            jax.ShapeDtypeStruct((1, units), F32),
            jax.ShapeDtypeStruct((1, width), F32),
        ],
        scratch_shapes=[
            pltpu.VMEM((rows, width), BF),
            pltpu.VMEM((rows, width), F32),
            pltpu.VMEM((width, rows), BF),
            pltpu.VMEM((width, units), BF),
            pltpu.VMEM((units, width), BF),
        ],
        compiler_params=pltpu.CompilerParams(vmem_limit_bytes=32 * 1024 * 1024),
        cost_estimate=pl.CostEstimate(
            flops=8 * rows * width * units, bytes_accessed=12 * 1024 * 1024, transcendentals=0
        ),
        name="ffn_back",
    )(where, *blocks, active, slope, normed, *weights)


def grad_second_kernel(
    core_ref, tok_ref, tok_far_ref, here_ref, far_ref, ctx_ref, attn_ref, sums_ref, mine_ref,
    send_ref, vec_ref,
):
    at = pl.program_id(0)
    grads = t_dot(tok_ref[...], here_ref[...])
    grads_far = t_dot(tok_far_ref[...], far_ref[...])
    queries = grads[:, :256].astype(BF)
    others = (grads[:, 256:] + grads_far).astype(BF)
    attn = t_dot(ctx_ref[...], attn_ref[...]).astype(BF)

    def store(core, put):
        for x in range(4):
            for z in range(4):
                row = 64 * core + 16 * x
                rows = slice(128 * z + row, 128 * z + row + 16)
                put(x, z, slice(0, 256), queries[rows])
                put(x, z, slice(256, 768), others[rows])
                put(x, z, slice(768, 1024), attn[row : row + 16, 256 * z : 256 * z + 256])

    def put_mine(x, z, cols, value):
        mine_ref[x, 0, 16 * z : 16 * z + 16, cols] = value

    def put_send(x, z, cols, value):
        first = pl.multiple_of(128 * x + 64 * at + 16 * z, 16)
        send_ref[pl.ds(first, 16), cols] = value

    def store_all(core):
        store(core, put_mine)
        store(1 - core, put_send)

    pl.when(core_ref[0] == 0)(lambda: store_all(0))
    pl.when(core_ref[0] != 0)(lambda: store_all(1))

    @pl.when(pl.program_id(0) == 0)
    def _():
        here = jnp.sum(here_ref[...].astype(F32), axis=0, keepdims=True)
        far = jnp.sum(far_ref[...].astype(F32), axis=0, keepdims=True)
        bias = jnp.concatenate(
            [here[:, :256], here[:, 512:] + far[:, 256:], jnp.zeros((1, 512), F32)], axis=1
        )
        attn_sum = jnp.sum(attn_ref[...].astype(F32), axis=0, keepdims=True)
        row_of = lax.broadcasted_iota(jnp.int32, (16, 1), 0)
        total = jnp.where(row_of == 0, bias, sums_ref[...])
        low = jnp.where(row_of == 2, attn_sum, total).astype(BF)
        vec_ref[...] = low
        send_ref[512:] = low


def grad_second(tokens_own, tokens_far, d_here, d_far, context, d_attn, sums, core):
    rows, cols = tokens_own.shape
    half = cols // 2
    return pl.pallas_call(
        grad_second_kernel,
        grid_spec=pltpu.PrefetchScalarGridSpec(
            num_scalar_prefetch=1,
            grid=(2,),
            in_specs=[
                pl.BlockSpec((rows, half), lambda i, core: (0, i)),
                pl.BlockSpec((rows, half), lambda i, core: (0, i)),
                pl.BlockSpec(d_here.shape, lambda i, core: (0, 0)),
                pl.BlockSpec(d_far.shape, lambda i, core: (0, 0)),
                pl.BlockSpec((rows, context.shape[1] // 2), lambda i, core: (0, i)),
                pl.BlockSpec(d_attn.shape, lambda i, core: (0, 0)),
                pl.BlockSpec(sums.shape, lambda i, core: (0, 0)),
            ],
            out_specs=[
                pl.BlockSpec((4, 1, 64, 1024), lambda i, core: (0, i, 0, 0)),
                pl.BlockSpec((528, 1024), lambda i, core: (0, 0)),
                pl.BlockSpec(sums.shape, lambda i, core: (0, 0)),
            ],
        ),
        out_shape=[
            jax.ShapeDtypeStruct((4, 2, 64, 1024), BF),
            jax.ShapeDtypeStruct((528, 1024), BF),
            jax.ShapeDtypeStruct(sums.shape, BF),
        ],
        compiler_params=pltpu.CompilerParams(vmem_limit_bytes=16 * 1024 * 1024),
        cost_estimate=pl.CostEstimate(
            flops=3 * rows * cols * 1024, bytes_accessed=8 * 1024 * 1024, transcendentals=0
        ),
        name="grad_second",
    )(core.reshape(1), tokens_own, tokens_far, d_here, d_far, context, d_attn, sums)


def norm_stats(values):
    mean = jnp.mean(values, axis=-1, keepdims=True)
    centered = values - mean
    rstd = lax.rsqrt(jnp.mean(centered * centered, axis=-1, keepdims=True) + EPSILON)
    return centered * rstd, rstd


def norm_back(grad_out, gain, xhat, rstd):
    g = grad_out * gain
    return rstd * (
        g
        - jnp.mean(g, axis=-1, keepdims=True)
        - xhat * jnp.mean(g * xhat, axis=-1, keepdims=True)
    )


def unroll_ring(blocks, index):
    stacked = jnp.concatenate([b[None] for b in blocks + blocks], axis=0)
    return lax.dynamic_slice_in_dim(stacked, (4 - index) % 4, 4, axis=0)


def swap(value, axis, groups):
    return lax.all_to_all(value, axis, 0, 0, axis_index_groups=groups, tiled=True)


Z_RINGS = [[0, 1, 2, 3], [4, 5, 6, 7]]
X_RINGS = [[8 * yl + 2 * x + core for x in range(4)] for yl in range(2) for core in range(2)]


def with_rows(block, vectors):
    flat = block.reshape(-1, block.shape[-1])
    return flat if vectors is None else jnp.concatenate([flat, vectors], axis=0)


def core_sum(mine, vectors, got):
    rows = mine.size // mine.shape[-1]
    total = (mine.astype(F32) + got[:rows].reshape(mine.shape).astype(F32)).astype(BF)
    if vectors is None:
        return total, None
    return total, (vectors.astype(F32) + got[rows:].astype(F32)).astype(BF)


def x_send(pieces, x):
    return [pick(pieces, x)] + [x_shift(pick(pieces, (x + k) % 4), k) for k in (1, 2, 3)]


def x_flat(pieces, vectors):
    flat = pieces.reshape(4, -1, pieces.shape[-1])
    return jnp.concatenate([flat, jnp.broadcast_to(vectors, (4,) + vectors.shape)], axis=1)


def x_sum(got, rows):
    total = jnp.sum(got.astype(F32), axis=0).astype(BF)
    return total[: 2 * rows].reshape(2, rows, -1), total[2 * rows :]


def y_send(pieces, vectors, yh):
    own, other = pick(pieces, yh), pick(pieces, 1 - yh)
    got = [
        y_flip(with_rows(block, vectors), lo, hi)
        for block, lo, hi in ((own, 1, 0), (other, 0, 1), (other, 1, 1))
    ]
    return [with_rows(own, vectors)] + got


def ring_of(piece):
    return [piece] + [x_shift(piece, -k) for k in (1, 2, 3)]


def both_cores(blocks, *others):
    ring = jnp.stack(after(tuple(blocks), *others), axis=0)
    return ring, core_flip(ring)


def lay_first_kernel(where_ref, ring_ref, far_ref, down_ref, up_ref):
    def lay(src_ref):
        for k in range(4):
            x = (where_ref[2] + k) % 4
            down_ref[pl.ds(pl.multiple_of(64 * x, 64), 64)] = src_ref[k, :64].astype(F32)
            rows = pl.ds(pl.multiple_of(16 * x, 16), 16)
            for z in range(4):
                block = src_ref[k, 64 + 16 * z : 80 + 16 * z].astype(F32)
                up_ref[rows, 512 * z : 512 * (z + 1)] = block[:, :512]
                up_ref[rows, 2048 + 512 * z : 2048 + 512 * (z + 1)] = block[:, 512:]

    at = pl.program_id(0)
    pl.when(at == 0)(lambda: lay(ring_ref))
    pl.when(at == 1)(lambda: lay(far_ref))


def lay_second_kernel(where_ref, ring_ref, far_ref, qkv_ref, out_ref):
    def lay(src_ref):
        for k in range(4):
            rows = pl.ds(pl.multiple_of(16 * ((where_ref[2] + k) % 4), 16), 16)
            for z in range(4):
                block = src_ref[k, 16 * z : 16 * (z + 1)].astype(F32)
                for part in range(6):
                    at = 512 * part + 128 * z
                    qkv_ref[rows, at : at + 128] = block[:, 128 * part : 128 * (part + 1)]
                out_ref[rows, 256 * z : 256 * (z + 1)] = block[:, 768:]

    at = pl.program_id(0)
    pl.when(at == 0)(lambda: lay(ring_ref))
    pl.when(at == 1)(lambda: lay(far_ref))


def lay_pieces(kernel, ring, far, blocks, place, name):
    x, core = place[1], place[2]
    where = jnp.stack([core, 1 - core, x]).astype(jnp.int32)
    return pl.pallas_call(
        kernel,
        grid_spec=pltpu.PrefetchScalarGridSpec(
            num_scalar_prefetch=1,
            grid=(2,),
            in_specs=[
                pl.BlockSpec(ring.shape, lambda i, where: (0, 0, 0)),
                pl.BlockSpec(far.shape, lambda i, where: (0, 0, 0)),
            ],
            out_specs=[
                pl.BlockSpec((4 * rows, cols), lambda i, where: (where[i], 0))
                for rows, cols in blocks
            ],
        ),
        out_shape=[jax.ShapeDtypeStruct((8 * rows, cols), F32) for rows, cols in blocks],
        compiler_params=pltpu.CompilerParams(vmem_limit_bytes=16 * 1024 * 1024),
        name=name,
    )(where, ring, far)


def on_device(
    tokens,
    counts,
    w_qkv,
    bias_qv,
    w_out,
    bias_out,
    gain_attn,
    shift_attn,
    w_up,
    bias_up,
    w_down,
    bias_down,
    gain_ffn,
    shift_ffn,
    cotangent,
):
    row_count, model_width = tokens.shape
    replica = lax.axis_index("replica")
    group = lax.axis_index("fsdp")
    yl, x, core = replica // 8, (replica // 2) % 4, replica % 2
    yh, z = group // 4, group % 4
    place = (yl, x, core, yh, z)
    lanes = 128
    counts_row = counts[0]

    ring = (z + jnp.arange(4, dtype=jnp.int32)) % 4
    own_counts = jnp.take(counts_row, yh * 4 + ring)
    far_counts = jnp.take(counts_row, (1 - yh) * 4 + ring)
    slot = jnp.arange(row_count, dtype=jnp.int32)
    own_ok = (slot[None, :] < own_counts[:, None]).reshape(-1)
    far_ok = (slot[None, :] < far_counts[:, None]).reshape(-1)
    key_mask = jnp.where(jnp.concatenate([own_ok, far_ok]), 0.0, -1e30).astype(F32)[None, :]
    row_ok = own_ok.astype(F32)[:, None]

    sent = pack(w_qkv, (bias_qv,), core, lanes, "pack_qkv")
    small = (bias_out, gain_attn, shift_attn, bias_up, bias_down, gain_ffn, shift_ffn)
    up_sent = pack(w_up, small, core, 512, "pack_up")
    token_blocks = z_gather(tokens)
    out_far = y_flip(w_out, 0, 1)
    got = lax.all_to_all(sent, "fsdp", 0, 0, tiled=True)
    got_far = core_flip(got.reshape(640, 768)).reshape(8, 80, 768)
    bias_own = got[:, 64, :256].astype(F32).reshape(2, 2, 4, lanes)
    bias_own = pick(bias_own, z, 2).reshape(2, 2 * lanes)

    tokens_all = jnp.concatenate(token_blocks, axis=0)
    queries, kv_own, qkv_w = project(token_blocks, got, got_far, bias_own, core)
    kv_far = y_flip(kv_own, 0, 1)

    up_own = swap(after(up_sent, got), "fsdp", None)
    vec_all = up_own[:, 64:72].astype(F32)
    bout_all = vec_all[:, 0, :lanes].reshape(1, -1)
    ga_all = vec_all[:, 1, :lanes].reshape(1, -1)
    sa_all = vec_all[:, 2, :lanes].reshape(1, -1)
    bup_own = pick(vec_all[:, 3, :512].reshape(2, 4, 512), z, 1).reshape(1, -1)
    bdown_all = vec_all[:, 4, :lanes].reshape(1, -1)
    gf_all = vec_all[:, 5, :lanes].reshape(1, -1)
    sf_all = vec_all[:, 6, :lanes].reshape(1, -1)
    up_far = core_flip(after(up_own, kv_far).reshape(640, 1024)).reshape(8, 80, 1024)
    down_mine = y_flip(pick(after(w_down, kv_far).reshape(2, 256, 1024), core), 0, 1)
    where = jnp.stack([core, yh]).astype(jnp.int32)

    def order(own, far):
        return jnp.where(
            yh == 0, jnp.concatenate([own, far], axis=0), jnp.concatenate([far, own], axis=0)
        )

    out_w = order(w_out, out_far)
    context, probs, attn_part = attend(queries, kv_own, kv_far, key_mask, row_ok, out_w)
    resid1 = add_terms([tokens] + z_scatter(attn_part)) + bout_all
    xhat1, rstd1 = norm_stats(resid1)
    normed = xhat1 * ga_all + sa_all
    normed_blocks = z_gather(normed.astype(BF))
    down_other = core_flip(after(down_mine, normed_blocks[2]))
    weights = (up_own, up_far, w_down, down_mine, down_other)
    active, slope, ffn_part, normed_all = ffn(normed_blocks, bup_own, weights, where)
    tokens_far = y_flip(after(tokens_all, ffn_part), 0, 1)
    resid2 = add_terms([normed] + z_scatter(ffn_part)) + bdown_all
    xhat2, rstd2 = norm_stats(resid2)
    layer_out = (xhat2 * gf_all + sf_all).astype(BF)

    cot = cotangent.astype(F32)
    d_resid2 = norm_back(cot, gf_all, xhat2, rstd2)

    dn_part, first, first_sent, hidden_sum, ffn_sum = ffn_back(
        z_gather(d_resid2.astype(BF)), active, slope, normed_all, weights, where
    )
    dn_terms = z_scatter(dn_part)
    first_got = core_flip(first_sent.reshape(1024, 1024))

    first_core, _ = core_sum(first, None, first_got)
    d_normed = after(add_terms([d_resid2] + dn_terms), first_core)
    d_resid1 = norm_back(d_normed, ga_all, xhat1, rstd1)
    dattn_blocks = z_gather(d_resid1.astype(BF))
    first_got = x_send(first_core, x)
    dattn_all = jnp.concatenate(dattn_blocks, axis=0)
    d_here, dkv_far = attend_back(
        queries, kv_own, kv_far, dattn_all, row_ok, out_w, probs
    )

    zero = jnp.zeros((1024,), F32)
    sums = pack_rows(
        [
            zero,
            hidden_sum[0],
            zero,
            ffn_sum[0],
            jnp.sum(d_normed * xhat1, axis=0),
            jnp.sum(d_normed, axis=0),
            jnp.sum(cot * xhat2, axis=0),
            jnp.sum(cot, axis=0),
        ],
        16,
        1024,
    )
    far_terms = y_flip(dkv_far, 0, 1)
    second, second_sent, vectors = grad_second(
        tokens_all, tokens_far, after(d_here, *first_got), dkv_far, context, dattn_all, sums, core
    )

    second_got = core_flip(second_sent)
    first_x = add_terms(after(tuple(first_got), second)).astype(BF)
    first_terms = y_send(first_x, None, yh)
    second_core, vec_core = core_sum(second, vectors, after(second_got, first_x))
    second_flat = x_flat(second_core, vec_core)
    second_got = swap(second_flat, "replica", X_RINGS)

    far_terms = after(far_terms, second_flat)
    dkv = (d_here[:, 256:].astype(F32) + far_terms.astype(F32)).astype(BF)
    d_projected = jnp.concatenate([d_here[:, :256], dkv], axis=1)

    second_x, vec_x = x_sum(after(second_got, far_terms), 64)
    second_terms = y_send(second_x, vec_x, yh)
    first_sum = add_terms(after(tuple(first_terms), second_x)).astype(BF)
    up_sum = swap(after(first_sum, second_x)[64:].reshape(4, 16, 1024), "fsdp", Z_RINGS)
    up_sum = up_sum.reshape(64, 1024)

    first_ring = ring_of(jnp.concatenate([first_sum[:64], up_sum], axis=0))
    second_all = add_terms(after(tuple(second_terms), up_sum)).astype(BF)
    second_sum, vec_sum = second_all[:64], second_all[64:]
    input_part = dot_t(after(d_projected, up_sum), qkv_w).astype(BF)
    input_grad = add_terms([d_resid1] + z_scatter(input_part))
    bias_row = jnp.broadcast_to(vec_sum[None, 0:1, :512], (4, 1, 512))
    norm_row = pick(vec_sum[4:8].reshape(4, 2, 4, lanes), yh, 1).transpose(1, 0, 2)
    side = jnp.pad(
        jnp.concatenate([bias_row, norm_row.reshape(4, 1, 512)], axis=1),
        ((0, 0), (0, 14), (0, 256)),
    )
    swapped = swap(
        jnp.concatenate([second_sum[:, :768].reshape(4, 16, 768), side], axis=1), "fsdp", Z_RINGS
    )
    second_ring = ring_of(
        jnp.concatenate([swapped[:, :16].reshape(64, 768), second_sum[:, 768:]], axis=1)
    )
    ring, far = both_cores(first_ring, swapped)
    grad_w_down, grad_w_up = lay_pieces(
        lay_first_kernel, ring, far, ((64, 1024), (16, 4096)), place, "lay_first"
    )
    ring, far = both_cores(second_ring, grad_w_down)
    grad_w_qkv, grad_w_out = lay_pieces(
        lay_second_kernel, ring, far, ((16, 3072), (16, 1024)), place, "lay_second"
    )
    bqv_all = swapped[:, 16, :512].astype(F32).reshape(4, 2, 2, lanes).transpose(1, 2, 0, 3)
    grad_bqv = pick(bqv_all.reshape(8, 256), group)
    norms = jnp.sum(swapped[:, 17, :512].astype(F32), axis=0).reshape(4, lanes)
    grad_bup = pick(vec_sum[1].reshape(2, 512), yh).astype(F32)
    rest = pick(vec_sum[2:4].reshape(2, 8, lanes), group, 1).astype(F32)

    return (
        layer_out,
        input_grad,
        grad_w_qkv,
        grad_bqv,
        grad_w_out,
        rest[0],
        norms[0],
        norms[1],
        grad_w_up,
        grad_bup,
        grad_w_down,
        rest[1],
        norms[2],
        norms[3],
    )


def solution(mesh):
    in_specs = (
        P(("replica", "fsdp"), None),
        P("replica", None),
        P("fsdp", None),
        P("fsdp"),
        P("fsdp", None),
        P("fsdp"),
        P("fsdp"),
        P("fsdp"),
        P("fsdp", None),
        P("fsdp"),
        P("fsdp", None),
        P("fsdp"),
        P("fsdp"),
        P("fsdp"),
        P(("replica", "fsdp"), None),
    )
    out_specs = (
        P(("replica", "fsdp"), None),
        P(("replica", "fsdp"), None),
        P("fsdp", None),
        P("fsdp"),
        P("fsdp", None),
        P("fsdp"),
        P("fsdp"),
        P("fsdp"),
        P("fsdp", None),
        P("fsdp"),
        P("fsdp", None),
        P("fsdp"),
        P("fsdp"),
        P("fsdp"),
    )
    return jax.shard_map(
        on_device, mesh=mesh, in_specs=in_specs, out_specs=out_specs, check_vma=False
    )
```

```python
import functools

import jax
import jax.numpy as jnp
from jax import lax
from jax.experimental import pallas as pl
from jax.experimental.pallas import tpu as pltpu
from jax.sharding import PartitionSpec as P

HEAD_DIM = 64
EPSILON = 1e-05
BF = jnp.bfloat16
F32 = jnp.float32
BOTH = ("replica", "fsdp")


def all_pairs(move):
    pairs = []
    for yl in range(2):
        for x in range(4):
            for core in range(2):
                for yh in range(2):
                    for z in range(4):
                        a, b, c, d, e = move(yl, x, core, yh, z)
                        pairs.append(
                            (
                                ((yl * 4 + x) * 2 + core) * 8 + yh * 4 + z,
                                ((a * 4 + b) * 2 + c) * 8 + d * 4 + e,
                            )
                        )
    return pairs


def z_shift(value, k):
    return lax.ppermute(
        value, BOTH, all_pairs(lambda yl, x, c, yh, z: (yl, x, c, yh, (z + k) % 4))
    )


def x_shift(value, k):
    return lax.ppermute(
        value, BOTH, all_pairs(lambda yl, x, c, yh, z: (yl, (x + k) % 4, c, yh, z))
    )


def core_flip(value):
    return lax.ppermute(value, BOTH, all_pairs(lambda yl, x, c, yh, z: (yl, x, 1 - c, yh, z)))


def y_flip(value, lo, hi):
    return lax.ppermute(
        value, BOTH, all_pairs(lambda yl, x, c, yh, z: (yl ^ lo, x, c, yh ^ hi, z))
    )


def z_gather(value):
    return [value] + [z_shift(value, -k) for k in (1, 2, 3)]


def z_scatter(partial):
    rows = partial.shape[0] // 4
    terms = [partial[:rows]]
    for k in (1, 2, 3):
        terms.append(z_shift(partial[k * rows : (k + 1) * rows], k))
    return terms


def add_terms(terms):
    total = terms[0].astype(F32)
    for term in terms[1:]:
        total = total + term.astype(F32)
    return total


def dot(left, right):
    return jnp.dot(left, right, preferred_element_type=F32)


def dot_t(left, right):
    return lax.dot_general(left, right, (((1,), (1,)), ((), ())), preferred_element_type=F32)


def t_dot(left, right):
    return lax.dot_general(left, right, (((0,), (0,)), ((), ())), preferred_element_type=F32)


def after(value, *others):
    return lax.optimization_barrier((value,) + others)[0]


def pick(stacked, index, axis=0):
    return lax.dynamic_index_in_dim(stacked, index, axis, keepdims=False)


def pack_rows(vectors, rows, cols):
    total = jnp.zeros((rows, cols), vectors[0].dtype)
    for i, vec in enumerate(vectors):
        total = total + jnp.pad(
            vec.reshape(1, -1), ((i, rows - 1 - i), (0, cols - vec.shape[0]))
        )
    return total


def rows_of(v_refs, cols):
    row_of = lax.broadcasted_iota(jnp.int32, (16, 1), 0)
    total = jnp.zeros((16, cols), F32)
    for i, v_ref in enumerate(v_refs):
        vec = v_ref[...].astype(F32)
        wide = jnp.concatenate([vec, jnp.zeros((1, cols - vec.shape[1]), F32)], axis=1)
        total = jnp.where(row_of == i, wide, total)
    return total.astype(BF)


def pack_kernel(width, core_ref, w_ref, *refs):
    out_ref = refs[-1]
    parts = w_ref.shape[1] // (4 * width)
    rows = rows_of(refs[:-1], out_ref.shape[2])
    for f in range(8):
        for part in range(parts):
            at = width * (4 * part + f % 4)
            out_ref[f, :64, width * part : width * (part + 1)] = w_ref[:, at : at + width]
        out_ref[f, 64:] = rows


def pack(weight, vectors, core, width, name):
    cols = weight.shape[1]
    out = (8, 80, cols // 4)
    return pl.pallas_call(
        functools.partial(pack_kernel, width),
        grid_spec=pltpu.PrefetchScalarGridSpec(
            num_scalar_prefetch=1,
            grid=(1,),
            in_specs=[pl.BlockSpec((64, cols), lambda i, core: (core[0], 0))]
            + [pl.BlockSpec((1, v.shape[0]), lambda i, core: (0, 0)) for v in vectors],
            out_specs=pl.BlockSpec(out, lambda i, core: (0, 0, 0)),
        ),
        out_shape=jax.ShapeDtypeStruct(out, BF),
        compiler_params=pltpu.CompilerParams(vmem_limit_bytes=8 * 1024 * 1024),
        name=name,
    )(core.reshape(1), weight, *[v.reshape(1, -1) for v in vectors])


def project_kernel(
    core_ref, t0_ref, t1_ref, t2_ref, t3_ref, own_ref, far_ref, bias_ref, q_ref, kv_ref, w_ref
):
    lay_halves(core_ref[0], own_ref, far_ref, w_ref)
    weights = w_ref[...]
    width = q_ref.shape[1]
    for i, t_ref in enumerate((t0_ref, t1_ref, t2_ref, t3_ref)):
        rows = pl.ds(128 * i, 128)
        out = dot(t_ref[...], weights)
        queries = (out[:, :width] + bias_ref[0:1]).astype(BF).astype(F32)
        q_ref[rows] = (queries * HEAD_DIM**-0.5).astype(BF)
        kv_ref[rows, :width] = out[:, width : 2 * width].astype(BF)
        kv_ref[rows, width:] = (out[:, 2 * width :] + bias_ref[1:2]).astype(BF)


def project(token_blocks, own, far, bias, core):
    rows = 4 * token_blocks[0].shape[0]
    width = bias.shape[1]
    vmem = pl.BlockSpec(memory_space=pltpu.VMEM)
    return pl.pallas_call(
        project_kernel,
        in_specs=[pl.BlockSpec(memory_space=pltpu.SMEM)] + [vmem] * 7,
        out_specs=[vmem] * 3,
        out_shape=[
            jax.ShapeDtypeStruct((rows, width), BF),
            jax.ShapeDtypeStruct((rows, 2 * width), BF),
            jax.ShapeDtypeStruct((1024, 3 * width), BF),
        ],
        compiler_params=pltpu.CompilerParams(vmem_limit_bytes=12 * 1024 * 1024),
        cost_estimate=pl.CostEstimate(
            flops=6 * rows * 1024 * width, bytes_accessed=4 * 1024 * 1024, transcendentals=0
        ),
        name="project",
    )(core.reshape(1), *token_blocks, own, far, bias)


def attend_kernel(q_ref, own_ref, far_ref, mask_ref, ok_ref, w_ref, ctx_ref, p_ref, out_ref):
    queries = q_ref[...]
    width = queries.shape[1]
    half = own_ref.shape[0]
    head_of = lax.broadcasted_iota(jnp.int32, (1, width), 1) // HEAD_DIM
    context = jnp.zeros(queries.shape, F32)
    for h in range(width // HEAD_DIM):
        q_h = jnp.where(head_of == h, queries, jnp.zeros_like(queries))
        s_own = dot_t(q_h, own_ref[:, :width]) + mask_ref[:, :half]
        s_far = dot_t(q_h, far_ref[:, :width]) + mask_ref[:, half:]
        top = jnp.maximum(
            jnp.max(s_own, axis=1, keepdims=True), jnp.max(s_far, axis=1, keepdims=True)
        )
        e_own = jnp.exp(s_own - top)
        e_far = jnp.exp(s_far - top)
        scale = 1.0 / (
            jnp.sum(e_own, axis=1, keepdims=True) + jnp.sum(e_far, axis=1, keepdims=True)
        )
        p_own = (e_own * scale).astype(BF)
        p_far = (e_far * scale).astype(BF)
        p_ref[h, :, :half] = p_own
        p_ref[h, :, half:] = p_far
        out = dot(p_own, own_ref[:, width:]) + dot(p_far, far_ref[:, width:])
        context = jnp.where(head_of == h, out, context)
    low = (context * ok_ref[...]).astype(BF)
    ctx_ref[...] = low
    out_ref[...] = dot(low, w_ref[...]).astype(BF)


def attend(queries, kv_own, kv_far, key_mask, row_ok, out_w):
    rows, width = queries.shape
    heads = width // HEAD_DIM
    keys = 2 * kv_own.shape[0]
    step = 256
    return pl.pallas_call(
        attend_kernel,
        grid=(rows // step,),
        in_specs=[
            pl.BlockSpec((step, width), lambda i: (i, 0)),
            pl.BlockSpec(kv_own.shape, lambda i: (0, 0)),
            pl.BlockSpec(kv_far.shape, lambda i: (0, 0)),
            pl.BlockSpec((1, keys), lambda i: (0, 0)),
            pl.BlockSpec((step, 1), lambda i: (i, 0)),
            pl.BlockSpec(out_w.shape, lambda i: (0, 0)),
        ],
        out_specs=[
            pl.BlockSpec((step, width), lambda i: (i, 0)),
            pl.BlockSpec((heads, step, keys), lambda i: (0, i, 0)),
            pl.BlockSpec((step, out_w.shape[1]), lambda i: (i, 0)),
        ],
        out_shape=[
            jax.ShapeDtypeStruct((rows, width), BF),
            jax.ShapeDtypeStruct((heads, rows, keys), BF),
            jax.ShapeDtypeStruct((rows, out_w.shape[1]), BF),
        ],
        compiler_params=pltpu.CompilerParams(vmem_limit_bytes=16 * 1024 * 1024),
        cost_estimate=pl.CostEstimate(
            flops=16 * rows * keys * width, bytes_accessed=6 * 1024 * 1024, transcendentals=0
        ),
        name="attend",
    )(queries, kv_own, kv_far, key_mask, row_ok, out_w)


def attend_back_kernel(
    q_ref,
    own_ref,
    far_ref,
    grad_ref,
    ok_ref,
    w_ref,
    p_ref,
    here_ref,
    far_grad_ref,
    acc_own,
    acc_far,
):
    at = pl.program_id(0)
    queries = q_ref[...]
    grads = (dot_t(grad_ref[...], w_ref[...]) * ok_ref[...]).astype(BF)
    width = queries.shape[1]
    half = own_ref.shape[0]
    head_of = lax.broadcasted_iota(jnp.int32, (1, width), 1) // HEAD_DIM
    zero = jnp.zeros_like(queries)

    @pl.when(at == 0)
    def _():
        acc_own[...] = jnp.zeros_like(acc_own)
        acc_far[...] = jnp.zeros_like(acc_far)

    d_queries = jnp.zeros(queries.shape, F32)
    for h in range(width // HEAD_DIM):
        q_h = jnp.where(head_of == h, queries, zero)
        g_h = jnp.where(head_of == h, grads, zero)
        p_own_low = p_ref[h, :, :half]
        p_far_low = p_ref[h, :, half:]
        p_own = p_own_low.astype(F32)
        p_far = p_far_low.astype(F32)
        t_own = p_own * dot_t(g_h, own_ref[:, width:])
        t_far = p_far * dot_t(g_h, far_ref[:, width:])
        inner = jnp.sum(t_own, axis=1, keepdims=True) + jnp.sum(t_far, axis=1, keepdims=True)
        ds_own = (t_own - p_own * inner).astype(BF)
        ds_far = (t_far - p_far * inner).astype(BF)
        out = dot(ds_own, own_ref[:, :width]) + dot(ds_far, far_ref[:, :width])
        d_queries = jnp.where(head_of == h, out, d_queries)
        acc_own[:, :width] += t_dot(ds_own, q_h)
        acc_far[:, :width] += t_dot(ds_far, q_h)
        acc_own[:, width:] += t_dot(p_own_low, g_h)
        acc_far[:, width:] += t_dot(p_far_low, g_h)
    rows = pl.ds(pl.multiple_of(at * queries.shape[0], queries.shape[0]), queries.shape[0])
    here_ref[rows, :width] = (d_queries * HEAD_DIM**-0.5).astype(BF)

    @pl.when(at == pl.num_programs(0) - 1)
    def _():
        here_ref[:, width:] = acc_own[...].astype(BF)
        far_grad_ref[...] = acc_far[...].astype(BF)


def attend_back(queries, kv_own, kv_far, d_attn, row_ok, out_w, probs):
    rows, width = queries.shape
    heads, _, keys = probs.shape
    step = 256
    return pl.pallas_call(
        attend_back_kernel,
        grid=(rows // step,),
        in_specs=[
            pl.BlockSpec((step, width), lambda i: (i, 0)),
            pl.BlockSpec(kv_own.shape, lambda i: (0, 0)),
            pl.BlockSpec(kv_far.shape, lambda i: (0, 0)),
            pl.BlockSpec((step, d_attn.shape[1]), lambda i: (i, 0)),
            pl.BlockSpec((step, 1), lambda i: (i, 0)),
            pl.BlockSpec(out_w.shape, lambda i: (0, 0)),
            pl.BlockSpec((heads, step, keys), lambda i: (0, i, 0)),
        ],
        out_specs=[
            pl.BlockSpec((rows, 3 * width), lambda i: (0, 0)),
            pl.BlockSpec(kv_own.shape, lambda i: (0, 0)),
        ],
        out_shape=[
            jax.ShapeDtypeStruct((rows, 3 * width), BF),
            jax.ShapeDtypeStruct(kv_own.shape, BF),
        ],
        scratch_shapes=[pltpu.VMEM(kv_own.shape, F32), pltpu.VMEM(kv_own.shape, F32)],
        compiler_params=pltpu.CompilerParams(vmem_limit_bytes=20 * 1024 * 1024),
        cost_estimate=pl.CostEstimate(
            flops=40 * rows * keys * width, bytes_accessed=8 * 1024 * 1024, transcendentals=0
        ),
        name="attend_back",
    )(queries, kv_own, kv_far, d_attn, row_ok, out_w, probs)


def lay_halves(core, own_ref, far_ref, to_ref):
    def lay(low_ref, high_ref):
        for f in range(8):
            to_ref[128 * f : 128 * f + 64] = low_ref[f, :64]
            to_ref[128 * f + 64 : 128 * f + 128] = high_ref[f, :64]

    pl.when(core == 0)(lambda: lay(own_ref, far_ref))
    pl.when(core != 0)(lambda: lay(far_ref, own_ref))


def lay_down(where_ref, own_ref, mine_ref, other_ref, to_ref):
    def lay(y_hi, core):
        far = 512 * (1 - y_hi)
        to_ref[512 * y_hi : 512 * (y_hi + 1)] = own_ref[...]
        to_ref[far + 256 * core : far + 256 * (core + 1)] = mine_ref[...]
        to_ref[far + 256 * (1 - core) : far + 256 * (2 - core)] = other_ref[...]

    for y_hi in range(2):
        for core in range(2):
            here = (where_ref[0] == core) & (where_ref[1] == y_hi)
            pl.when(here)(functools.partial(lay, y_hi, core))


STEP = 256


def ffn_kernel(
    where_ref, x0_ref, x1_ref, x2_ref, x3_ref, bias_ref, up_own_ref, up_far_ref, down_ref,
    down_mine_ref, down_other_ref, act_ref, slope_ref, part_ref, x_ref, up_ref, w_ref,
):
    lay_halves(where_ref[0], up_own_ref, up_far_ref, up_ref)
    lay_down(where_ref, down_ref, down_mine_ref, down_other_ref, w_ref)
    for i, block_ref in enumerate((x0_ref, x1_ref, x2_ref, x3_ref)):
        rows = slice(128 * i, 128 * (i + 1))
        x_ref[rows] = block_ref[...]
    for i in range(2):
        rows = slice(256 * i, 256 * (i + 1))
        total = jnp.zeros((256, part_ref.shape[1]), F32)
        for at in range(0, act_ref.shape[1], STEP):
            cols = slice(at, at + STEP)
            hidden = dot(x_ref[rows], up_ref[:, cols]) + bias_ref[:, cols]
            cdf = 0.5 * (1.0 + lax.erf(hidden * 0.7071067811865476))
            active = (hidden * cdf).astype(BF)
            act_ref[rows, cols] = active
            slope = cdf + hidden * (0.3989422804014327 * jnp.exp(-0.5 * hidden * hidden))
            slope_ref[rows, cols] = slope.astype(BF)
            total += dot(active, w_ref[cols])
        part_ref[rows] = total.astype(BF)


def ffn(blocks, bias, weights, where):
    rows, width, units = 4 * blocks[0].shape[0], 1024, 1024
    vmem = pl.BlockSpec(memory_space=pltpu.VMEM)
    return pl.pallas_call(
        ffn_kernel,
        in_specs=[pl.BlockSpec(memory_space=pltpu.SMEM)] + [vmem] * 10,
        out_specs=[vmem] * 4,
        out_shape=[
            jax.ShapeDtypeStruct((rows, units), BF),
            jax.ShapeDtypeStruct((rows, units), BF),
            jax.ShapeDtypeStruct((rows, width), BF),
            jax.ShapeDtypeStruct((rows, width), BF),
        ],
        scratch_shapes=[pltpu.VMEM((width, units), BF), pltpu.VMEM((units, width), BF)],
        compiler_params=pltpu.CompilerParams(vmem_limit_bytes=24 * 1024 * 1024),
        cost_estimate=pl.CostEstimate(
            flops=4 * rows * width * units, bytes_accessed=8 * 1024 * 1024, transcendentals=0
        ),
        name="ffn",
    )(where, *blocks, bias, *weights)


def ffn_back_kernel(
    where_ref, d0_ref, d1_ref, d2_ref, d3_ref, act_ref, slope_ref, x_ref, up_own_ref, up_far_ref,
    down_ref, down_mine_ref, down_other_ref, part_ref, mine_ref, send_ref, hidden_sum_ref,
    out_sum_ref, d_ref, acc_ref, turned_ref, up_ref, w_ref,
):
    lay_halves(where_ref[0], up_own_ref, up_far_ref, up_ref)
    lay_down(where_ref, down_ref, down_mine_ref, down_other_ref, w_ref)
    total = jnp.zeros(out_sum_ref.shape, F32)
    for i, block_ref in enumerate((d0_ref, d1_ref, d2_ref, d3_ref)):
        block = block_ref[...]
        d_ref[128 * i : 128 * (i + 1)] = block
        total += jnp.sum(block.astype(F32), axis=0, keepdims=True)
    out_sum_ref[...] = total
    turned_ref[...] = x_ref[...].T
    own_core = where_ref[0]

    for at in range(4):
        cols = slice(STEP * at, STEP * (at + 1))
        d_hidden = slope_ref[:, cols].astype(F32) * dot_t(d_ref[...], w_ref[cols])
        d_hidden = d_hidden.astype(BF)
        hidden_sum_ref[:, cols] = jnp.sum(d_hidden.astype(F32), axis=0, keepdims=True)
        d_normed = dot_t(d_hidden, up_ref[:, cols])
        if at == 0:
            acc_ref[...] = d_normed
        elif at < 3:
            acc_ref[...] += d_normed
        else:
            part_ref[...] = (acc_ref[...] + d_normed).astype(BF)

        down = t_dot(act_ref[:, cols], d_ref[...]).astype(BF)
        up = dot(turned_ref[...], d_hidden).astype(BF)

        def store(to_ref, core, at=at, cols=cols, down=down, up=up):
            for x in range(4):
                if at % 2 == core:
                    to_ref[x, at // 2, :64] = down[64 * x : 64 * (x + 1)]
                for yh in range(2):
                    for z in range(4):
                        row = 512 * yh + 128 * z + 64 * core + 16 * x
                        to_ref[x, yh, 64 + 16 * z : 80 + 16 * z, cols] = up[row : row + 16]

        def store_all(core, store=store):
            store(mine_ref, core)
            store(send_ref, 1 - core)

        pl.when(own_core == 0)(functools.partial(store_all, 0))
        pl.when(own_core != 0)(functools.partial(store_all, 1))


def ffn_back(blocks, active, slope, normed, weights, where):
    rows, units = active.shape
    width = normed.shape[1]
    vmem = pl.BlockSpec(memory_space=pltpu.VMEM)
    grads = (4, 2, 128, 1024)
    return pl.pallas_call(
        ffn_back_kernel,
        in_specs=[pl.BlockSpec(memory_space=pltpu.SMEM)] + [vmem] * 12,
        out_specs=[vmem] * 5,
        out_shape=[
            jax.ShapeDtypeStruct((rows, width), BF),
            jax.ShapeDtypeStruct(grads, BF),
            jax.ShapeDtypeStruct(grads, BF),
            jax.ShapeDtypeStruct((1, units), F32),
            jax.ShapeDtypeStruct((1, width), F32),
        ],
        scratch_shapes=[
            pltpu.VMEM((rows, width), BF),
            pltpu.VMEM((rows, width), F32),
            pltpu.VMEM((width, rows), BF),
            pltpu.VMEM((width, units), BF),
            pltpu.VMEM((units, width), BF),
        ],
        compiler_params=pltpu.CompilerParams(vmem_limit_bytes=32 * 1024 * 1024),
        cost_estimate=pl.CostEstimate(
            flops=8 * rows * width * units, bytes_accessed=12 * 1024 * 1024, transcendentals=0
        ),
        name="ffn_back",
    )(where, *blocks, active, slope, normed, *weights)


def grad_second_kernel(
    core_ref, tok_ref, tok_far_ref, here_ref, far_ref, ctx_ref, attn_ref, sums_ref, mine_ref,
    send_ref, vec_ref,
):
    at = pl.program_id(0)
    grads = t_dot(tok_ref[...], here_ref[...])
    grads_far = t_dot(tok_far_ref[...], far_ref[...])
    queries = grads[:, :256].astype(BF)
    others = (grads[:, 256:] + grads_far).astype(BF)
    attn = t_dot(ctx_ref[...], attn_ref[...]).astype(BF)

    def store(core, put):
        for x in range(4):
            for z in range(4):
                row = 64 * core + 16 * x
                rows = slice(128 * z + row, 128 * z + row + 16)
                put(x, z, slice(0, 256), queries[rows])
                put(x, z, slice(256, 768), others[rows])
                put(x, z, slice(768, 1024), attn[row : row + 16, 256 * z : 256 * z + 256])

    def put_mine(x, z, cols, value):
        mine_ref[x, 0, 16 * z : 16 * z + 16, cols] = value

    def put_send(x, z, cols, value):
        first = pl.multiple_of(128 * x + 64 * at + 16 * z, 16)
        send_ref[pl.ds(first, 16), cols] = value

    def store_all(core):
        store(core, put_mine)
        store(1 - core, put_send)

    pl.when(core_ref[0] == 0)(lambda: store_all(0))
    pl.when(core_ref[0] != 0)(lambda: store_all(1))

    @pl.when(pl.program_id(0) == 0)
    def _():
        here = jnp.sum(here_ref[...].astype(F32), axis=0, keepdims=True)
        far = jnp.sum(far_ref[...].astype(F32), axis=0, keepdims=True)
        bias = jnp.concatenate(
            [here[:, :256], here[:, 512:] + far[:, 256:], jnp.zeros((1, 512), F32)], axis=1
        )
        attn_sum = jnp.sum(attn_ref[...].astype(F32), axis=0, keepdims=True)
        row_of = lax.broadcasted_iota(jnp.int32, (16, 1), 0)
        total = jnp.where(row_of == 0, bias, sums_ref[...])
        low = jnp.where(row_of == 2, attn_sum, total).astype(BF)
        vec_ref[...] = low
        send_ref[512:] = low


def grad_second(tokens_own, tokens_far, d_here, d_far, context, d_attn, sums, core):
    rows, cols = tokens_own.shape
    half = cols // 2
    return pl.pallas_call(
        grad_second_kernel,
        grid_spec=pltpu.PrefetchScalarGridSpec(
            num_scalar_prefetch=1,
            grid=(2,),
            in_specs=[
                pl.BlockSpec((rows, half), lambda i, core: (0, i)),
                pl.BlockSpec((rows, half), lambda i, core: (0, i)),
                pl.BlockSpec(d_here.shape, lambda i, core: (0, 0)),
                pl.BlockSpec(d_far.shape, lambda i, core: (0, 0)),
                pl.BlockSpec((rows, context.shape[1] // 2), lambda i, core: (0, i)),
                pl.BlockSpec(d_attn.shape, lambda i, core: (0, 0)),
                pl.BlockSpec(sums.shape, lambda i, core: (0, 0)),
            ],
            out_specs=[
                pl.BlockSpec((4, 1, 64, 1024), lambda i, core: (0, i, 0, 0)),
                pl.BlockSpec((528, 1024), lambda i, core: (0, 0)),
                pl.BlockSpec(sums.shape, lambda i, core: (0, 0)),
            ],
        ),
        out_shape=[
            jax.ShapeDtypeStruct((4, 2, 64, 1024), BF),
            jax.ShapeDtypeStruct((528, 1024), BF),
            jax.ShapeDtypeStruct(sums.shape, BF),
        ],
        compiler_params=pltpu.CompilerParams(vmem_limit_bytes=16 * 1024 * 1024),
        cost_estimate=pl.CostEstimate(
            flops=3 * rows * cols * 1024, bytes_accessed=8 * 1024 * 1024, transcendentals=0
        ),
        name="grad_second",
    )(core.reshape(1), tokens_own, tokens_far, d_here, d_far, context, d_attn, sums)


def norm_stats(values):
    mean = jnp.mean(values, axis=-1, keepdims=True)
    centered = values - mean
    rstd = lax.rsqrt(jnp.mean(centered * centered, axis=-1, keepdims=True) + EPSILON)
    return centered * rstd, rstd


def norm_back(grad_out, gain, xhat, rstd):
    g = grad_out * gain
    return rstd * (
        g
        - jnp.mean(g, axis=-1, keepdims=True)
        - xhat * jnp.mean(g * xhat, axis=-1, keepdims=True)
    )


def unroll_ring(blocks, index):
    stacked = jnp.concatenate([b[None] for b in blocks + blocks], axis=0)
    return lax.dynamic_slice_in_dim(stacked, (4 - index) % 4, 4, axis=0)


def swap(value, axis, groups):
    return lax.all_to_all(value, axis, 0, 0, axis_index_groups=groups, tiled=True)


Z_RINGS = [[0, 1, 2, 3], [4, 5, 6, 7]]
X_RINGS = [[8 * yl + 2 * x + core for x in range(4)] for yl in range(2) for core in range(2)]


def with_rows(block, vectors):
    flat = block.reshape(-1, block.shape[-1])
    return flat if vectors is None else jnp.concatenate([flat, vectors], axis=0)


def core_sum(mine, vectors, got):
    rows = mine.size // mine.shape[-1]
    total = (mine.astype(F32) + got[:rows].reshape(mine.shape).astype(F32)).astype(BF)
    if vectors is None:
        return total, None
    return total, (vectors.astype(F32) + got[rows:].astype(F32)).astype(BF)


def x_send(pieces, x):
    return [pick(pieces, x)] + [x_shift(pick(pieces, (x + k) % 4), k) for k in (1, 2, 3)]


def x_flat(pieces, vectors):
    flat = pieces.reshape(4, -1, pieces.shape[-1])
    return jnp.concatenate([flat, jnp.broadcast_to(vectors, (4,) + vectors.shape)], axis=1)


def x_sum(got, rows):
    total = jnp.sum(got.astype(F32), axis=0).astype(BF)
    return total[: 2 * rows].reshape(2, rows, -1), total[2 * rows :]


def y_send(pieces, vectors, yh):
    own, other = pick(pieces, yh), pick(pieces, 1 - yh)
    got = [
        y_flip(with_rows(block, vectors), lo, hi)
        for block, lo, hi in ((own, 1, 0), (other, 0, 1), (other, 1, 1))
    ]
    return [with_rows(own, vectors)] + got


def ring_of(piece):
    return [piece] + [x_shift(piece, -k) for k in (1, 2, 3)]


def both_cores(blocks, *others):
    ring = jnp.stack(after(tuple(blocks), *others), axis=0)
    return ring, core_flip(ring)


def lay_first_kernel(where_ref, ring_ref, far_ref, down_ref, up_ref):
    def lay(src_ref):
        for k in range(4):
            x = (where_ref[2] + k) % 4
            down_ref[pl.ds(pl.multiple_of(64 * x, 64), 64)] = src_ref[k, :64].astype(F32)
            rows = pl.ds(pl.multiple_of(16 * x, 16), 16)
            for z in range(4):
                block = src_ref[k, 64 + 16 * z : 80 + 16 * z].astype(F32)
                up_ref[rows, 512 * z : 512 * (z + 1)] = block[:, :512]
                up_ref[rows, 2048 + 512 * z : 2048 + 512 * (z + 1)] = block[:, 512:]

    at = pl.program_id(0)
    pl.when(at == 0)(lambda: lay(ring_ref))
    pl.when(at == 1)(lambda: lay(far_ref))


def lay_second_kernel(where_ref, ring_ref, far_ref, qkv_ref, out_ref):
    def lay(src_ref):
        for k in range(4):
            rows = pl.ds(pl.multiple_of(16 * ((where_ref[2] + k) % 4), 16), 16)
            for z in range(4):
                block = src_ref[k, 16 * z : 16 * (z + 1)].astype(F32)
                for part in range(6):
                    at = 512 * part + 128 * z
                    qkv_ref[rows, at : at + 128] = block[:, 128 * part : 128 * (part + 1)]
                out_ref[rows, 256 * z : 256 * (z + 1)] = block[:, 768:]

    at = pl.program_id(0)
    pl.when(at == 0)(lambda: lay(ring_ref))
    pl.when(at == 1)(lambda: lay(far_ref))


def lay_pieces(kernel, ring, far, blocks, place, name):
    x, core = place[1], place[2]
    where = jnp.stack([core, 1 - core, x]).astype(jnp.int32)
    return pl.pallas_call(
        kernel,
        grid_spec=pltpu.PrefetchScalarGridSpec(
            num_scalar_prefetch=1,
            grid=(2,),
            in_specs=[
                pl.BlockSpec(ring.shape, lambda i, where: (0, 0, 0)),
                pl.BlockSpec(far.shape, lambda i, where: (0, 0, 0)),
            ],
            out_specs=[
                pl.BlockSpec((4 * rows, cols), lambda i, where: (where[i], 0))
                for rows, cols in blocks
            ],
        ),
        out_shape=[jax.ShapeDtypeStruct((8 * rows, cols), F32) for rows, cols in blocks],
        compiler_params=pltpu.CompilerParams(vmem_limit_bytes=16 * 1024 * 1024),
        name=name,
    )(where, ring, far)


def on_device(
    tokens,
    counts,
    w_qkv,
    bias_qv,
    w_out,
    bias_out,
    gain_attn,
    shift_attn,
    w_up,
    bias_up,
    w_down,
    bias_down,
    gain_ffn,
    shift_ffn,
    cotangent,
):
    row_count, model_width = tokens.shape
    replica = lax.axis_index("replica")
    group = lax.axis_index("fsdp")
    yl, x, core = replica // 8, (replica // 2) % 4, replica % 2
    yh, z = group // 4, group % 4
    place = (yl, x, core, yh, z)
    lanes = 128
    counts_row = counts[0]

    ring = (z + jnp.arange(4, dtype=jnp.int32)) % 4
    own_counts = jnp.take(counts_row, yh * 4 + ring)
    far_counts = jnp.take(counts_row, (1 - yh) * 4 + ring)
    slot = jnp.arange(row_count, dtype=jnp.int32)
    own_ok = (slot[None, :] < own_counts[:, None]).reshape(-1)
    far_ok = (slot[None, :] < far_counts[:, None]).reshape(-1)
    key_mask = jnp.where(jnp.concatenate([own_ok, far_ok]), 0.0, -1e30).astype(F32)[None, :]
    row_ok = own_ok.astype(F32)[:, None]

    sent = pack(w_qkv, (bias_qv,), core, lanes, "pack_qkv")
    small = (bias_out, gain_attn, shift_attn, bias_up, bias_down, gain_ffn, shift_ffn)
    up_sent = pack(w_up, small, core, 512, "pack_up")
    token_blocks = z_gather(tokens)
    out_far = y_flip(w_out, 0, 1)
    got = lax.all_to_all(sent, "fsdp", 0, 0, tiled=True)
    got_far = core_flip(got.reshape(640, 768)).reshape(8, 80, 768)
    bias_own = got[:, 64, :256].astype(F32).reshape(2, 2, 4, lanes)
    bias_own = pick(bias_own, z, 2).reshape(2, 2 * lanes)

    tokens_all = jnp.concatenate(token_blocks, axis=0)
    queries, kv_own, qkv_w = project(token_blocks, got, got_far, bias_own, core)
    kv_far = y_flip(kv_own, 0, 1)

    up_own = swap(after(up_sent, kv_own), "fsdp", None)
    vec_all = up_own[:, 64:72].astype(F32)
    bout_all = vec_all[:, 0, :lanes].reshape(1, -1)
    ga_all = vec_all[:, 1, :lanes].reshape(1, -1)
    sa_all = vec_all[:, 2, :lanes].reshape(1, -1)
    bup_own = pick(vec_all[:, 3, :512].reshape(2, 4, 512), z, 1).reshape(1, -1)
    bdown_all = vec_all[:, 4, :lanes].reshape(1, -1)
    gf_all = vec_all[:, 5, :lanes].reshape(1, -1)
    sf_all = vec_all[:, 6, :lanes].reshape(1, -1)
    up_far = core_flip(after(up_own, kv_far).reshape(640, 1024)).reshape(8, 80, 1024)
    down_mine = y_flip(pick(after(w_down, kv_far).reshape(2, 256, 1024), core), 0, 1)
    where = jnp.stack([core, yh]).astype(jnp.int32)

    def order(own, far):
        return jnp.where(
            yh == 0, jnp.concatenate([own, far], axis=0), jnp.concatenate([far, own], axis=0)
        )

    out_w = order(w_out, out_far)
    context, probs, attn_part = attend(queries, kv_own, kv_far, key_mask, row_ok, out_w)
    resid1 = add_terms([tokens] + z_scatter(attn_part)) + bout_all
    xhat1, rstd1 = norm_stats(resid1)
    normed = xhat1 * ga_all + sa_all
    normed_blocks = z_gather(normed.astype(BF))
    down_other = core_flip(after(down_mine, normed_blocks[2]))
    weights = (up_own, up_far, w_down, down_mine, down_other)
    active, slope, ffn_part, normed_all = ffn(normed_blocks, bup_own, weights, where)
    tokens_far = y_flip(after(tokens_all, ffn_part), 0, 1)
    resid2 = add_terms([normed] + z_scatter(ffn_part)) + bdown_all
    xhat2, rstd2 = norm_stats(resid2)
    layer_out = (xhat2 * gf_all + sf_all).astype(BF)

    cot = cotangent.astype(F32)
    d_resid2 = norm_back(cot, gf_all, xhat2, rstd2)

    dn_part, first, first_sent, hidden_sum, ffn_sum = ffn_back(
        z_gather(d_resid2.astype(BF)), active, slope, normed_all, weights, where
    )
    dn_terms = z_scatter(dn_part)
    first_got = core_flip(first_sent.reshape(1024, 1024))

    d_normed = add_terms([d_resid2] + dn_terms)
    d_resid1 = norm_back(d_normed, ga_all, xhat1, rstd1)
    dattn_blocks = z_gather(d_resid1.astype(BF))
    first_core, _ = core_sum(first, None, after(first_got, d_resid1))
    first_got = x_send(first_core, x)
    dattn_all = jnp.concatenate(dattn_blocks, axis=0)
    d_here, dkv_far = attend_back(
        queries, kv_own, kv_far, dattn_all, row_ok, out_w, probs
    )

    zero = jnp.zeros((1024,), F32)
    sums = pack_rows(
        [
            zero,
            hidden_sum[0],
            zero,
            ffn_sum[0],
            jnp.sum(d_normed * xhat1, axis=0),
            jnp.sum(d_normed, axis=0),
            jnp.sum(cot * xhat2, axis=0),
            jnp.sum(cot, axis=0),
        ],
        16,
        1024,
    )
    far_terms = y_flip(dkv_far, 0, 1)
    second, second_sent, vectors = grad_second(
        tokens_all, tokens_far, after(d_here, *first_got), dkv_far, context, dattn_all, sums, core
    )

    second_got = core_flip(second_sent)
    first_x = add_terms(after(tuple(first_got), second)).astype(BF)
    first_terms = y_send(first_x, None, yh)
    second_core, vec_core = core_sum(second, vectors, after(second_got, first_x))
    second_flat = x_flat(second_core, vec_core)
    second_got = swap(second_flat, "replica", X_RINGS)

    far_terms = after(far_terms, second_flat)
    dkv = (d_here[:, 256:].astype(F32) + far_terms.astype(F32)).astype(BF)
    d_projected = jnp.concatenate([d_here[:, :256], dkv], axis=1)

    second_x, vec_x = x_sum(after(second_got, far_terms), 64)
    second_terms = y_send(second_x, vec_x, yh)
    first_sum = add_terms(after(tuple(first_terms), second_x)).astype(BF)
    up_sum = swap(after(first_sum, second_x)[64:].reshape(4, 16, 1024), "fsdp", Z_RINGS)
    up_sum = up_sum.reshape(64, 1024)

    first_ring = ring_of(jnp.concatenate([first_sum[:64], up_sum], axis=0))
    second_all = add_terms(after(tuple(second_terms), up_sum)).astype(BF)
    second_sum, vec_sum = second_all[:64], second_all[64:]
    input_part = dot_t(after(d_projected, up_sum), qkv_w).astype(BF)
    input_grad = add_terms([d_resid1] + z_scatter(input_part))
    bias_row = jnp.broadcast_to(vec_sum[None, 0:1, :512], (4, 1, 512))
    norm_row = pick(vec_sum[4:8].reshape(4, 2, 4, lanes), yh, 1).transpose(1, 0, 2)
    side = jnp.pad(
        jnp.concatenate([bias_row, norm_row.reshape(4, 1, 512)], axis=1),
        ((0, 0), (0, 14), (0, 256)),
    )
    swapped = swap(
        jnp.concatenate([second_sum[:, :768].reshape(4, 16, 768), side], axis=1), "fsdp", Z_RINGS
    )
    second_ring = ring_of(
        jnp.concatenate([swapped[:, :16].reshape(64, 768), second_sum[:, 768:]], axis=1)
    )
    ring, far = both_cores(first_ring, swapped)
    grad_w_down, grad_w_up = lay_pieces(
        lay_first_kernel, ring, far, ((64, 1024), (16, 4096)), place, "lay_first"
    )
    ring, far = both_cores(second_ring, grad_w_down)
    grad_w_qkv, grad_w_out = lay_pieces(
        lay_second_kernel, ring, far, ((16, 3072), (16, 1024)), place, "lay_second"
    )
    bqv_all = swapped[:, 16, :512].astype(F32).reshape(4, 2, 2, lanes).transpose(1, 2, 0, 3)
    grad_bqv = pick(bqv_all.reshape(8, 256), group)
    norms = jnp.sum(swapped[:, 17, :512].astype(F32), axis=0).reshape(4, lanes)
    grad_bup = pick(vec_sum[1].reshape(2, 512), yh).astype(F32)
    rest = pick(vec_sum[2:4].reshape(2, 8, lanes), group, 1).astype(F32)

    return (
        layer_out,
        input_grad,
        grad_w_qkv,
        grad_bqv,
        grad_w_out,
        rest[0],
        norms[0],
        norms[1],
        grad_w_up,
        grad_bup,
        grad_w_down,
        rest[1],
        norms[2],
        norms[3],
    )


def solution(mesh):
    in_specs = (
        P(("replica", "fsdp"), None),
        P("replica", None),
        P("fsdp", None),
        P("fsdp"),
        P("fsdp", None),
        P("fsdp"),
        P("fsdp"),
        P("fsdp"),
        P("fsdp", None),
        P("fsdp"),
        P("fsdp", None),
        P("fsdp"),
        P("fsdp"),
        P("fsdp"),
        P(("replica", "fsdp"), None),
    )
    out_specs = (
        P(("replica", "fsdp"), None),
        P(("replica", "fsdp"), None),
        P("fsdp", None),
        P("fsdp"),
        P("fsdp", None),
        P("fsdp"),
        P("fsdp"),
        P("fsdp"),
        P("fsdp", None),
        P("fsdp"),
        P("fsdp", None),
        P("fsdp"),
        P("fsdp"),
        P("fsdp"),
    )
    return jax.shard_map(
        on_device, mesh=mesh, in_specs=in_specs, out_specs=out_specs, check_vma=False
    )
```

```python
import functools

import jax
import jax.numpy as jnp
from jax import lax
from jax.experimental import pallas as pl
from jax.experimental.pallas import tpu as pltpu
from jax.sharding import PartitionSpec as P

HEAD_DIM = 64
EPSILON = 1e-05
BF = jnp.bfloat16
F32 = jnp.float32
BOTH = ("replica", "fsdp")


def all_pairs(move):
    pairs = []
    for yl in range(2):
        for x in range(4):
            for core in range(2):
                for yh in range(2):
                    for z in range(4):
                        a, b, c, d, e = move(yl, x, core, yh, z)
                        pairs.append(
                            (
                                ((yl * 4 + x) * 2 + core) * 8 + yh * 4 + z,
                                ((a * 4 + b) * 2 + c) * 8 + d * 4 + e,
                            )
                        )
    return pairs


def z_shift(value, k):
    return lax.ppermute(
        value, BOTH, all_pairs(lambda yl, x, c, yh, z: (yl, x, c, yh, (z + k) % 4))
    )


def x_shift(value, k):
    return lax.ppermute(
        value, BOTH, all_pairs(lambda yl, x, c, yh, z: (yl, (x + k) % 4, c, yh, z))
    )


def core_flip(value):
    return lax.ppermute(value, BOTH, all_pairs(lambda yl, x, c, yh, z: (yl, x, 1 - c, yh, z)))


def y_flip(value, lo, hi):
    return lax.ppermute(
        value, BOTH, all_pairs(lambda yl, x, c, yh, z: (yl ^ lo, x, c, yh ^ hi, z))
    )


def z_gather(value):
    return [value] + [z_shift(value, -k) for k in (1, 2, 3)]


def z_scatter(partial):
    rows = partial.shape[0] // 4
    terms = [partial[:rows]]
    for k in (1, 2, 3):
        terms.append(z_shift(partial[k * rows : (k + 1) * rows], k))
    return terms


def add_terms(terms):
    total = terms[0].astype(F32)
    for term in terms[1:]:
        total = total + term.astype(F32)
    return total


def dot(left, right):
    return jnp.dot(left, right, preferred_element_type=F32)


def dot_t(left, right):
    return lax.dot_general(left, right, (((1,), (1,)), ((), ())), preferred_element_type=F32)


def t_dot(left, right):
    return lax.dot_general(left, right, (((0,), (0,)), ((), ())), preferred_element_type=F32)


def after(value, *others):
    return lax.optimization_barrier((value,) + others)[0]


def pick(stacked, index, axis=0):
    return lax.dynamic_index_in_dim(stacked, index, axis, keepdims=False)


def pack_rows(vectors, rows, cols):
    total = jnp.zeros((rows, cols), vectors[0].dtype)
    for i, vec in enumerate(vectors):
        total = total + jnp.pad(
            vec.reshape(1, -1), ((i, rows - 1 - i), (0, cols - vec.shape[0]))
        )
    return total


def rows_of(v_refs, cols):
    row_of = lax.broadcasted_iota(jnp.int32, (16, 1), 0)
    total = jnp.zeros((16, cols), F32)
    for i, v_ref in enumerate(v_refs):
        vec = v_ref[...].astype(F32)
        wide = jnp.concatenate([vec, jnp.zeros((1, cols - vec.shape[1]), F32)], axis=1)
        total = jnp.where(row_of == i, wide, total)
    return total.astype(BF)


def pack_kernel(width, core_ref, w_ref, *refs):
    out_ref = refs[-1]
    parts = w_ref.shape[1] // (4 * width)
    rows = rows_of(refs[:-1], out_ref.shape[2])
    for f in range(8):
        for part in range(parts):
            at = width * (4 * part + f % 4)
            out_ref[f, :64, width * part : width * (part + 1)] = w_ref[:, at : at + width]
        out_ref[f, 64:] = rows


def pack(weight, vectors, core, width, name):
    cols = weight.shape[1]
    out = (8, 80, cols // 4)
    return pl.pallas_call(
        functools.partial(pack_kernel, width),
        grid_spec=pltpu.PrefetchScalarGridSpec(
            num_scalar_prefetch=1,
            grid=(1,),
            in_specs=[pl.BlockSpec((64, cols), lambda i, core: (core[0], 0))]
            + [pl.BlockSpec((1, v.shape[0]), lambda i, core: (0, 0)) for v in vectors],
            out_specs=pl.BlockSpec(out, lambda i, core: (0, 0, 0)),
        ),
        out_shape=jax.ShapeDtypeStruct(out, BF),
        compiler_params=pltpu.CompilerParams(vmem_limit_bytes=8 * 1024 * 1024),
        name=name,
    )(core.reshape(1), weight, *[v.reshape(1, -1) for v in vectors])


def project_kernel(
    core_ref, t0_ref, t1_ref, t2_ref, t3_ref, own_ref, far_ref, bias_ref, q_ref, kv_ref, w_ref
):
    lay_halves(core_ref[0], own_ref, far_ref, w_ref)
    weights = w_ref[...]
    width = q_ref.shape[1]
    for i, t_ref in enumerate((t0_ref, t1_ref, t2_ref, t3_ref)):
        rows = pl.ds(128 * i, 128)
        out = dot(t_ref[...], weights)
        queries = (out[:, :width] + bias_ref[0:1]).astype(BF).astype(F32)
        q_ref[rows] = (queries * HEAD_DIM**-0.5).astype(BF)
        kv_ref[rows, :width] = out[:, width : 2 * width].astype(BF)
        kv_ref[rows, width:] = (out[:, 2 * width :] + bias_ref[1:2]).astype(BF)


def project(token_blocks, own, far, bias, core):
    rows = 4 * token_blocks[0].shape[0]
    width = bias.shape[1]
    vmem = pl.BlockSpec(memory_space=pltpu.VMEM)
    return pl.pallas_call(
        project_kernel,
        in_specs=[pl.BlockSpec(memory_space=pltpu.SMEM)] + [vmem] * 7,
        out_specs=[vmem] * 3,
        out_shape=[
            jax.ShapeDtypeStruct((rows, width), BF),
            jax.ShapeDtypeStruct((rows, 2 * width), BF),
            jax.ShapeDtypeStruct((1024, 3 * width), BF),
        ],
        compiler_params=pltpu.CompilerParams(vmem_limit_bytes=12 * 1024 * 1024),
        cost_estimate=pl.CostEstimate(
            flops=6 * rows * 1024 * width, bytes_accessed=4 * 1024 * 1024, transcendentals=0
        ),
        name="project",
    )(core.reshape(1), *token_blocks, own, far, bias)


def attend_kernel(q_ref, own_ref, far_ref, mask_ref, ok_ref, w_ref, ctx_ref, p_ref, out_ref):
    queries = q_ref[...]
    width = queries.shape[1]
    half = own_ref.shape[0]
    head_of = lax.broadcasted_iota(jnp.int32, (1, width), 1) // HEAD_DIM
    context = jnp.zeros(queries.shape, F32)
    for h in range(width // HEAD_DIM):
        q_h = jnp.where(head_of == h, queries, jnp.zeros_like(queries))
        s_own = dot_t(q_h, own_ref[:, :width]) + mask_ref[:, :half]
        s_far = dot_t(q_h, far_ref[:, :width]) + mask_ref[:, half:]
        top = jnp.maximum(
            jnp.max(s_own, axis=1, keepdims=True), jnp.max(s_far, axis=1, keepdims=True)
        )
        e_own = jnp.exp(s_own - top)
        e_far = jnp.exp(s_far - top)
        scale = 1.0 / (
            jnp.sum(e_own, axis=1, keepdims=True) + jnp.sum(e_far, axis=1, keepdims=True)
        )
        p_own = (e_own * scale).astype(BF)
        p_far = (e_far * scale).astype(BF)
        p_ref[h, :, :half] = p_own
        p_ref[h, :, half:] = p_far
        out = dot(p_own, own_ref[:, width:]) + dot(p_far, far_ref[:, width:])
        context = jnp.where(head_of == h, out, context)
    low = (context * ok_ref[...]).astype(BF)
    ctx_ref[...] = low
    out_ref[...] = dot(low, w_ref[...]).astype(BF)


def attend(queries, kv_own, kv_far, key_mask, row_ok, out_w):
    rows, width = queries.shape
    heads = width // HEAD_DIM
    keys = 2 * kv_own.shape[0]
    step = 256
    return pl.pallas_call(
        attend_kernel,
        grid=(rows // step,),
        in_specs=[
            pl.BlockSpec((step, width), lambda i: (i, 0)),
            pl.BlockSpec(kv_own.shape, lambda i: (0, 0)),
            pl.BlockSpec(kv_far.shape, lambda i: (0, 0)),
            pl.BlockSpec((1, keys), lambda i: (0, 0)),
            pl.BlockSpec((step, 1), lambda i: (i, 0)),
            pl.BlockSpec(out_w.shape, lambda i: (0, 0)),
        ],
        out_specs=[
            pl.BlockSpec((step, width), lambda i: (i, 0)),
            pl.BlockSpec((heads, step, keys), lambda i: (0, i, 0)),
            pl.BlockSpec((step, out_w.shape[1]), lambda i: (i, 0)),
        ],
        out_shape=[
            jax.ShapeDtypeStruct((rows, width), BF),
            pltpu.HBM((heads, rows, keys), BF),
            jax.ShapeDtypeStruct((rows, out_w.shape[1]), BF),
        ],
        compiler_params=pltpu.CompilerParams(vmem_limit_bytes=16 * 1024 * 1024),
        cost_estimate=pl.CostEstimate(
            flops=16 * rows * keys * width, bytes_accessed=6 * 1024 * 1024, transcendentals=0
        ),
        name="attend",
    )(queries, kv_own, kv_far, key_mask, row_ok, out_w)


def attend_back_kernel(
    q_ref,
    own_ref,
    far_ref,
    grad_ref,
    ok_ref,
    w_ref,
    p_ref,
    here_ref,
    far_grad_ref,
    acc_own,
    acc_far,
):
    at = pl.program_id(0)
    queries = q_ref[...]
    grads = (dot_t(grad_ref[...], w_ref[...]) * ok_ref[...]).astype(BF)
    width = queries.shape[1]
    half = own_ref.shape[0]
    head_of = lax.broadcasted_iota(jnp.int32, (1, width), 1) // HEAD_DIM
    zero = jnp.zeros_like(queries)

    @pl.when(at == 0)
    def _():
        acc_own[...] = jnp.zeros_like(acc_own)
        acc_far[...] = jnp.zeros_like(acc_far)

    d_queries = jnp.zeros(queries.shape, F32)
    for h in range(width // HEAD_DIM):
        q_h = jnp.where(head_of == h, queries, zero)
        g_h = jnp.where(head_of == h, grads, zero)
        p_own_low = p_ref[h, :, :half]
        p_far_low = p_ref[h, :, half:]
        p_own = p_own_low.astype(F32)
        p_far = p_far_low.astype(F32)
        t_own = p_own * dot_t(g_h, own_ref[:, width:])
        t_far = p_far * dot_t(g_h, far_ref[:, width:])
        inner = jnp.sum(t_own, axis=1, keepdims=True) + jnp.sum(t_far, axis=1, keepdims=True)
        ds_own = (t_own - p_own * inner).astype(BF)
        ds_far = (t_far - p_far * inner).astype(BF)
        out = dot(ds_own, own_ref[:, :width]) + dot(ds_far, far_ref[:, :width])
        d_queries = jnp.where(head_of == h, out, d_queries)
        acc_own[:, :width] += t_dot(ds_own, q_h)
        acc_far[:, :width] += t_dot(ds_far, q_h)
        acc_own[:, width:] += t_dot(p_own_low, g_h)
        acc_far[:, width:] += t_dot(p_far_low, g_h)
    rows = pl.ds(pl.multiple_of(at * queries.shape[0], queries.shape[0]), queries.shape[0])
    here_ref[rows, :width] = (d_queries * HEAD_DIM**-0.5).astype(BF)

    @pl.when(at == pl.num_programs(0) - 1)
    def _():
        here_ref[:, width:] = acc_own[...].astype(BF)
        far_grad_ref[...] = acc_far[...].astype(BF)


def attend_back(queries, kv_own, kv_far, d_attn, row_ok, out_w, probs):
    rows, width = queries.shape
    heads, _, keys = probs.shape
    step = 256
    return pl.pallas_call(
        attend_back_kernel,
        grid=(rows // step,),
        in_specs=[
            pl.BlockSpec((step, width), lambda i: (i, 0)),
            pl.BlockSpec(kv_own.shape, lambda i: (0, 0)),
            pl.BlockSpec(kv_far.shape, lambda i: (0, 0)),
            pl.BlockSpec((step, d_attn.shape[1]), lambda i: (i, 0)),
            pl.BlockSpec((step, 1), lambda i: (i, 0)),
            pl.BlockSpec(out_w.shape, lambda i: (0, 0)),
            pl.BlockSpec((heads, step, keys), lambda i: (0, i, 0)),
        ],
        out_specs=[
            pl.BlockSpec((rows, 3 * width), lambda i: (0, 0)),
            pl.BlockSpec(kv_own.shape, lambda i: (0, 0)),
        ],
        out_shape=[
            jax.ShapeDtypeStruct((rows, 3 * width), BF),
            jax.ShapeDtypeStruct(kv_own.shape, BF),
        ],
        scratch_shapes=[pltpu.VMEM(kv_own.shape, F32), pltpu.VMEM(kv_own.shape, F32)],
        compiler_params=pltpu.CompilerParams(vmem_limit_bytes=20 * 1024 * 1024),
        cost_estimate=pl.CostEstimate(
            flops=40 * rows * keys * width, bytes_accessed=8 * 1024 * 1024, transcendentals=0
        ),
        name="attend_back",
    )(queries, kv_own, kv_far, d_attn, row_ok, out_w, probs)


def lay_halves(core, own_ref, far_ref, to_ref):
    def lay(low_ref, high_ref):
        for f in range(8):
            to_ref[128 * f : 128 * f + 64] = low_ref[f, :64]
            to_ref[128 * f + 64 : 128 * f + 128] = high_ref[f, :64]

    pl.when(core == 0)(lambda: lay(own_ref, far_ref))
    pl.when(core != 0)(lambda: lay(far_ref, own_ref))


def lay_down(where_ref, own_ref, mine_ref, other_ref, to_ref):
    def lay(y_hi, core):
        far = 512 * (1 - y_hi)
        to_ref[512 * y_hi : 512 * (y_hi + 1)] = own_ref[...]
        to_ref[far + 256 * core : far + 256 * (core + 1)] = mine_ref[...]
        to_ref[far + 256 * (1 - core) : far + 256 * (2 - core)] = other_ref[...]

    for y_hi in range(2):
        for core in range(2):
            here = (where_ref[0] == core) & (where_ref[1] == y_hi)
            pl.when(here)(functools.partial(lay, y_hi, core))


STEP = 256


def ffn_kernel(
    where_ref, x0_ref, x1_ref, x2_ref, x3_ref, bias_ref, up_own_ref, up_far_ref, down_ref,
    down_mine_ref, down_other_ref, act_ref, slope_ref, part_ref, x_ref, up_ref, w_ref,
):
    lay_halves(where_ref[0], up_own_ref, up_far_ref, up_ref)
    lay_down(where_ref, down_ref, down_mine_ref, down_other_ref, w_ref)
    for i, block_ref in enumerate((x0_ref, x1_ref, x2_ref, x3_ref)):
        rows = slice(128 * i, 128 * (i + 1))
        x_ref[rows] = block_ref[...]
    for i in range(2):
        rows = slice(256 * i, 256 * (i + 1))
        total = jnp.zeros((256, part_ref.shape[1]), F32)
        for at in range(0, act_ref.shape[1], STEP):
            cols = slice(at, at + STEP)
            hidden = dot(x_ref[rows], up_ref[:, cols]) + bias_ref[:, cols]
            cdf = 0.5 * (1.0 + lax.erf(hidden * 0.7071067811865476))
            active = (hidden * cdf).astype(BF)
            act_ref[rows, cols] = active
            slope = cdf + hidden * (0.3989422804014327 * jnp.exp(-0.5 * hidden * hidden))
            slope_ref[rows, cols] = slope.astype(BF)
            total += dot(active, w_ref[cols])
        part_ref[rows] = total.astype(BF)


def ffn(blocks, bias, weights, where):
    rows, width, units = 4 * blocks[0].shape[0], 1024, 1024
    vmem = pl.BlockSpec(memory_space=pltpu.VMEM)
    return pl.pallas_call(
        ffn_kernel,
        in_specs=[pl.BlockSpec(memory_space=pltpu.SMEM)] + [vmem] * 10,
        out_specs=[vmem] * 4,
        out_shape=[
            jax.ShapeDtypeStruct((rows, units), BF),
            jax.ShapeDtypeStruct((rows, units), BF),
            jax.ShapeDtypeStruct((rows, width), BF),
            jax.ShapeDtypeStruct((rows, width), BF),
        ],
        scratch_shapes=[pltpu.VMEM((width, units), BF), pltpu.VMEM((units, width), BF)],
        compiler_params=pltpu.CompilerParams(vmem_limit_bytes=24 * 1024 * 1024),
        cost_estimate=pl.CostEstimate(
            flops=4 * rows * width * units, bytes_accessed=8 * 1024 * 1024, transcendentals=0
        ),
        name="ffn",
    )(where, *blocks, bias, *weights)


def ffn_back_kernel(
    where_ref, d0_ref, d1_ref, d2_ref, d3_ref, act_ref, slope_ref, x_ref, up_own_ref, up_far_ref,
    down_ref, down_mine_ref, down_other_ref, part_ref, mine_ref, send_ref, hidden_sum_ref,
    out_sum_ref, d_ref, acc_ref, turned_ref, up_ref, w_ref,
):
    lay_halves(where_ref[0], up_own_ref, up_far_ref, up_ref)
    lay_down(where_ref, down_ref, down_mine_ref, down_other_ref, w_ref)
    total = jnp.zeros(out_sum_ref.shape, F32)
    for i, block_ref in enumerate((d0_ref, d1_ref, d2_ref, d3_ref)):
        block = block_ref[...]
        d_ref[128 * i : 128 * (i + 1)] = block
        total += jnp.sum(block.astype(F32), axis=0, keepdims=True)
    out_sum_ref[...] = total
    turned_ref[...] = x_ref[...].T
    own_core = where_ref[0]

    for at in range(4):
        cols = slice(STEP * at, STEP * (at + 1))
        d_hidden = slope_ref[:, cols].astype(F32) * dot_t(d_ref[...], w_ref[cols])
        d_hidden = d_hidden.astype(BF)
        hidden_sum_ref[:, cols] = jnp.sum(d_hidden.astype(F32), axis=0, keepdims=True)
        d_normed = dot_t(d_hidden, up_ref[:, cols])
        if at == 0:
            acc_ref[...] = d_normed
        elif at < 3:
            acc_ref[...] += d_normed
        else:
            part_ref[...] = (acc_ref[...] + d_normed).astype(BF)

        down = t_dot(act_ref[:, cols], d_ref[...]).astype(BF)
        up = dot(turned_ref[...], d_hidden).astype(BF)

        def store(to_ref, core, at=at, cols=cols, down=down, up=up):
            for x in range(4):
                if at % 2 == core:
                    to_ref[x, at // 2, :64] = down[64 * x : 64 * (x + 1)]
                for yh in range(2):
                    for z in range(4):
                        row = 512 * yh + 128 * z + 64 * core + 16 * x
                        to_ref[x, yh, 64 + 16 * z : 80 + 16 * z, cols] = up[row : row + 16]

        def store_all(core, store=store):
            store(mine_ref, core)
            store(send_ref, 1 - core)

        pl.when(own_core == 0)(functools.partial(store_all, 0))
        pl.when(own_core != 0)(functools.partial(store_all, 1))


def ffn_back(blocks, active, slope, normed, weights, where):
    rows, units = active.shape
    width = normed.shape[1]
    vmem = pl.BlockSpec(memory_space=pltpu.VMEM)
    grads = (4, 2, 128, 1024)
    return pl.pallas_call(
        ffn_back_kernel,
        in_specs=[pl.BlockSpec(memory_space=pltpu.SMEM)] + [vmem] * 12,
        out_specs=[vmem] * 5,
        out_shape=[
            jax.ShapeDtypeStruct((rows, width), BF),
            jax.ShapeDtypeStruct(grads, BF),
            jax.ShapeDtypeStruct(grads, BF),
            jax.ShapeDtypeStruct((1, units), F32),
            jax.ShapeDtypeStruct((1, width), F32),
        ],
        scratch_shapes=[
            pltpu.VMEM((rows, width), BF),
            pltpu.VMEM((rows, width), F32),
            pltpu.VMEM((width, rows), BF),
            pltpu.VMEM((width, units), BF),
            pltpu.VMEM((units, width), BF),
        ],
        compiler_params=pltpu.CompilerParams(vmem_limit_bytes=32 * 1024 * 1024),
        cost_estimate=pl.CostEstimate(
            flops=8 * rows * width * units, bytes_accessed=12 * 1024 * 1024, transcendentals=0
        ),
        name="ffn_back",
    )(where, *blocks, active, slope, normed, *weights)


def grad_second_kernel(
    core_ref, tok_ref, tok_far_ref, here_ref, far_ref, ctx_ref, attn_ref, sums_ref, mine_ref,
    send_ref, vec_ref,
):
    at = pl.program_id(0)
    grads = t_dot(tok_ref[...], here_ref[...])
    grads_far = t_dot(tok_far_ref[...], far_ref[...])
    queries = grads[:, :256].astype(BF)
    others = (grads[:, 256:] + grads_far).astype(BF)
    attn = t_dot(ctx_ref[...], attn_ref[...]).astype(BF)

    def store(core, put):
        for x in range(4):
            for z in range(4):
                row = 64 * core + 16 * x
                rows = slice(128 * z + row, 128 * z + row + 16)
                put(x, z, slice(0, 256), queries[rows])
                put(x, z, slice(256, 768), others[rows])
                put(x, z, slice(768, 1024), attn[row : row + 16, 256 * z : 256 * z + 256])

    def put_mine(x, z, cols, value):
        mine_ref[x, 0, 16 * z : 16 * z + 16, cols] = value

    def put_send(x, z, cols, value):
        first = pl.multiple_of(128 * x + 64 * at + 16 * z, 16)
        send_ref[pl.ds(first, 16), cols] = value

    def store_all(core):
        store(core, put_mine)
        store(1 - core, put_send)

    pl.when(core_ref[0] == 0)(lambda: store_all(0))
    pl.when(core_ref[0] != 0)(lambda: store_all(1))

    @pl.when(pl.program_id(0) == 0)
    def _():
        here = jnp.sum(here_ref[...].astype(F32), axis=0, keepdims=True)
        far = jnp.sum(far_ref[...].astype(F32), axis=0, keepdims=True)
        bias = jnp.concatenate(
            [here[:, :256], here[:, 512:] + far[:, 256:], jnp.zeros((1, 512), F32)], axis=1
        )
        attn_sum = jnp.sum(attn_ref[...].astype(F32), axis=0, keepdims=True)
        row_of = lax.broadcasted_iota(jnp.int32, (16, 1), 0)
        total = jnp.where(row_of == 0, bias, sums_ref[...])
        low = jnp.where(row_of == 2, attn_sum, total).astype(BF)
        vec_ref[...] = low
        send_ref[512:] = low


def grad_second(tokens_own, tokens_far, d_here, d_far, context, d_attn, sums, core):
    rows, cols = tokens_own.shape
    half = cols // 2
    return pl.pallas_call(
        grad_second_kernel,
        grid_spec=pltpu.PrefetchScalarGridSpec(
            num_scalar_prefetch=1,
            grid=(2,),
            in_specs=[
                pl.BlockSpec((rows, half), lambda i, core: (0, i)),
                pl.BlockSpec((rows, half), lambda i, core: (0, i)),
                pl.BlockSpec(d_here.shape, lambda i, core: (0, 0)),
                pl.BlockSpec(d_far.shape, lambda i, core: (0, 0)),
                pl.BlockSpec((rows, context.shape[1] // 2), lambda i, core: (0, i)),
                pl.BlockSpec(d_attn.shape, lambda i, core: (0, 0)),
                pl.BlockSpec(sums.shape, lambda i, core: (0, 0)),
            ],
            out_specs=[
                pl.BlockSpec((4, 1, 64, 1024), lambda i, core: (0, i, 0, 0)),
                pl.BlockSpec((528, 1024), lambda i, core: (0, 0)),
                pl.BlockSpec(sums.shape, lambda i, core: (0, 0)),
            ],
        ),
        out_shape=[
            jax.ShapeDtypeStruct((4, 2, 64, 1024), BF),
            jax.ShapeDtypeStruct((528, 1024), BF),
            jax.ShapeDtypeStruct(sums.shape, BF),
        ],
        compiler_params=pltpu.CompilerParams(vmem_limit_bytes=16 * 1024 * 1024),
        cost_estimate=pl.CostEstimate(
            flops=3 * rows * cols * 1024, bytes_accessed=8 * 1024 * 1024, transcendentals=0
        ),
        name="grad_second",
    )(core.reshape(1), tokens_own, tokens_far, d_here, d_far, context, d_attn, sums)


def norm_stats(values):
    mean = jnp.mean(values, axis=-1, keepdims=True)
    centered = values - mean
    rstd = lax.rsqrt(jnp.mean(centered * centered, axis=-1, keepdims=True) + EPSILON)
    return centered * rstd, rstd


def norm_back(grad_out, gain, xhat, rstd):
    g = grad_out * gain
    return rstd * (
        g
        - jnp.mean(g, axis=-1, keepdims=True)
        - xhat * jnp.mean(g * xhat, axis=-1, keepdims=True)
    )


def unroll_ring(blocks, index):
    stacked = jnp.concatenate([b[None] for b in blocks + blocks], axis=0)
    return lax.dynamic_slice_in_dim(stacked, (4 - index) % 4, 4, axis=0)


def swap(value, axis, groups):
    return lax.all_to_all(value, axis, 0, 0, axis_index_groups=groups, tiled=True)


Z_RINGS = [[0, 1, 2, 3], [4, 5, 6, 7]]
X_RINGS = [[8 * yl + 2 * x + core for x in range(4)] for yl in range(2) for core in range(2)]


def with_rows(block, vectors):
    flat = block.reshape(-1, block.shape[-1])
    return flat if vectors is None else jnp.concatenate([flat, vectors], axis=0)


def core_sum(mine, vectors, got):
    rows = mine.size // mine.shape[-1]
    total = (mine.astype(F32) + got[:rows].reshape(mine.shape).astype(F32)).astype(BF)
    if vectors is None:
        return total, None
    return total, (vectors.astype(F32) + got[rows:].astype(F32)).astype(BF)


def x_send(pieces, x):
    return [pick(pieces, x)] + [x_shift(pick(pieces, (x + k) % 4), k) for k in (1, 2, 3)]


def x_flat(pieces, vectors):
    flat = pieces.reshape(4, -1, pieces.shape[-1])
    return jnp.concatenate([flat, jnp.broadcast_to(vectors, (4,) + vectors.shape)], axis=1)


def x_sum(got, rows):
    total = jnp.sum(got.astype(F32), axis=0).astype(BF)
    return total[: 2 * rows].reshape(2, rows, -1), total[2 * rows :]


def y_send(pieces, vectors, yh):
    own, other = pick(pieces, yh), pick(pieces, 1 - yh)
    got = [
        y_flip(with_rows(block, vectors), lo, hi)
        for block, lo, hi in ((own, 1, 0), (other, 0, 1), (other, 1, 1))
    ]
    return [with_rows(own, vectors)] + got


def ring_of(piece):
    return [piece] + [x_shift(piece, -k) for k in (1, 2, 3)]


def both_cores(blocks, *others):
    ring = jnp.stack(after(tuple(blocks), *others), axis=0)
    return ring, core_flip(ring)


def lay_first_kernel(where_ref, ring_ref, far_ref, down_ref, up_ref):
    def lay(src_ref):
        for k in range(4):
            x = (where_ref[2] + k) % 4
            down_ref[pl.ds(pl.multiple_of(64 * x, 64), 64)] = src_ref[k, :64].astype(F32)
            rows = pl.ds(pl.multiple_of(16 * x, 16), 16)
            for z in range(4):
                block = src_ref[k, 64 + 16 * z : 80 + 16 * z].astype(F32)
                up_ref[rows, 512 * z : 512 * (z + 1)] = block[:, :512]
                up_ref[rows, 2048 + 512 * z : 2048 + 512 * (z + 1)] = block[:, 512:]

    at = pl.program_id(0)
    pl.when(at == 0)(lambda: lay(ring_ref))
    pl.when(at == 1)(lambda: lay(far_ref))


def lay_second_kernel(where_ref, ring_ref, far_ref, qkv_ref, out_ref):
    def lay(src_ref):
        for k in range(4):
            rows = pl.ds(pl.multiple_of(16 * ((where_ref[2] + k) % 4), 16), 16)
            for z in range(4):
                block = src_ref[k, 16 * z : 16 * (z + 1)].astype(F32)
                for part in range(6):
                    at = 512 * part + 128 * z
                    qkv_ref[rows, at : at + 128] = block[:, 128 * part : 128 * (part + 1)]
                out_ref[rows, 256 * z : 256 * (z + 1)] = block[:, 768:]

    at = pl.program_id(0)
    pl.when(at == 0)(lambda: lay(ring_ref))
    pl.when(at == 1)(lambda: lay(far_ref))


def lay_pieces(kernel, ring, far, blocks, place, name):
    x, core = place[1], place[2]
    where = jnp.stack([core, 1 - core, x]).astype(jnp.int32)
    return pl.pallas_call(
        kernel,
        grid_spec=pltpu.PrefetchScalarGridSpec(
            num_scalar_prefetch=1,
            grid=(2,),
            in_specs=[
                pl.BlockSpec(ring.shape, lambda i, where: (0, 0, 0)),
                pl.BlockSpec(far.shape, lambda i, where: (0, 0, 0)),
            ],
            out_specs=[
                pl.BlockSpec((4 * rows, cols), lambda i, where: (where[i], 0))
                for rows, cols in blocks
            ],
        ),
        out_shape=[jax.ShapeDtypeStruct((8 * rows, cols), F32) for rows, cols in blocks],
        compiler_params=pltpu.CompilerParams(vmem_limit_bytes=16 * 1024 * 1024),
        name=name,
    )(where, ring, far)


def on_device(
    tokens,
    counts,
    w_qkv,
    bias_qv,
    w_out,
    bias_out,
    gain_attn,
    shift_attn,
    w_up,
    bias_up,
    w_down,
    bias_down,
    gain_ffn,
    shift_ffn,
    cotangent,
):
    row_count, model_width = tokens.shape
    replica = lax.axis_index("replica")
    group = lax.axis_index("fsdp")
    yl, x, core = replica // 8, (replica // 2) % 4, replica % 2
    yh, z = group // 4, group % 4
    place = (yl, x, core, yh, z)
    lanes = 128
    counts_row = counts[0]

    ring = (z + jnp.arange(4, dtype=jnp.int32)) % 4
    own_counts = jnp.take(counts_row, yh * 4 + ring)
    far_counts = jnp.take(counts_row, (1 - yh) * 4 + ring)
    slot = jnp.arange(row_count, dtype=jnp.int32)
    own_ok = (slot[None, :] < own_counts[:, None]).reshape(-1)
    far_ok = (slot[None, :] < far_counts[:, None]).reshape(-1)
    key_mask = jnp.where(jnp.concatenate([own_ok, far_ok]), 0.0, -1e30).astype(F32)[None, :]
    row_ok = own_ok.astype(F32)[:, None]

    sent = pack(w_qkv, (bias_qv,), core, lanes, "pack_qkv")
    small = (bias_out, gain_attn, shift_attn, bias_up, bias_down, gain_ffn, shift_ffn)
    up_sent = pack(w_up, small, core, 512, "pack_up")
    token_blocks = z_gather(tokens)
    out_far = y_flip(w_out, 0, 1)
    got = lax.all_to_all(sent, "fsdp", 0, 0, tiled=True)
    got_far = core_flip(got.reshape(640, 768)).reshape(8, 80, 768)
    bias_own = got[:, 64, :256].astype(F32).reshape(2, 2, 4, lanes)
    bias_own = pick(bias_own, z, 2).reshape(2, 2 * lanes)

    tokens_all = jnp.concatenate(token_blocks, axis=0)
    queries, kv_own, qkv_w = project(token_blocks, got, got_far, bias_own, core)
    kv_far = y_flip(kv_own, 0, 1)

    up_own = swap(after(up_sent, kv_own), "fsdp", None)
    vec_all = up_own[:, 64:72].astype(F32)
    bout_all = vec_all[:, 0, :lanes].reshape(1, -1)
    ga_all = vec_all[:, 1, :lanes].reshape(1, -1)
    sa_all = vec_all[:, 2, :lanes].reshape(1, -1)
    bup_own = pick(vec_all[:, 3, :512].reshape(2, 4, 512), z, 1).reshape(1, -1)
    bdown_all = vec_all[:, 4, :lanes].reshape(1, -1)
    gf_all = vec_all[:, 5, :lanes].reshape(1, -1)
    sf_all = vec_all[:, 6, :lanes].reshape(1, -1)
    up_far = core_flip(after(up_own, kv_far).reshape(640, 1024)).reshape(8, 80, 1024)
    down_mine = y_flip(pick(after(w_down, kv_far).reshape(2, 256, 1024), core), 0, 1)
    where = jnp.stack([core, yh]).astype(jnp.int32)

    def order(own, far):
        return jnp.where(
            yh == 0, jnp.concatenate([own, far], axis=0), jnp.concatenate([far, own], axis=0)
        )

    out_w = order(w_out, out_far)
    context, probs, attn_part = attend(queries, kv_own, kv_far, key_mask, row_ok, out_w)
    resid1 = add_terms([tokens] + z_scatter(attn_part)) + bout_all
    xhat1, rstd1 = norm_stats(resid1)
    normed = xhat1 * ga_all + sa_all
    normed_blocks = z_gather(normed.astype(BF))
    down_other = core_flip(after(down_mine, normed_blocks[2]))
    weights = (up_own, up_far, w_down, down_mine, down_other)
    active, slope, ffn_part, normed_all = ffn(normed_blocks, bup_own, weights, where)
    tokens_far = y_flip(after(tokens_all, ffn_part), 0, 1)
    resid2 = add_terms([normed] + z_scatter(ffn_part)) + bdown_all
    xhat2, rstd2 = norm_stats(resid2)
    layer_out = (xhat2 * gf_all + sf_all).astype(BF)

    cot = cotangent.astype(F32)
    d_resid2 = norm_back(cot, gf_all, xhat2, rstd2)

    dn_part, first, first_sent, hidden_sum, ffn_sum = ffn_back(
        z_gather(d_resid2.astype(BF)), active, slope, normed_all, weights, where
    )
    dn_terms = z_scatter(dn_part)
    first_got = core_flip(first_sent.reshape(1024, 1024))

    d_normed = add_terms([d_resid2] + dn_terms)
    d_resid1 = norm_back(d_normed, ga_all, xhat1, rstd1)
    dattn_blocks = z_gather(d_resid1.astype(BF))
    first_core, _ = core_sum(first, None, after(first_got, d_resid1))
    first_got = x_send(first_core, x)
    dattn_all = jnp.concatenate(dattn_blocks, axis=0)
    d_here, dkv_far = attend_back(
        queries, kv_own, kv_far, dattn_all, row_ok, out_w, probs
    )

    zero = jnp.zeros((1024,), F32)
    sums = pack_rows(
        [
            zero,
            hidden_sum[0],
            zero,
            ffn_sum[0],
            jnp.sum(d_normed * xhat1, axis=0),
            jnp.sum(d_normed, axis=0),
            jnp.sum(cot * xhat2, axis=0),
            jnp.sum(cot, axis=0),
        ],
        16,
        1024,
    )
    far_terms = y_flip(dkv_far, 0, 1)
    second, second_sent, vectors = grad_second(
        tokens_all, tokens_far, after(d_here, *first_got), dkv_far, context, dattn_all, sums, core
    )

    second_got = core_flip(second_sent)
    first_x = add_terms(after(tuple(first_got), second)).astype(BF)
    first_terms = y_send(first_x, None, yh)
    second_core, vec_core = core_sum(second, vectors, after(second_got, first_x))
    second_flat = x_flat(second_core, vec_core)
    second_got = swap(second_flat, "replica", X_RINGS)

    far_terms = after(far_terms, second_flat)
    dkv = (d_here[:, 256:].astype(F32) + far_terms.astype(F32)).astype(BF)
    d_projected = jnp.concatenate([d_here[:, :256], dkv], axis=1)

    second_x, vec_x = x_sum(after(second_got, far_terms), 64)
    second_terms = y_send(second_x, vec_x, yh)
    first_sum = add_terms(after(tuple(first_terms), second_x)).astype(BF)
    up_sum = swap(after(first_sum, second_x)[64:].reshape(4, 16, 1024), "fsdp", Z_RINGS)
    up_sum = up_sum.reshape(64, 1024)

    first_ring = ring_of(jnp.concatenate([first_sum[:64], up_sum], axis=0))
    second_all = add_terms(after(tuple(second_terms), up_sum)).astype(BF)
    second_sum, vec_sum = second_all[:64], second_all[64:]
    input_part = dot_t(after(d_projected, up_sum), qkv_w).astype(BF)
    input_grad = add_terms([d_resid1] + z_scatter(input_part))
    bias_row = jnp.broadcast_to(vec_sum[None, 0:1, :512], (4, 1, 512))
    norm_row = pick(vec_sum[4:8].reshape(4, 2, 4, lanes), yh, 1).transpose(1, 0, 2)
    side = jnp.pad(
        jnp.concatenate([bias_row, norm_row.reshape(4, 1, 512)], axis=1),
        ((0, 0), (0, 14), (0, 256)),
    )
    swapped = swap(
        jnp.concatenate([second_sum[:, :768].reshape(4, 16, 768), side], axis=1), "fsdp", Z_RINGS
    )
    second_ring = ring_of(
        jnp.concatenate([swapped[:, :16].reshape(64, 768), second_sum[:, 768:]], axis=1)
    )
    ring, far = both_cores(first_ring, swapped)
    grad_w_down, grad_w_up = lay_pieces(
        lay_first_kernel, ring, far, ((64, 1024), (16, 4096)), place, "lay_first"
    )
    ring, far = both_cores(second_ring, grad_w_down)
    grad_w_qkv, grad_w_out = lay_pieces(
        lay_second_kernel, ring, far, ((16, 3072), (16, 1024)), place, "lay_second"
    )
    bqv_all = swapped[:, 16, :512].astype(F32).reshape(4, 2, 2, lanes).transpose(1, 2, 0, 3)
    grad_bqv = pick(bqv_all.reshape(8, 256), group)
    norms = jnp.sum(swapped[:, 17, :512].astype(F32), axis=0).reshape(4, lanes)
    grad_bup = pick(vec_sum[1].reshape(2, 512), yh).astype(F32)
    rest = pick(vec_sum[2:4].reshape(2, 8, lanes), group, 1).astype(F32)

    return (
        layer_out,
        input_grad,
        grad_w_qkv,
        grad_bqv,
        grad_w_out,
        rest[0],
        norms[0],
        norms[1],
        grad_w_up,
        grad_bup,
        grad_w_down,
        rest[1],
        norms[2],
        norms[3],
    )


def solution(mesh):
    in_specs = (
        P(("replica", "fsdp"), None),
        P("replica", None),
        P("fsdp", None),
        P("fsdp"),
        P("fsdp", None),
        P("fsdp"),
        P("fsdp"),
        P("fsdp"),
        P("fsdp", None),
        P("fsdp"),
        P("fsdp", None),
        P("fsdp"),
        P("fsdp"),
        P("fsdp"),
        P(("replica", "fsdp"), None),
    )
    out_specs = (
        P(("replica", "fsdp"), None),
        P(("replica", "fsdp"), None),
        P("fsdp", None),
        P("fsdp"),
        P("fsdp", None),
        P("fsdp"),
        P("fsdp"),
        P("fsdp"),
        P("fsdp", None),
        P("fsdp"),
        P("fsdp", None),
        P("fsdp"),
        P("fsdp"),
        P("fsdp"),
    )
    return jax.shard_map(
        on_device, mesh=mesh, in_specs=in_specs, out_specs=out_specs, check_vma=False
    )
```
